128 devices in a mesh: req: 32 (over y, x, core), tp: 4 (over z).
Axes of the slice: x: 4, y: 4, z: 4, core: 2. Of those that a mesh axis runs over, the one named last changes fastest.
Arguments:
- hidden: bfloat16 [32, 8192], P(None, 'req')
- attn_gain: bfloat16 [2, 8192], P(None, 'req'), may hold values from 0.5 to 1.5
- q_weight: bfloat16 [2, 8192, 4096], P(None, 'req', 'tp'), may hold values from -0.0625 to 0.0625
- o_weight: bfloat16 [2, 4096, 8192], P(None, 'tp', 'req'), may hold values from -0.09375 to 0.09375
- ffn_gain: bfloat16 [2, 8192], P(None, 'req'), may hold values from 0.5 to 1.5
- gate_weight: bfloat16 [2, 8192, 14336], P(None, 'req', 'tp'), may hold values from -0.0625 to 0.0625
- up_weight: bfloat16 [2, 8192, 14336], P(None, 'req', 'tp'), may hold values from -0.0625 to 0.0625
- down_weight: bfloat16 [2, 14336, 8192], P(None, 'tp', 'req'), may hold values from -0.046875 to 0.046875
- kv_pool: bfloat16 [2, 1024, 4, 2, 128, 128], P(None, 'req', 'tp')
- block_home: int32 [32, 32], P('req'), may hold values from 0 to 1023, as said below
- chosen: int32 [2, 32, 4, 24], P(None, 'req', 'tp'), may hold values from 0 to 31, as said below
- chosen_count: int32 [2, 32, 4], P(None, 'req', 'tp'), may hold values from 6 to 24
Outputs:
- new_hidden: bfloat16 [32, 8192], P(None, 'req')
The draws below stay inside these ranges and needn't reach their ends.
Inputs may be any that keep to these rules, and one draw needn't show every extreme that they name: `block_home`: pool slot p lies on store device p // 32 of req; every slot belongs to exactly one block of one request, and every request has exactly 1 block on each store device. `chosen`: entries of a list are distinct. The used entries of a list are the one block of some store devices and some blocks of one more; entries from chosen_count on are ignored.
All inputs are finite; a program needn't handle non-finite values.
Results may differ from the reference program's by a relative error of at most 0.038.
Values may be sent and summed in bfloat16 or wider, within the bound.
No kernel may reach another device: no remote copies, remote signals or barrier semaphores. Data moves between devices by JAX's collectives and lax.ppermute only.
A program may use at most 64 MiB of HBM per device.

```python
import math
import jax
import jax.numpy as jnp
from jax import lax

D = 8192
FF = 14336
HK = 4
QPK = 8
HD = 128
BLOCK = 128
CTX_BLK = 32
MAXSEL = 24
LAYERS = 2
REQ_DEV = 1
REQUESTS = 32
POOL = 1024
PER_STORE = 1
SEL_MIN = 6


def store_layout(key):
    order_scores = jax.random.randint(key, (REQUESTS, CTX_BLK), 0, 1 << 20) * CTX_BLK + jnp.arange(CTX_BLK)[None, :]
    return jnp.argsort(order_scores, axis=1).astype(jnp.int32)


def draw_block_home(key, part):
    order = store_layout(key)
    key = jax.random.fold_in(key, 5)
    stores_n = CTX_BLK // PER_STORE
    pool_dev = REQ_DEV * CTX_BLK
    position = jnp.argsort(order, axis=1).astype(jnp.int32)
    store_of = position % stores_n
    within = position // stores_n
    slot_scores = jax.random.randint(key, (stores_n, pool_dev), 0, 1 << 20) * pool_dev + jnp.arange(pool_dev)[None, :]
    slot_perm = jnp.argsort(slot_scores, axis=1).astype(jnp.int32)
    request = jnp.arange(REQUESTS)[:, None]
    slot_of = slot_perm[store_of, request * PER_STORE + within]
    return (store_of * pool_dev + slot_of).astype(jnp.int32)


def draw_chosen(key, part):
    order = store_layout(key)
    key = jax.random.fold_in(key, 7)
    stores_n = CTX_BLK // PER_STORE
    store_scores = jax.random.randint(key, (LAYERS, REQUESTS, HK, stores_n), 0, 1 << 20) * stores_n + jnp.arange(stores_n)
    store_order = jnp.argsort(store_scores, axis=3).astype(jnp.int32)
    entry = jnp.arange(MAXSEL)
    picked_store = store_order[..., entry // PER_STORE]
    position = picked_store + entry % PER_STORE * stores_n
    request = jnp.arange(REQUESTS)[None, :, None, None]
    return order[request, position].astype(jnp.int32)


def draw_chosen_count(key, part):
    key = jax.random.fold_in(key, 9)
    count_key, spot_key = jax.random.split(key)
    counts = jax.random.randint(count_key, (LAYERS, REQUESTS, HK), SEL_MIN, MAXSEL + 1)
    flat_counts = counts.reshape(-1)
    spot = jax.random.randint(spot_key, (), 0, flat_counts.shape[0])
    flat_counts = flat_counts.at[spot].set(MAXSEL)
    return flat_counts.reshape(LAYERS, REQUESTS, HK).astype(jnp.int32)


def draw_kv_pool(key, part):
    key = jax.random.fold_in(key, 11)
    shape_all = (LAYERS, POOL, HK, 2, BLOCK, HD)
    normal_key = jax.random.fold_in(key, 0)
    which_part = jnp.arange(2).reshape(1, 1, 1, 2, 1, 1)
    base = jnp.clip(jax.random.normal(normal_key, shape_all, jnp.float32), -6.0, 6.0)
    return (base * jnp.where(which_part == 0, 1.9, 1.0)).astype(jnp.bfloat16)


def draw_hidden(key, part):
    key = jax.random.fold_in(key, 13)
    normal_key = jax.random.fold_in(key, 0)
    column_ramp = 0.3 * jnp.exp(jnp.arange(D).astype(jnp.float32) * (math.log(3.0) / D))
    base = jnp.clip(jax.random.normal(normal_key, (REQUESTS, D), jnp.float32), -6.0, 6.0)
    return (base * column_ramp[None, :]).astype(jnp.bfloat16)


def steps_of(stream_key, extent, cuts, low, largest):
    def one(dim, shards_of):
        steps = jax.random.uniform(jax.random.fold_in(jax.random.fold_in(stream_key, 6), dim), (shards_of,), jnp.float32, low / len(cuts), largest / len(cuts))
        return jnp.repeat(jnp.exp(steps), extent[dim] // shards_of).reshape((-1,) + (1,) * (len(extent) - dim - 1))

    level = one(*cuts[0])
    for cut in cuts[1:]:
        level = level * one(*cut)
    return level


def centred(rng, dims, deviation, most, cuts=(), kind=jnp.bfloat16):
    result = jax.random.normal(rng, dims, jnp.float32) * deviation
    if len(cuts) > 0:
        result = steps_of(rng, dims, cuts, -0.22, 0.18) * result
    return jnp.clip(result, min=-most, max=most).astype(kind)


def setup_inputs(seed: int = 0) -> dict:
    key_list = jax.random.split(jax.random.key(seed), 13)
    hidden = draw_hidden(jax.random.fold_in(key_list[12], 71), 0)
    attn_gain = jnp.clip(1.0 + 0.1 * jax.random.normal(key_list[1], (LAYERS, D), jnp.float32), 0.5, 1.5).astype(jnp.bfloat16)
    q_weight = centred(key_list[2], (LAYERS, D, HK * QPK * HD), D ** -0.5, 0.0625, ((1, 32), (2, 4)))
    o_weight = centred(key_list[3], (LAYERS, HK * QPK * HD, D), (HK * QPK * HD) ** -0.5, 0.09375, ((1, 4), (2, 32)))
    ffn_gain = jnp.clip(1.0 + 0.1 * jax.random.normal(key_list[4], (LAYERS, D), jnp.float32), 0.5, 1.5).astype(jnp.bfloat16)
    gate_weight = centred(key_list[5], (LAYERS, D, FF), D ** -0.5, 0.0625, ((1, 32), (2, 4)))
    up_weight = centred(key_list[6], (LAYERS, D, FF), D ** -0.5, 0.0625, ((1, 32), (2, 4)))
    down_weight = centred(key_list[7], (LAYERS, FF, D), FF ** -0.5, 0.046875, ((1, 4), (2, 32)))
    kv_pool = draw_kv_pool(jax.random.fold_in(key_list[12], 71), 0)
    block_home = draw_block_home(jax.random.fold_in(key_list[12], 71), 0)
    chosen = draw_chosen(jax.random.fold_in(key_list[12], 71), 0)
    chosen_count = draw_chosen_count(jax.random.fold_in(key_list[12], 71), 0)
    return {"hidden": hidden, "attn_gain": attn_gain, "q_weight": q_weight, "o_weight": o_weight, "ffn_gain": ffn_gain, "gate_weight": gate_weight, "up_weight": up_weight, "down_weight": down_weight, "kv_pool": kv_pool, "block_home": block_home, "chosen": chosen, "chosen_count": chosen_count}


MASK_FILL = -1e+30
EPSILON = 1e-05

def rotary(queries, position):
    head_size = queries.shape[-1]
    half_size = head_size // 2
    freq_idx = jnp.arange(half_size).astype(queries.dtype)
    angles = position * jnp.exp(freq_idx * (-2.0 * math.log(500000.0) / head_size))
    cosine = jnp.cos(angles)
    sine_part = jnp.sin(angles)
    lower_half = queries[..., :half_size]
    upper_half = queries[..., half_size:]
    return jnp.concatenate([lower_half * cosine - upper_half * sine_part, upper_half * cosine + lower_half * sine_part], axis=-1)

def inverse_rms(current):
    widened = current.astype(jnp.float32)
    return lax.rsqrt(lax.optimization_barrier(jnp.mean(widened * widened, axis=1)) + EPSILON)

def apply_gain(current, gain):
    return (current.astype(jnp.float32) * gain.astype(jnp.float32)).astype(jnp.bfloat16)

def attend_request(query_r, pool_ids, count_r, pool_layer):
    head_index = jnp.arange(pool_ids.shape[0])[:, None]
    blocks = pool_layer[pool_ids, head_index]
    key_part = blocks[:, :, 0].astype(jnp.float32)
    value_part = blocks[:, :, 1].astype(jnp.float32)
    scores = jnp.einsum('geh,gkbh->gekb', query_r.astype(jnp.float32), key_part, precision=lax.Precision.HIGHEST)
    block_max = lax.optimization_barrier(jnp.max(scores, axis=3))
    exp_terms = jnp.exp(scores - block_max[..., None])
    block_sum = lax.optimization_barrier(jnp.sum(exp_terms, axis=3))
    weights = lax.optimization_barrier(exp_terms.astype(jnp.bfloat16)).astype(jnp.float32)
    block_acc = jnp.einsum('gekb,gkbh->gekh', weights, value_part, precision=lax.Precision.HIGHEST)
    used_mask = jnp.arange(pool_ids.shape[1])[None, :] < count_r[:, None]
    block_max = jnp.where(used_mask[:, None, :], block_max, MASK_FILL)
    overall = lax.optimization_barrier(jnp.max(block_max, axis=2, keepdims=True))
    rescale = jnp.exp(block_max - overall)
    numerator = lax.optimization_barrier(jnp.sum(rescale[..., None] * block_acc, axis=2))
    denominator = lax.optimization_barrier(jnp.sum(rescale * block_sum, axis=2))
    return (numerator / denominator[..., None]).astype(jnp.bfloat16)

def reference(hidden, attn_gain, q_weight, o_weight, ffn_gain, gate_weight, up_weight, down_weight, kv_pool, block_home, chosen, chosen_count):
    position = float(CTX_BLK * BLOCK - 1)
    current = hidden
    row_index = jnp.arange(current.shape[0])[:, None, None]
    for layer_no in range(LAYERS):
        inv = inverse_rms(current)
        scaled = apply_gain(current, attn_gain[layer_no])
        queries = jnp.dot(scaled, q_weight[layer_no], preferred_element_type=jnp.float32) * inv[:, None]
        queries = queries.reshape(current.shape[0], HK, QPK, HD)
        queries = (rotary(queries, position) * HD ** (-0.5)).astype(jnp.bfloat16)
        pool_ids = block_home[row_index, chosen[layer_no]].astype(jnp.int32)
        pool_layer = kv_pool[layer_no]
        context = lax.map(lambda packed: attend_request(packed[0], packed[1], packed[2], pool_layer), (queries, pool_ids, chosen_count[layer_no]))
        context = context.reshape(current.shape[0], HK * QPK * HD)
        attended = (current.astype(jnp.float32) + jnp.dot(context, o_weight[layer_no], preferred_element_type=jnp.float32)).astype(jnp.bfloat16)
        inv2 = inverse_rms(attended)
        scaled = apply_gain(attended, ffn_gain[layer_no])
        gate = jnp.dot(scaled, gate_weight[layer_no], preferred_element_type=jnp.float32) * inv2[:, None]
        up_part = jnp.dot(scaled, up_weight[layer_no], preferred_element_type=jnp.float32) * inv2[:, None]
        activated = (jax.nn.silu(gate) * up_part).astype(jnp.bfloat16)
        current = (attended.astype(jnp.float32) + jnp.dot(activated, down_weight[layer_no], preferred_element_type=jnp.float32)).astype(jnp.bfloat16)
    return current
```

```python
import math

import jax
import jax.numpy as jnp
from jax import lax
from jax.sharding import PartitionSpec as P

D = 8192
LAYERS = 2

MASK_FILL = -1e30
EPSILON = 1e-05


def rotary(queries, position):
    head_size = queries.shape[-1]
    half_size = head_size // 2
    freq_idx = jnp.arange(half_size).astype(queries.dtype)
    angles = position * jnp.exp(freq_idx * (-2.0 * math.log(500000.0) / head_size))
    cosine = jnp.cos(angles)
    sine_part = jnp.sin(angles)
    lower_half = queries[..., :half_size]
    upper_half = queries[..., half_size:]
    return jnp.concatenate(
        [
            lower_half * cosine - upper_half * sine_part,
            upper_half * cosine + lower_half * sine_part,
        ],
        axis=-1,
    )


def apply_gain(current, gain):
    return (current.astype(jnp.float32) * gain.astype(jnp.float32)).astype(jnp.bfloat16)


def split_squares(current):
    widened = current.astype(jnp.float32)
    squares = jnp.sum(widened * widened, axis=1)
    high = squares.astype(jnp.bfloat16)
    low = (squares - high.astype(jnp.float32)).astype(jnp.bfloat16)
    return high, low


def exchange(array):
    return lax.all_to_all(array, "req", split_axis=0, concat_axis=0, tiled=True)


def with_squares(partial_sums, current, lanes, rows):
    requests, width = partial_sums.shape
    body = partial_sums.astype(jnp.bfloat16).reshape(requests, width // lanes, lanes)
    high, low = split_squares(current)
    spare = rows - width // lanes
    tail = jnp.zeros((requests, spare, lanes), jnp.bfloat16)
    tail = tail.at[:, 0, :].set(high[:, None]).at[:, 1, :].set(low[:, None])
    return jnp.concatenate([body, tail], axis=1)


def reduce_request(partial_sums, current, rows):
    width = partial_sums.shape[1]
    received = exchange(with_squares(partial_sums, current, 128, rows))
    totals = jnp.sum(received.astype(jnp.float32), axis=0)
    used = width // 128
    squares = totals[used, 0] + totals[used + 1, 0]
    return totals[:used], lax.rsqrt(squares / D + EPSILON)


def gather_requests(own):
    n_req = lax.axis_size("req")
    return exchange(jnp.broadcast_to(own[None], (n_req,) + own.shape))


def sum_over_heads(partial_sum):
    n_tp = lax.axis_size("tp")
    total = partial_sum
    for shift in (2, 1, 3):
        pairs = [(i, (i + shift) % n_tp) for i in range(n_tp)]
        total = total + lax.ppermute(partial_sum, "tp", pairs)
    return total


def shards(
    hidden,
    attn_gain,
    q_weight,
    o_weight,
    ffn_gain,
    gate_weight,
    up_weight,
    down_weight,
    kv_pool,
    block_home,
    chosen,
    chosen_count,
):
    n_req = lax.axis_size("req")
    most_sel = chosen.shape[3]
    pool_dev = kv_pool.shape[1]
    head_size = kv_pool.shape[5]
    position = float(block_home.shape[1] * kv_pool.shape[4] - 1)
    store_ids = jnp.arange(n_req)
    homes = block_home[0]
    at_store = homes[None, :] // pool_dev == store_ids[:, None]
    slots = jnp.sum(jnp.where(at_store, homes[None, :] % pool_dev, 0), axis=1)
    wanted = exchange(slots.reshape(n_req, 1, 1).astype(jnp.int32)).reshape(n_req)
    fetched = [
        exchange(jnp.take(kv_pool[layer_no, :, 0], wanted, axis=0)) for layer_no in range(LAYERS)
    ]
    valid = []
    for layer_no in range(LAYERS):
        stores = homes[chosen[layer_no, 0, 0]] // pool_dev
        used = jnp.arange(most_sel) < chosen_count[layer_no, 0, 0]
        valid.append(jnp.any((stores[None, :] == store_ids[:, None]) & used[None, :], axis=1))
    current = hidden
    for layer_no in range(LAYERS):
        scaled = apply_gain(current, attn_gain[layer_no])
        product = jnp.dot(scaled, q_weight[layer_no], preferred_element_type=jnp.float32)
        totals, inv = reduce_request(product, current, 16)
        queries = (rotary(totals * inv, position) * head_size ** (-0.5)).astype(jnp.bfloat16)
        blocks = fetched[layer_no]
        scores = jnp.einsum("eh,sbh->seb", queries, blocks[:, 0], preferred_element_type=jnp.float32)
        block_max = jnp.max(scores, axis=2)
        terms = jnp.exp(scores - block_max[..., None])
        block_sum = jnp.sum(terms, axis=2)
        block_acc = jnp.einsum(
            "seb,sbh->seh", terms.astype(jnp.bfloat16), blocks[:, 1], preferred_element_type=jnp.float32
        )
        block_max = jnp.where(valid[layer_no][:, None], block_max, MASK_FILL)
        rescale = jnp.exp(block_max - jnp.max(block_max, axis=0, keepdims=True))
        numerator = jnp.sum(rescale[..., None] * block_acc, axis=0)
        denominator = jnp.sum(rescale * block_sum, axis=0)
        context = (numerator / denominator[..., None]).astype(jnp.bfloat16)
        contexts = gather_requests(context).reshape(n_req, -1)
        attn_part = jnp.dot(contexts, o_weight[layer_no], preferred_element_type=jnp.float32)
        attended = (current.astype(jnp.float32) + sum_over_heads(attn_part)).astype(jnp.bfloat16)
        scaled = apply_gain(attended, ffn_gain[layer_no])
        gate = jnp.dot(scaled, gate_weight[layer_no], preferred_element_type=jnp.float32)
        up_part = jnp.dot(scaled, up_weight[layer_no], preferred_element_type=jnp.float32)
        totals, inv = reduce_request(jnp.concatenate([gate, up_part], axis=1), attended, 64)
        half = totals.shape[0] // 2
        activated = (jax.nn.silu(totals[:half] * inv) * (totals[half:] * inv)).astype(jnp.bfloat16)
        rows = gather_requests(activated).reshape(n_req, -1)
        ffn_part = jnp.dot(rows, down_weight[layer_no], preferred_element_type=jnp.float32)
        current = (attended.astype(jnp.float32) + sum_over_heads(ffn_part)).astype(jnp.bfloat16)
    return current


def solution(mesh):
    return jax.shard_map(
        shards,
        mesh=mesh,
        in_specs=(
            P(None, "req"),
            P(None, "req"),
            P(None, "req", "tp"),
            P(None, "tp", "req"),
            P(None, "req"),
            P(None, "req", "tp"),
            P(None, "req", "tp"),
            P(None, "tp", "req"),
            P(None, "req", "tp", None, None, None),
            P("req", None),
            P(None, "req", "tp", None),
            P(None, "req", "tp"),
        ),
        out_specs=P(None, "req"),
        check_vma=False,
    )
```

```python
import functools
import math

import jax
import jax.numpy as jnp
import numpy as np
from jax import lax
from jax.experimental import pallas as pl
from jax.experimental.pallas import tpu as pltpu
from jax.sharding import PartitionSpec as P

D = 8192
LAYERS = 2
LANES = 128

MASK_FILL = -1e30
EPSILON = 1e-05

VMEM = pl.BlockSpec(memory_space=pltpu.VMEM)
SMEM = pl.BlockSpec(memory_space=pltpu.SMEM)
ANY = pl.BlockSpec(memory_space=pl.ANY)
F32 = jnp.float32
BF16 = jnp.bfloat16


def rotary_tables(position, head_size):
    freq_idx = np.arange(head_size // 2)
    angles = position * np.exp(freq_idx * (-2.0 * math.log(500000.0) / head_size))
    cosine, sine_part = np.cos(angles), np.sin(angles)
    scale = head_size**-0.5
    tables = np.stack([np.concatenate([cosine, cosine]), np.concatenate([-sine_part, sine_part])])
    return jnp.asarray(tables * scale, F32)


def call(kernel, out_shape, in_specs, scratch=(), limit=16, out_specs=None, flops=0, nbytes=0):
    return pl.pallas_call(
        kernel,
        out_shape=out_shape,
        in_specs=in_specs,
        out_specs=out_specs if out_specs is not None else jax.tree.map(lambda _: VMEM, out_shape),
        scratch_shapes=list(scratch),
        compiler_params=pltpu.CompilerParams(vmem_limit_bytes=limit * 1024 * 1024),
        cost_estimate=pl.CostEstimate(flops=flops, bytes_accessed=nbytes, transcendentals=0),
    )


def store_squares(packed, current, stride, row):
    requests = current.shape[0]
    squares = jnp.sum(current * current, axis=1, keepdims=True)
    high = squares.astype(BF16).astype(F32)
    packed[pl.ds(row, requests, stride=stride), :] = jnp.broadcast_to(high, (requests, LANES))
    packed[pl.ds(row + 1, requests, stride=stride), :] = jnp.broadcast_to(
        squares - high, (requests, LANES)
    )


def store_blocks(packed, product, stride, row):
    requests, width = product.shape
    for k in range(width // LANES):
        packed[pl.ds(row + k, requests, stride=stride), :] = product[:, k * LANES : (k + 1) * LANES]


def store_zeros(packed, requests, stride, rows):
    for row in rows:
        packed[pl.ds(row, requests, stride=stride), :] = jnp.zeros((requests, LANES), F32)


def queries_of(current, gain_ref, layer_no, weight, packed, payload_ref):
    requests = current.shape[0]
    heads = weight.shape[1] // LANES
    stride = packed.shape[0] // requests
    scaled = (current * gain_ref[pl.ds(layer_no, 1), :].astype(F32)).astype(BF16)
    product = jnp.dot(scaled, weight[...], preferred_element_type=F32)
    store_blocks(packed, product, stride, 0)
    store_squares(packed, current, stride, heads)
    store_zeros(packed, requests, stride, range(heads + 2, stride))
    payload_ref[...] = packed[...].astype(BF16)


def first_query_kernel(layer_no, x_ref, gain_ref, weight_ref, payload_ref, weight, packed, sem):
    copy = pltpu.make_async_copy(weight_ref.at[layer_no], weight, sem)
    copy.start()
    current = x_ref[...].astype(F32)
    copy.wait()
    queries_of(current, gain_ref, layer_no, weight, packed, payload_ref)


def query_kernel(
    layer_no, x_ref, own, part_a, part_b, part_c, gain_ref, weight_ref, out_ref, payload_ref, weight, packed, sem
):
    copy = pltpu.make_async_copy(weight_ref.at[layer_no], weight, sem)
    copy.start()
    total = x_ref[...].astype(F32) + ((own[...] + part_a[...]) + (part_b[...] + part_c[...]))
    out_ref[...] = total.astype(BF16)
    current = out_ref[...].astype(F32)
    copy.wait()
    queries_of(current, gain_ref, layer_no, weight, packed, payload_ref)


def attention_kernel(received_ref, tables_ref, bias_ref, kv_ref, out_ref):
    stores = kv_ref.shape[0]
    rows = received_ref.shape[0] // stores
    heads = out_ref.shape[0] // stores
    totals = jnp.sum(received_ref[...].astype(F32).reshape(stores, rows, LANES), axis=0)
    squares = totals[heads : heads + 1, :] + totals[heads + 1 : heads + 2, :]
    queries = totals[:heads] * lax.rsqrt(squares / D + EPSILON)
    queries = queries * tables_ref[0:1, :] + pltpu.roll(queries, LANES // 2, 1) * tables_ref[1:2, :]
    keys = kv_ref[:, 0].reshape(-1, LANES)
    values = kv_ref[:, 1].reshape(-1, LANES)
    scores = lax.dot_general(
        queries.astype(BF16), keys, (((1,), (1,)), ((), ())), preferred_element_type=F32
    )
    scores = jnp.where(bias_ref[...] < 0.0, MASK_FILL, scores)
    terms = jnp.exp(scores - jnp.max(scores, axis=1, keepdims=True))
    total = jnp.sum(terms, axis=1, keepdims=True)
    context = jnp.dot(terms.astype(BF16), values, preferred_element_type=F32) / total
    out_ref[...] = jnp.broadcast_to(context[None], (stores, heads, LANES)).reshape(-1, LANES).astype(BF16)


def rows_of(packed, requests, blocks):
    stride = packed.shape[0] // requests
    return jnp.concatenate(
        [packed[pl.ds(k, requests, stride=stride), :].astype(BF16) for k in range(blocks)], axis=1
    )


def project_kernel(layer_no, requests, received_ref, weight_ref, out_ref, weight, packed, sem):
    copy = pltpu.make_async_copy(weight_ref.at[layer_no], weight, sem)
    copy.start()
    packed[...] = received_ref[...].astype(F32)
    rows = rows_of(packed, requests, weight.shape[0] // LANES)
    copy.wait()
    out_ref[...] = jnp.dot(rows, weight[...], preferred_element_type=F32)


def gate_up_kernel(
    layer_no,
    x_ref,
    own,
    part_a,
    part_b,
    part_c,
    gain_ref,
    gate_ref,
    up_ref,
    out_ref,
    payload_ref,
    gate,
    up,
    packed,
    sems,
):
    gate_copy = pltpu.make_async_copy(gate_ref.at[layer_no], gate, sems.at[0])
    up_copy = pltpu.make_async_copy(up_ref.at[layer_no], up, sems.at[1])
    gate_copy.start()
    up_copy.start()
    requests = x_ref.shape[0]
    stride = packed.shape[0] // requests
    half = stride // 2
    blocks = gate.shape[1] // LANES
    total = x_ref[...].astype(F32) + ((own[...] + part_a[...]) + (part_b[...] + part_c[...]))
    out_ref[...] = total.astype(BF16)
    current = out_ref[...].astype(F32)
    scaled = (current * gain_ref[pl.ds(layer_no, 1), :].astype(F32)).astype(BF16)
    store_squares(packed, current, stride, blocks)
    store_zeros(packed, requests, stride, range(blocks + 2, half))
    store_zeros(packed, requests, stride, range(half + blocks, stride))
    gate_copy.wait()
    store_blocks(packed, jnp.dot(scaled, gate[...], preferred_element_type=F32), stride, 0)
    up_copy.wait()
    store_blocks(packed, jnp.dot(scaled, up[...], preferred_element_type=F32), stride, half)
    payload_ref[...] = packed[...].astype(BF16)


def activation_kernel(blocks, received_ref, out_ref):
    half = 32
    rows = 2 * half
    sources = received_ref.shape[0] // rows
    totals = jnp.sum(received_ref[...].astype(F32).reshape(sources, rows, LANES), axis=0)
    squares = totals[blocks : blocks + 1, :] + totals[blocks + 1 : blocks + 2, :]
    inv = lax.rsqrt(squares / D + EPSILON)
    gate = totals[:half] * inv
    act = gate / (1.0 + jnp.exp(-gate)) * (totals[half:] * inv)
    out_ref[...] = jnp.broadcast_to(act[None], (sources, half, LANES)).reshape(-1, LANES).astype(BF16)


def serve_kernel(layer_no, wanted_ref, pool_ref, out_ref, sem):
    requests = out_ref.shape[0]

    def start(r, carry):
        pltpu.make_async_copy(pool_ref.at[layer_no, wanted_ref[r], 0], out_ref.at[r], sem).start()
        return carry

    lax.fori_loop(0, requests, start, 0)
    pltpu.make_async_copy(pool_ref.at[layer_no, :, 0], out_ref, sem).wait()


def exchange(array, n_req):
    shape = array.shape
    blocks = array.reshape((n_req, shape[0] // n_req) + shape[1:])
    return lax.all_to_all(blocks, "req", split_axis=0, concat_axis=0, tiled=True).reshape(shape)


def tp_parts(partial_sum):
    n_tp = lax.axis_size("tp")
    return [
        lax.ppermute(partial_sum, "tp", [(i, (i + shift) % n_tp) for i in range(n_tp)])
        for shift in (2, 1, 3)
    ]


def shards(
    hidden,
    attn_gain,
    q_weight,
    o_weight,
    ffn_gain,
    gate_weight,
    up_weight,
    down_weight,
    kv_pool,
    block_home,
    chosen,
    chosen_count,
):
    n_req = lax.axis_size("req")
    requests, width = hidden.shape
    most_sel = chosen.shape[3]
    pool_dev = kv_pool.shape[1]
    block_tokens, head_size = kv_pool.shape[4:]
    heads = q_weight.shape[2] // head_size
    hidden_units = gate_weight.shape[2]
    q_rows = 16
    f_rows = 32
    blocks = hidden_units // LANES
    position = float(block_home.shape[1] * block_tokens - 1)
    tables = rotary_tables(position, head_size)
    dma = pltpu.SemaphoreType.DMA

    store_ids = jnp.arange(n_req)
    homes = block_home[0]
    at_store = homes[None, :] // pool_dev == store_ids[:, None]
    slots = jnp.sum(jnp.where(at_store, homes[None, :] % pool_dev, 0), axis=1)
    wanted = exchange(slots.astype(jnp.int32).reshape(n_req, 1), n_req).reshape(n_req)
    fetched, biases = [], []
    for layer_no in range(LAYERS):
        served = call(
            functools.partial(serve_kernel, layer_no),
            jax.ShapeDtypeStruct((n_req, 2, block_tokens, head_size), BF16),
            [SMEM, ANY],
            [dma],
            out_specs=ANY,
        )(wanted, kv_pool)
        fetched.append(exchange(served, n_req))
        stores = jnp.sum(
            jnp.where(chosen[layer_no, 0, 0][:, None] == store_ids[None, :], homes[None, :] // pool_dev, 0),
            axis=1,
        )
        used = jnp.arange(most_sel) < chosen_count[layer_no, 0, 0]
        valid = jnp.any((stores[None, :] == store_ids[:, None]) & used[None, :], axis=1)
        bias = jnp.where(valid, 0.0, -1.0).astype(F32)
        biases.append(jnp.broadcast_to(bias[:, None], (n_req, block_tokens)).reshape(1, -1))

    current = hidden
    parts = None
    for layer_no in range(LAYERS):
        payload_shape = jax.ShapeDtypeStruct((requests * q_rows, LANES), BF16)
        scratch = [
            pltpu.VMEM(q_weight.shape[1:], BF16),
            pltpu.VMEM((requests * q_rows, LANES), F32),
            dma,
        ]
        if parts is None:
            payload = call(
                functools.partial(first_query_kernel, layer_no),
                payload_shape,
                [VMEM, VMEM, ANY],
                scratch,
            )(current, attn_gain, q_weight)
        else:
            current, payload = call(
                functools.partial(query_kernel, layer_no),
                [jax.ShapeDtypeStruct(current.shape, BF16), payload_shape],
                [VMEM] * 6 + [ANY],
                scratch,
            )(current, *parts, attn_gain, q_weight)
        received = exchange(payload, n_req)
        context = call(
            attention_kernel,
            jax.ShapeDtypeStruct((n_req * heads, LANES), BF16),
            [VMEM] * 4,
        )(received, tables, biases[layer_no], fetched[layer_no])
        contexts = exchange(context, n_req)
        own = call(
            functools.partial(project_kernel, layer_no, requests),
            jax.ShapeDtypeStruct((requests, width), F32),
            [VMEM, ANY],
            [pltpu.VMEM(o_weight.shape[1:], BF16), pltpu.VMEM(contexts.shape, F32), dma],
        )(contexts, o_weight)
        attended, payload = call(
            functools.partial(gate_up_kernel, layer_no),
            [
                jax.ShapeDtypeStruct(current.shape, BF16),
                jax.ShapeDtypeStruct((requests * 2 * f_rows, LANES), BF16),
            ],
            [VMEM] * 6 + [ANY] * 2,
            [
                pltpu.VMEM(gate_weight.shape[1:], BF16),
                pltpu.VMEM(up_weight.shape[1:], BF16),
                pltpu.VMEM((requests * 2 * f_rows, LANES), F32),
                dma((2,)),
            ],
        )(current, own, *tp_parts(own), ffn_gain, gate_weight, up_weight)
        received = exchange(payload, n_req)
        act = call(
            functools.partial(activation_kernel, blocks),
            jax.ShapeDtypeStruct((n_req * f_rows, LANES), BF16),
            [VMEM],
        )(received)
        acts = exchange(act, n_req)
        own = call(
            functools.partial(project_kernel, layer_no, requests),
            jax.ShapeDtypeStruct((requests, width), F32),
            [VMEM, ANY],
            [pltpu.VMEM(down_weight.shape[1:], BF16), pltpu.VMEM(acts.shape, F32), dma],
        )(acts, down_weight)
        current, parts = attended, [own] + tp_parts(own)
    total = (parts[0] + parts[1]) + (parts[2] + parts[3])
    return (current.astype(F32) + total).astype(BF16)


def solution(mesh):
    return jax.shard_map(
        shards,
        mesh=mesh,
        in_specs=(
            P(None, "req"),
            P(None, "req"),
            P(None, "req", "tp"),
            P(None, "tp", "req"),
            P(None, "req"),
            P(None, "req", "tp"),
            P(None, "req", "tp"),
            P(None, "tp", "req"),
            P(None, "req", "tp", None, None, None),
            P("req", None),
            P(None, "req", "tp", None),
            P(None, "req", "tp"),
        ),
        out_specs=P(None, "req"),
        check_vma=False,
    )
```

```python
import functools
import math

import jax
import jax.numpy as jnp
import numpy as np
from jax import lax
from jax.experimental import pallas as pl
from jax.experimental.pallas import tpu as pltpu
from jax.sharding import PartitionSpec as P

D = 8192
LAYERS = 2
LANES = 128

MASK_FILL = -1e30
EPSILON = 1e-05

VMEM = pl.BlockSpec(memory_space=pltpu.VMEM)
SMEM = pl.BlockSpec(memory_space=pltpu.SMEM)
HBM = pl.BlockSpec(memory_space=pltpu.HBM)
F32 = jnp.float32
BF16 = jnp.bfloat16


def rotary_tables(position, head_size):
    freq_idx = np.arange(head_size // 2)
    angles = position * np.exp(freq_idx * (-2.0 * math.log(500000.0) / head_size))
    cosine, sine_part = np.cos(angles), np.sin(angles)
    scale = head_size**-0.5
    tables = np.stack([np.concatenate([cosine, cosine]), np.concatenate([-sine_part, sine_part])])
    return jnp.asarray(tables * scale, F32)


def call(kernel, out_shape, in_specs, scratch=(), limit=16, out_specs=None, flops=0, nbytes=0):
    return pl.pallas_call(
        kernel,
        out_shape=out_shape,
        in_specs=in_specs,
        out_specs=out_specs if out_specs is not None else jax.tree.map(lambda _: VMEM, out_shape),
        scratch_shapes=list(scratch),
        compiler_params=pltpu.CompilerParams(vmem_limit_bytes=limit * 1024 * 1024),
        cost_estimate=pl.CostEstimate(flops=flops, bytes_accessed=nbytes, transcendentals=0),
    )


def store_squares(packed, current, stride, row):
    requests = current.shape[0]
    squares = jnp.sum(current * current, axis=1, keepdims=True)
    high = squares.astype(BF16).astype(F32)
    packed[pl.ds(row, requests, stride=stride), :] = jnp.broadcast_to(high, (requests, LANES))
    packed[pl.ds(row + 1, requests, stride=stride), :] = jnp.broadcast_to(
        squares - high, (requests, LANES)
    )


def store_blocks(packed, product, stride, row):
    requests, width = product.shape
    for k in range(width // LANES):
        packed[pl.ds(row + k, requests, stride=stride), :] = product[:, k * LANES : (k + 1) * LANES]


def store_zeros(packed, requests, stride, rows):
    for row in rows:
        packed[pl.ds(row, requests, stride=stride), :] = jnp.zeros((requests, LANES), F32)


def queries_of(current, gain, weight, packed, payload_ref, slots=None):
    requests = current.shape[0]
    heads = weight.shape[1] // LANES
    stride = packed.shape[0] // requests
    scaled = (current * gain).astype(BF16)
    product = jnp.dot(scaled, weight[...], preferred_element_type=F32)
    store_blocks(packed, product, stride, 0)
    store_squares(packed, current, stride, heads)
    first = heads + 2
    if slots is not None:
        packed[pl.ds(first, requests, stride=stride), :] = slots
        first += 1
    store_zeros(packed, requests, stride, range(first, stride))
    payload_ref[...] = packed[...].astype(BF16)


def first_query_kernel(pool_dev, x_hbm, gain_hbm, weight_hbm, homes_hbm, payload_ref, x, gain, weight, homes, packed, sems):
    copies = [
        pltpu.make_async_copy(weight_hbm.at[0], weight, sems.at[0]),
        pltpu.make_async_copy(x_hbm, x, sems.at[1]),
        pltpu.make_async_copy(gain_hbm, gain, sems.at[2]),
        pltpu.make_async_copy(homes_hbm, homes, sems.at[3]),
    ]
    for copy in copies:
        copy.start()
    copies[3].wait()
    requests = x.shape[0]
    n_blocks = homes.shape[1]
    places = jnp.broadcast_to(homes[...], (requests, n_blocks))
    store_ids = lax.broadcasted_iota(jnp.int32, (requests, n_blocks), 0)
    here = lax.div(places, pool_dev) == store_ids
    slots = jnp.sum(jnp.where(here, lax.rem(places, pool_dev), 0).astype(F32), axis=1, keepdims=True)
    slots = jnp.broadcast_to(slots, (requests, LANES))
    copies[1].wait()
    copies[2].wait()
    copies[0].wait()
    queries_of(x[...].astype(F32), gain[0:1, :].astype(F32), weight, packed, payload_ref, slots)


def query_kernel(
    layer_no, x_ref, own, part_a, part_b, part_c, gain_ref, weight_hbm, out_ref, payload_ref, weight, packed, sem
):
    copy = pltpu.make_async_copy(weight_hbm.at[layer_no], weight, sem)
    copy.start()
    total = x_ref[...].astype(F32) + ((own[...] + part_a[...]) + (part_b[...] + part_c[...]))
    out_ref[...] = total.astype(BF16)
    current = out_ref[...].astype(F32)
    copy.wait()
    gain = gain_ref[layer_no : layer_no + 1, :].astype(F32)
    queries_of(current, gain, weight, packed, payload_ref)


def rotate_kernel(sources, received_ref, tables_ref, out_ref):
    rows = received_ref.shape[0] // sources
    heads = out_ref.shape[0] // sources
    totals = jnp.sum(received_ref[...].astype(F32).reshape(sources, rows, LANES), axis=0)
    squares = totals[heads : heads + 1, :] + totals[heads + 1 : heads + 2, :]
    queries = totals[:heads] * lax.rsqrt(squares / D + EPSILON)
    queries = queries * tables_ref[0:1, :] + pltpu.roll(queries, LANES // 2, 1) * tables_ref[1:2, :]
    out_ref[...] = jnp.broadcast_to(queries[None], (sources, heads, LANES)).reshape(-1, LANES).astype(BF16)


def in_parts(values, count):
    parts = []
    for _ in range(count):
        part = values.astype(BF16).astype(F32)
        parts.append(part)
        values = values - part
    return parts


def block_kernel(layer_no, wanted_ref, queries_ref, pool_hbm, out_ref, blocks, sem):
    copy = pltpu.make_async_copy(pool_hbm.at[layer_no, :, 0], blocks, sem)
    copy.start()
    requests = wanted_ref.shape[0]
    heads = queries_ref.shape[0] // requests
    queries = queries_ref[...].astype(F32)
    copy.wait()
    scores = jnp.concatenate(
        [
            lax.dot_general(
                queries[r * heads : (r + 1) * heads].astype(BF16),
                blocks[wanted_ref[r], 0],
                (((1,), (1,)), ((), ())),
                preferred_element_type=F32,
            )
            for r in range(requests)
        ],
        axis=0,
    )
    block_max = jnp.max(scores, axis=1, keepdims=True)
    terms = jnp.exp(scores - block_max)
    block_sum = jnp.sum(terms, axis=1, keepdims=True)
    acc = jnp.concatenate(
        [
            jnp.dot(
                terms[r * heads : (r + 1) * heads].astype(BF16),
                blocks[wanted_ref[r], 1],
                preferred_element_type=F32,
            )
            for r in range(requests)
        ],
        axis=0,
    )
    lane = lax.broadcasted_iota(jnp.int32, scores.shape, 1)
    stats = jnp.zeros(scores.shape, F32)
    for place, part in enumerate(in_parts(block_max, 3) + in_parts(block_sum, 2)):
        stats = jnp.where(lane == place, part, stats)
    both = jnp.concatenate(
        [acc.reshape(requests, heads, LANES), stats.reshape(requests, heads, LANES)], axis=1
    )
    out_ref[...] = both.reshape(-1, LANES).astype(BF16)


def combine_kernel(layer_no, pool_dev, homes_ref, chosen_ref, count_ref, received_ref, out_ref, used):
    sources = homes_ref.shape[1]
    heads = out_ref.shape[0] // sources
    for s in range(sources):
        used[s] = 0
    for k in range(chosen_ref.shape[3]):
        store = lax.div(homes_ref[0, chosen_ref[layer_no, 0, 0, k]], pool_dev)
        used[store] = jnp.where(k < count_ref[layer_no, 0, 0], 1, used[store])
    both = received_ref[...].astype(F32).reshape(sources, 2 * heads, LANES)
    stats = both[:, heads:, :]
    block_max = stats[:, :, 0:1] + stats[:, :, 1:2] + stats[:, :, 2:3]
    block_sum = stats[:, :, 3:4] + stats[:, :, 4:5]
    masked = [jnp.where(used[s] > 0, block_max[s], MASK_FILL) for s in range(sources)]
    top = functools.reduce(jnp.maximum, masked)
    numerator = jnp.zeros((heads, LANES), F32)
    denominator = jnp.zeros((heads, 1), F32)
    for s in range(sources):
        rescale = jnp.exp(masked[s] - top)
        numerator += rescale * both[s, :heads, :]
        denominator += rescale * block_sum[s]
    context = numerator / denominator
    out_ref[...] = jnp.broadcast_to(context[None], (sources, heads, LANES)).reshape(-1, LANES).astype(BF16)


def rows_of(packed, requests, blocks):
    stride = packed.shape[0] // requests
    return jnp.concatenate(
        [packed[pl.ds(k, requests, stride=stride), :].astype(BF16) for k in range(blocks)], axis=1
    )


def project_kernel(layer_no, requests, received_ref, weight_ref, out_ref, weight, packed, sem):
    copy = pltpu.make_async_copy(weight_ref.at[layer_no], weight, sem)
    copy.start()
    packed[...] = received_ref[...].astype(F32)
    rows = rows_of(packed, requests, weight.shape[0] // LANES)
    copy.wait()
    out_ref[...] = jnp.dot(rows, weight[...], preferred_element_type=F32)


def gate_up_kernel(
    layer_no,
    x_ref,
    own,
    part_a,
    part_b,
    part_c,
    gain_ref,
    gate_ref,
    up_ref,
    out_ref,
    payload_ref,
    gate,
    up,
    packed,
    sems,
):
    gate_copy = pltpu.make_async_copy(gate_ref.at[layer_no], gate, sems.at[0])
    up_copy = pltpu.make_async_copy(up_ref.at[layer_no], up, sems.at[1])
    gate_copy.start()
    up_copy.start()
    requests = x_ref.shape[0]
    stride = packed.shape[0] // requests
    half = stride // 2
    blocks = gate.shape[1] // LANES
    total = x_ref[...].astype(F32) + ((own[...] + part_a[...]) + (part_b[...] + part_c[...]))
    out_ref[...] = total.astype(BF16)
    current = out_ref[...].astype(F32)
    scaled = (current * gain_ref[layer_no : layer_no + 1, :].astype(F32)).astype(BF16)
    store_squares(packed, current, stride, blocks)
    store_zeros(packed, requests, stride, range(blocks + 2, half))
    store_zeros(packed, requests, stride, range(half + blocks, stride))
    gate_copy.wait()
    store_blocks(packed, jnp.dot(scaled, gate[...], preferred_element_type=F32), stride, 0)
    up_copy.wait()
    store_blocks(packed, jnp.dot(scaled, up[...], preferred_element_type=F32), stride, half)
    payload_ref[...] = packed[...].astype(BF16)


def activation_kernel(blocks, received_ref, out_ref):
    half = 32
    rows = 2 * half
    sources = received_ref.shape[0] // rows
    totals = jnp.sum(received_ref[...].astype(F32).reshape(sources, rows, LANES), axis=0)
    squares = totals[blocks : blocks + 1, :] + totals[blocks + 1 : blocks + 2, :]
    inv = lax.rsqrt(squares / D + EPSILON)
    gate = totals[:half] * inv
    act = gate / (1.0 + jnp.exp(-gate)) * (totals[half:] * inv)
    out_ref[...] = jnp.broadcast_to(act[None], (sources, half, LANES)).reshape(-1, LANES).astype(BF16)


def exchange(array, n_req):
    shape = array.shape
    blocks = array.reshape((n_req, shape[0] // n_req) + shape[1:])
    return lax.all_to_all(blocks, "req", split_axis=0, concat_axis=0, tiled=True).reshape(shape)


def tp_parts(partial_sum):
    n_tp = lax.axis_size("tp")
    return [
        lax.ppermute(partial_sum, "tp", [(i, (i + shift) % n_tp) for i in range(n_tp)])
        for shift in (2, 1, 3)
    ]


def shards(
    hidden,
    attn_gain,
    q_weight,
    o_weight,
    ffn_gain,
    gate_weight,
    up_weight,
    down_weight,
    kv_pool,
    block_home,
    chosen,
    chosen_count,
):
    n_req = lax.axis_size("req")
    requests, width = hidden.shape
    pool_dev = kv_pool.shape[1]
    block_tokens, head_size = kv_pool.shape[4:]
    heads = q_weight.shape[2] // head_size
    hidden_units = gate_weight.shape[2]
    q_rows = 16
    f_rows = 32
    blocks = hidden_units // LANES
    position = float(block_home.shape[1] * block_tokens - 1)
    tables = rotary_tables(position, head_size)
    dma = pltpu.SemaphoreType.DMA

    current = hidden
    parts = None
    wanted = None
    for layer_no in range(LAYERS):
        payload_shape = jax.ShapeDtypeStruct((requests * q_rows, LANES), BF16)
        packed = pltpu.VMEM((requests * q_rows, LANES), F32)
        weight = pltpu.VMEM(q_weight.shape[1:], BF16)
        if parts is None:
            payload = call(
                functools.partial(first_query_kernel, pool_dev),
                payload_shape,
                [HBM] * 4,
                [
                    pltpu.VMEM(hidden.shape, BF16),
                    pltpu.VMEM(attn_gain.shape, BF16),
                    weight,
                    pltpu.VMEM(block_home.shape, jnp.int32),
                    packed,
                    dma((4,)),
                ],
            )(current, attn_gain, q_weight, block_home)
        else:
            current, payload = call(
                functools.partial(query_kernel, layer_no),
                [jax.ShapeDtypeStruct(current.shape, BF16), payload_shape],
                [VMEM] * 6 + [HBM],
                [weight, packed, dma],
            )(current, *parts, attn_gain, q_weight)
        received = exchange(payload, n_req)
        if wanted is None:
            wanted = received.reshape(n_req, q_rows, LANES)[:, heads + 2, 0].astype(jnp.int32)
        rotated = call(
            functools.partial(rotate_kernel, n_req),
            jax.ShapeDtypeStruct((n_req * heads, LANES), BF16),
            [VMEM] * 2,
        )(received, tables)
        queries = exchange(rotated, n_req)
        stats = call(
            functools.partial(block_kernel, layer_no),
            jax.ShapeDtypeStruct((requests * 2 * heads, LANES), BF16),
            [SMEM, VMEM, HBM],
            [pltpu.VMEM((pool_dev, 2, block_tokens, head_size), BF16), dma],
        )(wanted, queries, kv_pool)
        context = call(
            functools.partial(combine_kernel, layer_no, pool_dev),
            jax.ShapeDtypeStruct((n_req * heads, LANES), BF16),
            [SMEM] * 3 + [VMEM],
            [pltpu.SMEM((n_req,), jnp.int32)],
        )(block_home, chosen, chosen_count, exchange(stats, n_req))
        contexts = exchange(context, n_req)
        own = call(
            functools.partial(project_kernel, layer_no, requests),
            jax.ShapeDtypeStruct((requests, width), F32),
            [VMEM, HBM],
            [pltpu.VMEM(o_weight.shape[1:], BF16), pltpu.VMEM(contexts.shape, F32), dma],
        )(contexts, o_weight)
        attended, payload = call(
            functools.partial(gate_up_kernel, layer_no),
            [
                jax.ShapeDtypeStruct(current.shape, BF16),
                jax.ShapeDtypeStruct((requests * 2 * f_rows, LANES), BF16),
            ],
            [VMEM] * 6 + [HBM] * 2,
            [
                pltpu.VMEM(gate_weight.shape[1:], BF16),
                pltpu.VMEM(up_weight.shape[1:], BF16),
                pltpu.VMEM((requests * 2 * f_rows, LANES), F32),
                dma((2,)),
            ],
        )(current, own, *tp_parts(own), ffn_gain, gate_weight, up_weight)
        received = exchange(payload, n_req)
        act = call(
            functools.partial(activation_kernel, blocks),
            jax.ShapeDtypeStruct((n_req * f_rows, LANES), BF16),
            [VMEM],
        )(received)
        acts = exchange(act, n_req)
        own = call(
            functools.partial(project_kernel, layer_no, requests),
            jax.ShapeDtypeStruct((requests, width), F32),
            [VMEM, HBM],
            [pltpu.VMEM(down_weight.shape[1:], BF16), pltpu.VMEM(acts.shape, F32), dma],
        )(acts, down_weight)
        current, parts = attended, [own] + tp_parts(own)
    total = (parts[0] + parts[1]) + (parts[2] + parts[3])
    return (current.astype(F32) + total).astype(BF16)


def solution(mesh):
    return jax.shard_map(
        shards,
        mesh=mesh,
        in_specs=(
            P(None, "req"),
            P(None, "req"),
            P(None, "req", "tp"),
            P(None, "tp", "req"),
            P(None, "req"),
            P(None, "req", "tp"),
            P(None, "req", "tp"),
            P(None, "tp", "req"),
            P(None, "req", "tp", None, None, None),
            P("req", None),
            P(None, "req", "tp", None),
            P(None, "req", "tp"),
        ),
        out_specs=P(None, "req"),
        check_vma=False,
    )
```

```python
import functools
import math

import jax
import jax.numpy as jnp
import numpy as np
from jax import lax
from jax.experimental import pallas as pl
from jax.experimental.pallas import tpu as pltpu
from jax.sharding import PartitionSpec as P

D = 8192
LAYERS = 2
LANES = 128

MASK_FILL = -1e30
EPSILON = 1e-05

VMEM = pl.BlockSpec(memory_space=pltpu.VMEM)
SMEM = pl.BlockSpec(memory_space=pltpu.SMEM)
HBM = pl.BlockSpec(memory_space=pltpu.HBM)
F32 = jnp.float32
BF16 = jnp.bfloat16


def rotary_tables(position, head_size):
    freq_idx = np.arange(head_size // 2)
    angles = position * np.exp(freq_idx * (-2.0 * math.log(500000.0) / head_size))
    cosine, sine_part = np.cos(angles), np.sin(angles)
    scale = head_size**-0.5
    tables = np.stack([np.concatenate([cosine, cosine]), np.concatenate([-sine_part, sine_part])])
    return jnp.asarray(tables * scale, F32)


def call(kernel, out_shape, in_specs, scratch=(), limit=16, out_specs=None, flops=0, nbytes=0):
    return pl.pallas_call(
        kernel,
        out_shape=out_shape,
        in_specs=in_specs,
        out_specs=out_specs if out_specs is not None else jax.tree.map(lambda _: VMEM, out_shape),
        scratch_shapes=list(scratch),
        compiler_params=pltpu.CompilerParams(vmem_limit_bytes=limit * 1024 * 1024),
        cost_estimate=pl.CostEstimate(flops=flops, bytes_accessed=nbytes, transcendentals=0),
    )


def halves(values):
    middle = values.shape[0] // 2
    first = lax.rem(lax.axis_index("req"), 2) == 0
    keep = jnp.where(first, values[:middle], values[middle:])
    send = jnp.where(first, values[middle:], values[:middle])
    return keep, send


def joined(own, other):
    first = lax.rem(lax.axis_index("req"), 2) == 0
    return jnp.concatenate([jnp.where(first, own, other), jnp.where(first, other, own)], axis=0)


def squares_in_lanes(current):
    squares = jnp.sum(current * current, axis=1, keepdims=True)
    high = squares.astype(BF16).astype(F32)
    lane = lax.broadcasted_iota(jnp.int32, (current.shape[0], LANES), 1)
    return jnp.where(lane == 0, high, jnp.where(lane == 1, squares - high, 0.0))


def store_blocks(packed, product, stride, row):
    requests, width = product.shape
    for k in range(width // LANES):
        packed[pl.ds(row + k, requests, stride=stride), :] = product[:, k * LANES : (k + 1) * LANES]


def spread(packed, values, stride):
    for k in range(stride):
        packed[pl.ds(k, values.shape[0], stride=stride), :] = values
    return packed[...]


def rows_of(packed, requests, blocks):
    stride = packed.shape[0] // requests
    return jnp.concatenate(
        [packed[pl.ds(k, requests, stride=stride), :].astype(BF16) for k in range(blocks)], axis=1
    )


def repeat_into(out_ref, values):
    rows = values.shape[0]
    for i in range(out_ref.shape[0] // rows):
        out_ref[i * rows : (i + 1) * rows, :] = values


def queries_of(current, gain, weight, packed, keep_ref, send_ref, table=None):
    requests = current.shape[0]
    heads = weight.shape[1] // LANES
    scaled = (current * gain).astype(BF16)
    product = jnp.dot(scaled, weight[...], preferred_element_type=F32)
    store_blocks(packed, product, heads, 0)
    extra = squares_in_lanes(current)
    if table is not None:
        extra = extra + table
    rows = packed.shape[0] // 2
    keep, send = halves(packed[...])
    keep_ref[:rows, :] = keep
    send_ref[:rows, :] = send.astype(BF16)
    keep, send = halves(extra)
    keep_ref[rows:, :] = keep
    send_ref[rows:, :] = send.astype(BF16)


def slot_table(homes, chosen, counts, pool_dev, requests):
    n_blocks = homes.shape[1]
    shape = (n_blocks, n_blocks)
    row = lax.broadcasted_iota(jnp.int32, shape, 0)
    col = lax.broadcasted_iota(jnp.int32, shape, 1)
    places = jnp.broadcast_to(homes, shape)
    here = lax.div(places, pool_dev) == row

    def across(column):
        return jnp.sum(jnp.where(row == col, column, 0.0), axis=0, keepdims=True)

    slots = jnp.sum(jnp.where(here, lax.rem(places, pool_dev), 0).astype(F32), axis=1, keepdims=True)
    found = [jnp.zeros((1, n_blocks), F32), across(slots)]
    for layer_no in range(LAYERS):
        listed = chosen[layer_no]
        entry = lax.broadcasted_iota(jnp.int32, (n_blocks, listed.shape[1]), 1)
        block = lax.broadcasted_iota(jnp.int32, (n_blocks, listed.shape[1]), 0)
        hit = (listed == block) & (entry < counts[layer_no])
        taken = across(jnp.max(jnp.where(hit, 1.0, 0.0), axis=1, keepdims=True))
        found.append(across(jnp.max(jnp.where(here, taken, 0.0), axis=1, keepdims=True)))
    line = jnp.concatenate(found, axis=1)
    mine = lax.broadcasted_iota(jnp.int32, (requests, LANES), 0) == lax.axis_index("req")
    return jnp.where(mine, line, 0.0)


def first_query_kernel(
    pool_dev,
    x_hbm,
    gain_hbm,
    weight_hbm,
    homes_hbm,
    chosen_hbm,
    count_hbm,
    keep_ref,
    send_ref,
    x,
    gain,
    weight,
    homes,
    chosen,
    counts,
    packed,
    sems,
):
    copies = [
        pltpu.make_async_copy(source, target, sems.at[i])
        for i, (source, target) in enumerate(
            [
                (homes_hbm, homes),
                (chosen_hbm, chosen),
                (count_hbm, counts),
                (x_hbm, x),
                (gain_hbm, gain),
                (weight_hbm.at[0], weight),
            ]
        )
    ]
    for copy in copies:
        copy.start()
    for copy in copies[:3]:
        copy.wait()
    lists = [chosen[i : i + 1, :] for i in range(LAYERS)]
    limits = [counts[i : i + 1, :] for i in range(LAYERS)]
    table = slot_table(homes[...], lists, limits, pool_dev, x.shape[0])
    for copy in copies[3:]:
        copy.wait()
    queries_of(x[...].astype(F32), gain[0:1, :].astype(F32), weight, packed, keep_ref, send_ref, table)


def query_kernel(
    layer_no, x_ref, own, part_a, part_b, part_c, gain_ref, weight_hbm, out_ref, keep_ref, send_ref, weight, packed, sem
):
    copy = pltpu.make_async_copy(weight_hbm.at[layer_no], weight, sem)
    copy.start()
    total = x_ref[...].astype(F32) + ((own[...] + part_a[...]) + (part_b[...] + part_c[...]))
    out_ref[...] = total.astype(BF16)
    current = out_ref[...].astype(F32)
    copy.wait()
    gain = gain_ref[layer_no : layer_no + 1, :].astype(F32)
    queries_of(current, gain, weight, packed, keep_ref, send_ref)


def pair_sum_kernel(keep_ref, received_ref, out_ref):
    repeat_into(out_ref, (keep_ref[...] + received_ref[...].astype(F32)).astype(BF16))


def rotate_kernel(heads, received_ref, tables_ref, out_ref, factors):
    rows = factors.shape[0]
    sources = received_ref.shape[0] // (rows + rows // heads)
    totals = jnp.sum(received_ref[...].astype(F32).reshape(sources, -1, LANES), axis=0)
    extra = totals[rows:]
    inv = lax.rsqrt((extra[:, 0:1] + extra[:, 1:2]) / D + EPSILON)
    queries = totals[:rows] * spread(factors, jnp.broadcast_to(inv, extra.shape), heads)
    queries = queries * tables_ref[0:1, :] + pltpu.roll(queries, LANES // 2, 1) * tables_ref[1:2, :]
    out_ref[:rows, :] = queries.astype(BF16)
    if out_ref.shape[0] > rows:
        out_ref[rows:, :] = extra.astype(BF16)


def in_parts(values, count):
    parts = []
    for _ in range(count):
        part = values.astype(BF16).astype(F32)
        parts.append(part)
        values = values - part
    return parts


def stats_in_lanes(block_max, block_sum):
    shape = (block_max.shape[0], LANES)
    lane = lax.broadcasted_iota(jnp.int32, shape, 1)
    stats = jnp.zeros(shape, F32)
    for place, part in enumerate(in_parts(block_max, 3) + in_parts(block_sum, 2)):
        stats = jnp.where(lane == place, part, stats)
    return stats


def block_kernel(
    layer_no, own_ref, other_ref, own_table, other_table, pool_hbm, keep_ref, send_ref, blocks, packed, sem
):
    copy = pltpu.make_async_copy(pool_hbm.at[layer_no, :, 0], blocks, sem)
    copy.start()
    rows = packed.shape[0]
    n_slots = blocks.shape[0]
    requests = 2 * (own_table.shape[0] - rows // 2)
    heads = rows // requests
    me = lax.axis_index("req")
    queries = joined(own_ref[: rows // 2].astype(F32), other_ref[: rows // 2].astype(F32))
    table = joined(own_table[rows // 2 :].astype(F32), other_table[rows // 2 :].astype(F32))
    lane = lax.broadcasted_iota(jnp.int32, table.shape, 1)
    slots = jnp.sum(jnp.where(lane == n_slots + me, table, 0.0), axis=1, keepdims=True)
    used = jnp.sum(jnp.where(lane == (2 + layer_no) * n_slots + me, table, 0.0), axis=1, keepdims=True)
    used = spread(packed, jnp.broadcast_to(used, table.shape), heads)
    request = lax.broadcasted_iota(jnp.int32, (requests, rows), 0)
    column = lax.broadcasted_iota(jnp.int32, (requests, rows), 1)
    target = jnp.where(
        lax.div(column, heads) == request, slots * heads + lax.rem(column, heads).astype(F32), 0.0
    )
    target = jnp.sum(target, axis=0, keepdims=True).astype(jnp.int32)
    place = lax.broadcasted_iota(jnp.int32, (rows, rows), 0) == target
    by_slot = jnp.where(place, 1.0, 0.0)
    queries = jnp.dot(by_slot.astype(BF16), queries.astype(BF16), preferred_element_type=F32)
    copy.wait()
    scores = jnp.concatenate(
        [
            lax.dot_general(
                queries[p * heads : (p + 1) * heads].astype(BF16),
                blocks[p, 0],
                (((1,), (1,)), ((), ())),
                preferred_element_type=F32,
            )
            for p in range(n_slots)
        ],
        axis=0,
    )
    block_max = jnp.max(scores, axis=1, keepdims=True)
    terms = jnp.exp(scores - block_max)
    block_sum = jnp.sum(terms, axis=1, keepdims=True)
    acc = jnp.concatenate(
        [
            jnp.dot(
                terms[p * heads : (p + 1) * heads].astype(BF16), blocks[p, 1], preferred_element_type=F32
            )
            for p in range(n_slots)
        ],
        axis=0,
    )
    both = jnp.concatenate([acc, stats_in_lanes(block_max, block_sum)], axis=1).astype(BF16)
    both = jnp.dot(by_slot.T.astype(BF16), both, preferred_element_type=F32)
    lane = lax.broadcasted_iota(jnp.int32, (rows, LANES), 1)
    unused = jnp.where(lane == 0, MASK_FILL, 0.0)
    stats = jnp.where((used > 0.0) | (lane > 2), both[:, LANES:], unused)
    for at, values in ((0, both[:, :LANES]), (rows // 2, stats)):
        keep, send = halves(values)
        keep_ref[at : at + rows // 2, :] = keep
        send_ref[at : at + rows // 2, :] = send.astype(BF16)


def merge_kernel(keep_ref, received_ref, out_ref):
    rows = keep_ref.shape[0] // 2
    sides = []
    for both in (keep_ref[...], received_ref[...].astype(F32)):
        stats = both[rows:]
        block_max = stats[:, 0:1] + stats[:, 1:2] + stats[:, 2:3]
        sides.append((block_max, stats[:, 3:4] + stats[:, 4:5], both[:rows]))
    top = jnp.maximum(sides[0][0], sides[1][0])
    rescale = [jnp.exp(side[0] - top) for side in sides]
    total = rescale[0] * sides[0][1] + rescale[1] * sides[1][1]
    acc = rescale[0] * sides[0][2] + rescale[1] * sides[1][2]
    stats = stats_in_lanes(top, total).T
    extra = out_ref.shape[0] // 16 - rows
    repeat_into(out_ref, jnp.concatenate([acc, stats[:extra]], axis=0).astype(BF16))


def combine_kernel(sources, received_ref, out_ref):
    rows = out_ref.shape[0]
    both = received_ref[...].astype(F32).reshape(sources, -1, LANES)
    stats = [both[s, rows : rows + 8, :] for s in range(sources)]
    block_max = jnp.concatenate([x[0:1] + x[1:2] + x[2:3] for x in stats], axis=0)
    block_sum = jnp.concatenate([x[3:4] + x[4:5] for x in stats], axis=0)
    rescale = jnp.exp(block_max - jnp.max(block_max, axis=0, keepdims=True))
    factors = rescale / jnp.sum(rescale * block_sum, axis=0, keepdims=True)
    factors = jnp.concatenate([factors, jnp.zeros((LANES - sources, LANES), F32)], axis=0).T
    context = jnp.zeros((rows, LANES), F32)
    for s in range(sources):
        context += both[s, :rows, :] * factors[:, s : s + 1]
    out_ref[...] = context.astype(BF16)


def project_kernel(layer_no, requests, own_ref, other_ref, weight_hbm, out_ref, weight, packed, sem):
    copy = pltpu.make_async_copy(weight_hbm.at[layer_no], weight, sem)
    copy.start()
    packed[...] = joined(own_ref[...].astype(F32), other_ref[...].astype(F32))
    rows = rows_of(packed, requests, weight.shape[0] // LANES)
    copy.wait()
    out_ref[...] = jnp.dot(rows, weight[...], preferred_element_type=F32)


def gate_up_kernel(
    layer_no,
    x_ref,
    own,
    part_a,
    part_b,
    part_c,
    gain_ref,
    gate_hbm,
    up_hbm,
    out_ref,
    keep_ref,
    send_ref,
    gate,
    up,
    packed,
    sems,
):
    gate_copy = pltpu.make_async_copy(gate_hbm.at[layer_no], gate, sems.at[0])
    up_copy = pltpu.make_async_copy(up_hbm.at[layer_no], up, sems.at[1])
    gate_copy.start()
    up_copy.start()
    requests = x_ref.shape[0]
    stride = packed.shape[0] // requests
    half = stride // 2
    blocks = gate.shape[1] // LANES
    total = x_ref[...].astype(F32) + ((own[...] + part_a[...]) + (part_b[...] + part_c[...]))
    out_ref[...] = total.astype(BF16)
    current = out_ref[...].astype(F32)
    scaled = (current * gain_ref[layer_no : layer_no + 1, :].astype(F32)).astype(BF16)
    zeros = jnp.zeros((requests, LANES), F32)
    packed[pl.ds(blocks, requests, stride=stride), :] = squares_in_lanes(current)
    for row in [*range(blocks + 1, half), *range(half + blocks, stride)]:
        packed[pl.ds(row, requests, stride=stride), :] = zeros
    gate_copy.wait()
    store_blocks(packed, jnp.dot(scaled, gate[...], preferred_element_type=F32), stride, 0)
    up_copy.wait()
    store_blocks(packed, jnp.dot(scaled, up[...], preferred_element_type=F32), stride, half)
    keep, send = halves(packed[...])
    keep_ref[...] = keep
    send_ref[...] = send.astype(BF16)


def activation_kernel(blocks, sources, received_ref, out_ref):
    half = out_ref.shape[0] // sources
    totals = jnp.sum(received_ref[...].astype(F32).reshape(sources, 2 * half, LANES), axis=0)
    squares = totals[blocks : blocks + 1, 0:1] + totals[blocks : blocks + 1, 1:2]
    inv = lax.rsqrt(squares / D + EPSILON)
    gate = totals[:half] * inv
    act = gate / (1.0 + jnp.exp(-gate)) * (totals[half:] * inv)
    repeat_into(out_ref, act.astype(BF16))


def exchange(array, n_req):
    shape = array.shape
    sides = [list(range(core, n_req, 2)) for core in range(2)]
    count = n_req // 2
    blocks = array.reshape((count, shape[0] // count) + shape[1:])
    return lax.all_to_all(
        blocks, "req", split_axis=0, concat_axis=0, tiled=True, axis_index_groups=sides
    ).reshape(shape)


def from_pair(array, n_req):
    return lax.ppermute(array, "req", [(i, i ^ 1) for i in range(n_req)])


def tp_parts(partial_sum):
    n_tp = lax.axis_size("tp")
    return [
        lax.ppermute(partial_sum, "tp", [(i, (i + shift) % n_tp) for i in range(n_tp)])
        for shift in (2, 1, 3)
    ]


def shards(
    hidden,
    attn_gain,
    q_weight,
    o_weight,
    ffn_gain,
    gate_weight,
    up_weight,
    down_weight,
    kv_pool,
    block_home,
    chosen,
    chosen_count,
):
    n_req = lax.axis_size("req")
    requests, width = hidden.shape
    pool_dev = kv_pool.shape[1]
    block_tokens, head_size = kv_pool.shape[4:]
    heads = q_weight.shape[2] // head_size
    hidden_units = gate_weight.shape[2]
    side = n_req // 2
    q_rows = requests * heads // 2
    sent_rows = q_rows + requests // 2
    f_rows = 32
    blocks = hidden_units // LANES
    position = float(block_home.shape[1] * block_tokens - 1)
    tables = rotary_tables(position, head_size)
    dma = pltpu.SemaphoreType.DMA

    def rows_type(rows, kind=BF16):
        return jax.ShapeDtypeStruct((rows, LANES), kind)

    def rows_scratch(rows):
        return pltpu.VMEM((rows, LANES), F32)

    current = hidden
    parts = None
    slots = None
    for layer_no in range(LAYERS):
        halves_type = [rows_type(sent_rows, F32), rows_type(sent_rows)]
        packed = rows_scratch(2 * q_rows)
        weight = pltpu.VMEM(q_weight.shape[1:], BF16)
        if parts is None:
            keep, send = call(
                functools.partial(first_query_kernel, pool_dev),
                halves_type,
                [HBM] * 6,
                [
                    pltpu.VMEM(hidden.shape, BF16),
                    pltpu.VMEM(attn_gain.shape, BF16),
                    weight,
                    pltpu.VMEM(block_home.shape, jnp.int32),
                    pltpu.VMEM((LAYERS, chosen.shape[3]), jnp.int32),
                    pltpu.VMEM((LAYERS, 1), jnp.int32),
                    packed,
                    dma((6,)),
                ],
                limit=62,
            )(
                current,
                attn_gain,
                q_weight,
                block_home,
                chosen.reshape(LAYERS, -1),
                chosen_count.reshape(LAYERS, 1),
            )
        else:
            current, keep, send = call(
                functools.partial(query_kernel, layer_no),
                [jax.ShapeDtypeStruct(current.shape, BF16)] + halves_type,
                [VMEM] * 6 + [HBM],
                [weight, packed, dma],
            )(current, *parts, attn_gain, q_weight)
        payload = call(pair_sum_kernel, rows_type(side * sent_rows), [VMEM] * 2)(
            keep, from_pair(send, n_req)
        )
        own = call(
            functools.partial(rotate_kernel, heads),
            rows_type(sent_rows if slots is None else q_rows),
            [VMEM] * 2,
            [rows_scratch(q_rows)],
        )(exchange(payload, n_req), tables)
        other = from_pair(own, n_req)
        if slots is None:
            slots = (own, other)
        keep, send = call(
            functools.partial(block_kernel, layer_no),
            [rows_type(2 * q_rows, F32), rows_type(2 * q_rows)],
            [VMEM] * 4 + [HBM],
            [
                pltpu.VMEM((pool_dev, 2, block_tokens, head_size), BF16),
                rows_scratch(2 * q_rows),
                dma,
            ],
        )(own, other, *slots, kv_pool)
        payload = call(merge_kernel, rows_type(side * sent_rows), [VMEM] * 2)(
            keep, from_pair(send, n_req)
        )
        context = call(functools.partial(combine_kernel, side), rows_type(q_rows), [VMEM])(
            exchange(payload, n_req)
        )
        own = call(
            functools.partial(project_kernel, layer_no, requests),
            jax.ShapeDtypeStruct((requests, width), F32),
            [VMEM, VMEM, HBM],
            [pltpu.VMEM(o_weight.shape[1:], BF16), rows_scratch(2 * q_rows), dma],
        )(context, from_pair(context, n_req), o_weight)
        attended, keep, send = call(
            functools.partial(gate_up_kernel, layer_no),
            [
                jax.ShapeDtypeStruct(current.shape, BF16),
                rows_type(requests * f_rows, F32),
                rows_type(requests * f_rows),
            ],
            [VMEM] * 6 + [HBM] * 2,
            [
                pltpu.VMEM(gate_weight.shape[1:], BF16),
                pltpu.VMEM(up_weight.shape[1:], BF16),
                rows_scratch(requests * 2 * f_rows),
                dma((2,)),
            ],
        )(current, own, *tp_parts(own), ffn_gain, gate_weight, up_weight)
        payload = call(pair_sum_kernel, rows_type(requests * f_rows), [VMEM] * 2)(
            keep, from_pair(send, n_req)
        )
        act = call(
            functools.partial(activation_kernel, blocks, side), rows_type(side * f_rows), [VMEM]
        )(exchange(payload, n_req))
        acts = exchange(act, n_req)
        own = call(
            functools.partial(project_kernel, layer_no, requests),
            jax.ShapeDtypeStruct((requests, width), F32),
            [VMEM, VMEM, HBM],
            [pltpu.VMEM(down_weight.shape[1:], BF16), rows_scratch(requests * f_rows), dma],
        )(acts, from_pair(acts, n_req), down_weight)
        current, parts = attended, [own] + tp_parts(own)
    total = (parts[0] + parts[1]) + (parts[2] + parts[3])
    return (current.astype(F32) + total).astype(BF16)


def solution(mesh):
    return jax.shard_map(
        shards,
        mesh=mesh,
        in_specs=(
            P(None, "req"),
            P(None, "req"),
            P(None, "req", "tp"),
            P(None, "tp", "req"),
            P(None, "req"),
            P(None, "req", "tp"),
            P(None, "req", "tp"),
            P(None, "tp", "req"),
            P(None, "req", "tp", None, None, None),
            P("req", None),
            P(None, "req", "tp", None),
            P(None, "req", "tp"),
        ),
        out_specs=P(None, "req"),
        check_vma=False,
    )
```

```python
import functools
import math

import jax
import jax.numpy as jnp
import numpy as np
from jax import lax
from jax.experimental import pallas as pl
from jax.experimental.pallas import tpu as pltpu
from jax.sharding import PartitionSpec as P

D = 8192
LAYERS = 2
LANES = 128

MASK_FILL = -1e30
EPSILON = 1e-05

VMEM = pl.BlockSpec(memory_space=pltpu.VMEM)
SMEM = pl.BlockSpec(memory_space=pltpu.SMEM)
HBM = pl.BlockSpec(memory_space=pltpu.HBM)
F32 = jnp.float32
BF16 = jnp.bfloat16


def rotary_tables(position, head_size):
    freq_idx = np.arange(head_size // 2)
    angles = position * np.exp(freq_idx * (-2.0 * math.log(500000.0) / head_size))
    cosine, sine_part = np.cos(angles), np.sin(angles)
    scale = head_size**-0.5
    tables = np.stack([np.concatenate([cosine, cosine]), np.concatenate([-sine_part, sine_part])])
    return jnp.asarray(tables * scale, F32)


def call(kernel, out_shape, in_specs, scratch=(), limit=16, out_specs=None, flops=0, nbytes=0):
    return pl.pallas_call(
        kernel,
        out_shape=out_shape,
        in_specs=in_specs,
        out_specs=out_specs if out_specs is not None else jax.tree.map(lambda _: VMEM, out_shape),
        scratch_shapes=list(scratch),
        compiler_params=pltpu.CompilerParams(vmem_limit_bytes=limit * 1024 * 1024),
        cost_estimate=pl.CostEstimate(flops=flops, bytes_accessed=nbytes, transcendentals=0),
    )


def core_side():
    return lax.rem(lax.axis_index("req"), 2)


def joined(own, other, axis):
    first = core_side() == 0
    return jnp.concatenate([jnp.where(first, own, other), jnp.where(first, other, own)], axis=axis)


def pair_copies(own_hbm, other_hbm, own_target, other_target, sems):
    return [
        pltpu.make_async_copy(own_hbm, own_target, sems.at[0]),
        pltpu.make_async_copy(other_hbm, other_target, sems.at[1]),
    ]


def side_slices(size):
    side = core_side()
    return (
        pl.ds(pl.multiple_of(side * size, LANES), size),
        pl.ds(pl.multiple_of((1 - side) * size, LANES), size),
    )


def column_copies(layer_no, own_hbm, other_hbm, weight, sems):
    own, other = side_slices(own_hbm.shape[2])
    return pair_copies(
        own_hbm.at[layer_no], other_hbm.at[layer_no], weight.at[:, own], weight.at[:, other], sems
    )


def row_copies(layer_no, own_hbm, other_hbm, weight, sems):
    half, _ = side_slices(weight.shape[1])
    own, other = side_slices(own_hbm.shape[1])
    return pair_copies(
        own_hbm.at[layer_no, :, half],
        other_hbm.at[layer_no, :, half],
        weight.at[own],
        weight.at[other],
        sems,
    )


def start_all(copies):
    for copy in copies:
        copy.start()


def wait_all(copies):
    for copy in copies:
        copy.wait()


def squares_in_lanes(current):
    squares = jnp.sum(current * current, axis=1, keepdims=True)
    high = squares.astype(BF16).astype(F32)
    lane = lax.broadcasted_iota(jnp.int32, (current.shape[0], LANES), 1)
    return jnp.where(lane == 0, high, jnp.where(lane == 1, squares - high, 0.0))


def store_blocks(packed, product):
    requests, width = product.shape
    blocks = width // LANES
    for k in range(blocks):
        packed[pl.ds(k, requests, stride=blocks), :] = product[:, k * LANES : (k + 1) * LANES]
    return packed[...]


def spread(packed, values, stride):
    for k in range(stride):
        packed[pl.ds(k, values.shape[0], stride=stride), :] = values
    return packed[...]


def rows_of(packed, requests, blocks):
    return jnp.concatenate(
        [packed[pl.ds(k, requests, stride=blocks), :] for k in range(blocks)], axis=1
    )


def repeat_into(out_ref, values):
    rows = values.shape[0]
    for i in range(out_ref.shape[0] // rows):
        out_ref[i * rows : (i + 1) * rows, :] = values


def pair_sum(current, parts):
    a, b, c, d = [part[...].astype(F32) for part in parts]
    return (current[...].astype(F32) + ((a + b) + (c + d))).astype(BF16)


def slot_table(homes, chosen, counts, pool_dev, requests):
    n_blocks = homes.shape[1]
    shape = (n_blocks, n_blocks)
    row = lax.broadcasted_iota(jnp.int32, shape, 0)
    col = lax.broadcasted_iota(jnp.int32, shape, 1)
    places = jnp.broadcast_to(homes, shape)
    here = lax.div(places, pool_dev) == row

    def across(column):
        return jnp.sum(jnp.where(row == col, column, 0.0), axis=0, keepdims=True)

    slots = jnp.sum(jnp.where(here, lax.rem(places, pool_dev), 0).astype(F32), axis=1, keepdims=True)
    found = [jnp.zeros((1, n_blocks), F32), across(slots)]
    for layer_no in range(LAYERS):
        listed = chosen[layer_no]
        entry = lax.broadcasted_iota(jnp.int32, (n_blocks, listed.shape[1]), 1)
        block = lax.broadcasted_iota(jnp.int32, (n_blocks, listed.shape[1]), 0)
        hit = (listed == block) & (entry < counts[layer_no])
        taken = across(jnp.max(jnp.where(hit, 1.0, 0.0), axis=1, keepdims=True))
        found.append(across(jnp.max(jnp.where(here, taken, 0.0), axis=1, keepdims=True)))
    line = jnp.concatenate(found, axis=1)
    mine = lax.broadcasted_iota(jnp.int32, (requests, LANES), 0) == lax.axis_index("req")
    return jnp.where(mine, line, 0.0)


def first_query_kernel(
    pool_dev,
    x_hbm,
    gain_hbm,
    weight_hbm,
    homes_hbm,
    chosen_hbm,
    count_hbm,
    keep_ref,
    send_ref,
    x,
    gain,
    weight,
    homes,
    chosen,
    counts,
    packed,
    sems,
):
    copies = [
        pltpu.make_async_copy(source, target, sems.at[i])
        for i, (source, target) in enumerate(
            [
                (homes_hbm, homes),
                (chosen_hbm, chosen),
                (count_hbm, counts),
                (x_hbm, x),
                (gain_hbm, gain),
                (weight_hbm.at[0], weight),
            ]
        )
    ]
    start_all(copies)
    wait_all(copies[:3])
    lists = [chosen[i : i + 1, :] for i in range(LAYERS)]
    limits = [counts[i : i + 1, :] for i in range(LAYERS)]
    table = slot_table(homes[...], lists, limits, pool_dev, x.shape[0])
    wait_all(copies[3:])
    current = x[...].astype(F32)
    scaled = (current * gain[0:1, :].astype(F32)).astype(BF16)
    product = jnp.dot(scaled, weight[...], preferred_element_type=F32)
    middle = product.shape[1] // 2
    first = core_side() == 0
    rows = packed.shape[0]
    keep_ref[:rows, :] = store_blocks(packed, jnp.where(first, product[:, :middle], product[:, middle:]))
    send = store_blocks(packed, jnp.where(first, product[:, middle:], product[:, :middle]))
    send_ref[:rows, :] = send.astype(BF16)
    extra = squares_in_lanes(current) + table
    keep_ref[rows:, :] = extra
    send_ref[rows:, :] = extra.astype(BF16)


def pair_total_kernel(keep_ref, received_ref, out_ref):
    repeat_into(out_ref, (keep_ref[...] + received_ref[...].astype(F32)).astype(BF16))


def pair_state_kernel(x, x_other, gain, gain_other, ffn, ffn_other, x_out, gain_out, ffn_out):
    for own, other, out in ((x, x_other, x_out), (gain, gain_other, gain_out), (ffn, ffn_other, ffn_out)):
        out[...] = joined(own[...].astype(F32), other[...].astype(F32), 1).astype(BF16)


def query_kernel(
    layer_no, x_ref, a, b, c, d, gain_ref, own_hbm, other_hbm, out_ref, payload_ref, weight, packed, sems
):
    copies = row_copies(layer_no, own_hbm, other_hbm, weight, sems)
    start_all(copies)
    out_ref[...] = pair_sum(x_ref, (a, b, c, d))
    current = out_ref[...].astype(F32)
    scaled = (current * gain_ref[layer_no : layer_no + 1, :].astype(F32)).astype(BF16)
    extra = squares_in_lanes(current)
    wait_all(copies)
    product = jnp.dot(scaled, weight[...], preferred_element_type=F32)
    rows = jnp.concatenate([store_blocks(packed, product), extra], axis=0)
    repeat_into(payload_ref, rows.astype(BF16))


def in_parts(values, count):
    parts = []
    for _ in range(count):
        part = values.astype(BF16).astype(F32)
        parts.append(part)
        values = values - part
    return parts


def stats_in_lanes(block_max, block_sum):
    shape = (block_max.shape[0], LANES)
    lane = lax.broadcasted_iota(jnp.int32, shape, 1)
    stats = jnp.zeros(shape, F32)
    for place, part in enumerate(in_parts(block_max, 3) + in_parts(block_sum, 2)):
        stats = jnp.where(lane == place, part, stats)
    return stats


def block_kernel(
    layer_no, sources, received_ref, table_ref, tables_ref, own_hbm, other_hbm, out_ref, table_out, blocks, packed, sems
):
    copies = pair_copies(
        own_hbm.at[layer_no, :, 0], other_hbm.at[layer_no, :, 0], blocks.at[0], blocks.at[1], sems
    )
    start_all(copies)
    rows = packed.shape[0]
    n_slots = blocks.shape[1]
    totals = jnp.sum(received_ref[...].astype(F32).reshape(sources, -1, LANES), axis=0)
    extra = totals[rows:]
    requests = extra.shape[0]
    heads = rows // requests
    inv = lax.rsqrt((extra[:, 0:1] + extra[:, 1:2]) / D + EPSILON)
    queries = totals[:rows] * spread(packed, jnp.broadcast_to(inv, extra.shape), heads)
    queries = queries * tables_ref[0:1, :] + pltpu.roll(queries, LANES // 2, 1) * tables_ref[1:2, :]
    queries = queries.astype(BF16)

    table = extra if table_ref is None else table_ref[...]
    if table_out is not None:
        table_out[...] = extra
    me = lax.axis_index("req")
    lane = lax.broadcasted_iota(jnp.int32, table.shape, 1)
    request = lax.broadcasted_iota(jnp.int32, (requests, rows), 0)
    column = lax.broadcasted_iota(jnp.int32, (requests, rows), 1)
    row = lax.broadcasted_iota(jnp.int32, (2 * n_slots * heads, rows), 0)
    head = lax.rem(column, heads).astype(F32)
    places, used = [], []
    for b in range(2):
        store = me if b == 0 else me + 1 - 2 * core_side()
        slots = jnp.sum(jnp.where(lane == n_slots + store, table, 0.0), axis=1, keepdims=True)
        taken = jnp.where(lane == (2 + layer_no) * n_slots + store, table, 0.0)
        taken = jnp.broadcast_to(jnp.sum(taken, axis=1, keepdims=True), table.shape)
        used.append(spread(packed, taken, heads))
        target = jnp.where(
            lax.div(column, heads) == request, slots * (2 * heads) + (head + b * heads), 0.0
        )
        target = jnp.sum(target, axis=0, keepdims=True).astype(jnp.int32)
        places.append(jnp.where(row == target, 1.0, 0.0))
    by_slot = jnp.concatenate(places, axis=1)
    queries = jnp.dot(
        by_slot.astype(BF16), jnp.concatenate([queries, queries], axis=0), preferred_element_type=F32
    )
    group = 2 * heads
    mine = lax.broadcasted_iota(jnp.int32, (group, LANES), 0) < heads
    wait_all(copies)

    def of_slot(left, p, part, contract):
        left = left[p * group : (p + 1) * group].astype(BF16)
        sides = [
            lax.dot_general(
                left, blocks[b, p, part], (((1,), (contract,)), ((), ())), preferred_element_type=F32
            )
            for b in range(2)
        ]
        return jnp.where(mine, sides[0], sides[1])

    scores = jnp.concatenate([of_slot(queries, p, 0, 1) for p in range(n_slots)], axis=0)
    block_max = jnp.max(scores, axis=1, keepdims=True)
    terms = jnp.exp(scores - block_max)
    block_sum = jnp.sum(terms, axis=1, keepdims=True)
    acc = jnp.concatenate([of_slot(terms, p, 1, 0) for p in range(n_slots)], axis=0)
    both = jnp.concatenate([acc, stats_in_lanes(block_max, block_sum)], axis=1).astype(BF16)
    both = jnp.dot(by_slot.T.astype(BF16), both, preferred_element_type=F32)
    sides = []
    for b in range(2):
        side = both[b * rows : (b + 1) * rows]
        stats = side[:, LANES:]
        block_max = stats[:, 0:1] + stats[:, 1:2] + stats[:, 2:3]
        block_max = jnp.where(used[b][:, 0:1] > 0.0, block_max, MASK_FILL)
        sides.append((block_max, stats[:, 3:4] + stats[:, 4:5], side[:, :LANES]))
    top = jnp.maximum(sides[0][0], sides[1][0])
    rescale = [jnp.exp(side[0] - top) for side in sides]
    total = rescale[0] * sides[0][1] + rescale[1] * sides[1][1]
    acc = rescale[0] * sides[0][2] + rescale[1] * sides[1][2]
    stats = stats_in_lanes(top, total).T
    extra = out_ref.shape[0] // sources - rows
    repeat_into(out_ref, jnp.concatenate([acc, stats[:extra]], axis=0).astype(BF16))


def first_block_kernel(sources, received_ref, tables_ref, own_hbm, other_hbm, out_ref, table_out, *scratch):
    block_kernel(
        0, sources, received_ref, None, tables_ref, own_hbm, other_hbm, out_ref, table_out, *scratch
    )


def later_block_kernel(
    layer_no, sources, received_ref, table_ref, tables_ref, own_hbm, other_hbm, out_ref, *scratch
):
    block_kernel(
        layer_no, sources, received_ref, table_ref, tables_ref, own_hbm, other_hbm, out_ref, None, *scratch
    )


def combine_kernel(sources, received_ref, out_ref):
    rows = out_ref.shape[0]
    both = received_ref[...].astype(F32).reshape(sources, -1, LANES)
    stats = [both[s, rows : rows + 8, :] for s in range(sources)]
    block_max = jnp.concatenate([x[0:1] + x[1:2] + x[2:3] for x in stats], axis=0)
    block_sum = jnp.concatenate([x[3:4] + x[4:5] for x in stats], axis=0)
    rescale = jnp.exp(block_max - jnp.max(block_max, axis=0, keepdims=True))
    factors = rescale / jnp.sum(rescale * block_sum, axis=0, keepdims=True)
    factors = jnp.concatenate([factors, jnp.zeros((LANES - sources, LANES), F32)], axis=0).T
    context = jnp.zeros((rows, LANES), F32)
    for s in range(sources):
        context += both[s, :rows, :] * factors[:, s : s + 1]
    out_ref[...] = context.astype(BF16)


def context_kernel(
    layer_no, requests, own_ref, other_ref, own_hbm, other_hbm, out_ref, weight, packed, sems
):
    copies = column_copies(layer_no, own_hbm, other_hbm, weight, sems)
    start_all(copies)
    sides = []
    for ref in (own_ref, other_ref):
        packed[...] = ref[...].astype(F32)
        sides.append(rows_of(packed, requests, packed.shape[0] // requests))
    rows = joined(sides[0], sides[1], 1).astype(BF16)
    wait_all(copies)
    out_ref[...] = jnp.dot(rows, weight[...], preferred_element_type=F32).astype(BF16)


def gate_up_kernel(
    layer_no,
    chunk,
    x_ref,
    a,
    b,
    c,
    d,
    gain_ref,
    gate_hbm,
    gate_other,
    up_hbm,
    up_other,
    out_ref,
    payload_ref,
    gate,
    up,
    packed,
    sems,
):
    gate_copies = row_copies(layer_no, gate_hbm, gate_other, gate, sems.at[0])
    up_copies = row_copies(layer_no, up_hbm, up_other, up, sems.at[1])
    start_all(gate_copies)
    start_all(up_copies)
    requests = x_ref.shape[0]
    per_chunk = chunk // (packed.shape[0] // requests)
    stride = packed.shape[0] // requests
    count = requests // per_chunk
    blocks = gate.shape[1] // LANES
    half = stride // 2

    def store(row, values):
        for q in range(per_chunk):
            packed[pl.ds(q * stride + row, count, stride=chunk), :] = values[q * count : (q + 1) * count]

    out_ref[...] = pair_sum(x_ref, (a, b, c, d))
    current = out_ref[...].astype(F32)
    scaled = (current * gain_ref[layer_no : layer_no + 1, :].astype(F32)).astype(BF16)
    zeros = jnp.zeros((requests, LANES), F32)
    store(blocks, squares_in_lanes(current))
    for row in [*range(blocks + 1, half), *range(half + blocks, stride)]:
        store(row, zeros)
    for first, copies, weight in ((0, gate_copies, gate), (half, up_copies, up)):
        wait_all(copies)
        product = jnp.dot(scaled, weight[...], preferred_element_type=F32)
        for k in range(blocks):
            store(first + k, product[:, k * LANES : (k + 1) * LANES])
    payload_ref[...] = packed[...].astype(BF16)


def activation_kernel(blocks, sources, half, received_ref, out_ref):
    totals = jnp.sum(received_ref[...].astype(F32).reshape(sources, -1, LANES), axis=0)
    acts = []
    for at in range(0, totals.shape[0], 2 * half):
        squares = totals[at + blocks : at + blocks + 1, 0:1] + totals[at + blocks : at + blocks + 1, 1:2]
        inv = lax.rsqrt(squares / D + EPSILON)
        gate = totals[at : at + half] * inv
        acts.append(gate / (1.0 + jnp.exp(-gate)) * (totals[at + half : at + 2 * half] * inv))
    repeat_into(out_ref, jnp.concatenate(acts, axis=0).astype(BF16))


def down_kernel(
    layer_no, half, chunk, received_ref, own_hbm, other_hbm, out_ref, weight, packed, sems
):
    copies = column_copies(layer_no, own_hbm, other_hbm, weight, sems)
    start_all(copies)
    packed[...] = received_ref[...].astype(F32)
    blocks = weight.shape[0] // LANES // 2
    per_chunk = chunk // half
    count = out_ref.shape[0] // per_chunk
    columns = []
    for side in range(2):
        for k in range(blocks):
            columns.append(
                jnp.concatenate(
                    [
                        packed[pl.ds(side * chunk + q * half + k, count, stride=2 * chunk), :]
                        for q in range(per_chunk)
                    ],
                    axis=0,
                ).astype(BF16)
            )
    rows = jnp.concatenate(columns, axis=1)
    wait_all(copies)
    out_ref[...] = jnp.dot(rows, weight[...], preferred_element_type=F32).astype(BF16)


def last_kernel(x_ref, a, b, c, d, out_ref):
    total = pair_sum(x_ref, (a, b, c, d)).astype(F32)
    width = out_ref.shape[1]
    out_ref[...] = jnp.where(core_side() == 0, total[:, :width], total[:, width:]).astype(BF16)


def exchange(array, n_req):
    shape = array.shape
    sides = [list(range(core, n_req, 2)) for core in range(2)]
    count = n_req // 2
    blocks = array.reshape((count, shape[0] // count) + shape[1:])
    return lax.all_to_all(
        blocks, "req", split_axis=0, concat_axis=0, tiled=True, axis_index_groups=sides
    ).reshape(shape)


def exchange_all(array, n_req):
    shape = array.shape
    blocks = array.reshape((n_req, shape[0] // n_req) + shape[1:])
    return lax.all_to_all(blocks, "req", split_axis=0, concat_axis=0, tiled=True).reshape(shape)


def from_pair(array, n_req):
    return lax.ppermute(array, "req", [(i, i ^ 1) for i in range(n_req)])


def tp_parts(partial_sum):
    n_tp = lax.axis_size("tp")
    one, three, two = [
        lax.ppermute(partial_sum, "tp", [(i, (i + shift) % n_tp) for i in range(n_tp)])
        for shift in (1, 3, 2)
    ]
    return [partial_sum, two, one, three]


def shards(
    hidden,
    attn_gain,
    q_weight,
    o_weight,
    ffn_gain,
    gate_weight,
    up_weight,
    down_weight,
    kv_pool,
    block_home,
    chosen,
    chosen_count,
):
    n_req = lax.axis_size("req")
    requests, width = hidden.shape
    pool_dev = kv_pool.shape[1]
    block_tokens, head_size = kv_pool.shape[4:]
    heads = q_weight.shape[2] // head_size // 2
    side = n_req // 2
    q_rows = requests * heads
    sent_rows = q_rows + requests
    stat_rows = q_rows + 16
    f_rows = 16
    hidden_half = gate_weight.shape[2] // 2
    blocks = hidden_half // LANES
    tables = rotary_tables(float(block_home.shape[1] * block_tokens - 1), head_size)
    dma = pltpu.SemaphoreType.DMA

    def rows_type(rows, kind=BF16):
        return jax.ShapeDtypeStruct((rows, LANES), kind)

    def rows_scratch(rows):
        return pltpu.VMEM((rows, LANES), F32)

    def pair_type(rows):
        return jax.ShapeDtypeStruct((rows, 2 * width), BF16)

    keep, send = call(
        functools.partial(first_query_kernel, pool_dev),
        [rows_type(sent_rows, F32), rows_type(sent_rows)],
        [HBM] * 6,
        [
            pltpu.VMEM(hidden.shape, BF16),
            pltpu.VMEM(attn_gain.shape, BF16),
            pltpu.VMEM(q_weight.shape[1:], BF16),
            pltpu.VMEM(block_home.shape, jnp.int32),
            pltpu.VMEM((LAYERS, chosen.shape[3]), jnp.int32),
            pltpu.VMEM((LAYERS, 1), jnp.int32),
            rows_scratch(q_rows),
            dma((6,)),
        ],
        limit=62,
    )(
        hidden,
        attn_gain,
        q_weight,
        block_home,
        chosen.reshape(LAYERS, -1),
        chosen_count.reshape(LAYERS, 1),
    )
    payload = call(pair_total_kernel, rows_type(side * sent_rows), [VMEM] * 2)(
        keep, from_pair(send, n_req)
    )
    pool_other = from_pair(kv_pool, n_req)
    o_other = from_pair(o_weight, n_req)
    gate_other = from_pair(gate_weight, n_req)
    up_other = from_pair(up_weight, n_req)
    down_other = from_pair(down_weight, n_req)
    q_other = from_pair(q_weight, n_req)
    current, attn_gain, ffn_gain = call(
        pair_state_kernel,
        [pair_type(requests), pair_type(LAYERS), pair_type(LAYERS)],
        [VMEM] * 6,
    )(
        hidden,
        from_pair(hidden, n_req),
        attn_gain,
        from_pair(attn_gain, n_req),
        ffn_gain,
        from_pair(ffn_gain, n_req),
    )

    parts = None
    table = None
    for layer_no in range(LAYERS):
        if parts is not None:
            current, payload = call(
                functools.partial(query_kernel, layer_no),
                [pair_type(requests), rows_type(side * sent_rows)],
                [VMEM] * 6 + [HBM] * 2,
                [
                    pltpu.VMEM((2 * width, heads * head_size), BF16),
                    rows_scratch(q_rows),
                    dma((2,)),
                ],
            )(current, *parts, attn_gain, q_weight, q_other)
        received = exchange(payload, n_req)
        scratch = [
            pltpu.VMEM((2, pool_dev, 2, block_tokens, head_size), BF16),
            rows_scratch(q_rows),
            dma((2,)),
        ]
        if table is None:
            payload, table = call(
                functools.partial(first_block_kernel, side),
                [rows_type(side * stat_rows), rows_type(requests, F32)],
                [VMEM] * 2 + [HBM] * 2,
                scratch,
            )(received, tables, kv_pool, pool_other)
        else:
            payload = call(
                functools.partial(later_block_kernel, layer_no, side),
                rows_type(side * stat_rows),
                [VMEM] * 3 + [HBM] * 2,
                scratch,
            )(received, table, tables, kv_pool, pool_other)
        context = call(functools.partial(combine_kernel, side), rows_type(q_rows), [VMEM])(
            exchange(payload, n_req)
        )
        own = call(
            functools.partial(context_kernel, layer_no, requests),
            pair_type(requests),
            [VMEM] * 2 + [HBM] * 2,
            [pltpu.VMEM((o_weight.shape[1], 2 * width), BF16), rows_scratch(q_rows), dma((2,))],
        )(context, from_pair(context, n_req), o_weight, o_other)
        chunk = requests // side * 2 * f_rows
        current, payload = call(
            functools.partial(gate_up_kernel, layer_no, chunk),
            [pair_type(requests), rows_type(requests * 2 * f_rows)],
            [VMEM] * 6 + [HBM] * 4,
            [
                pltpu.VMEM((2 * width, hidden_half), BF16),
                pltpu.VMEM((2 * width, hidden_half), BF16),
                rows_scratch(requests * 2 * f_rows),
                dma((2, 2)),
            ],
        )(current, *tp_parts(own), ffn_gain, gate_weight, gate_other, up_weight, up_other)
        chunk = requests // side * f_rows
        act = call(
            functools.partial(activation_kernel, blocks, side, f_rows),
            rows_type(n_req * chunk),
            [VMEM],
        )(exchange(payload, n_req))
        own = call(
            functools.partial(down_kernel, layer_no, f_rows, chunk),
            pair_type(requests),
            [VMEM] + [HBM] * 2,
            [
                pltpu.VMEM((down_weight.shape[1], 2 * width), BF16),
                rows_scratch(n_req * chunk),
                dma((2,)),
            ],
        )(exchange_all(act, n_req), down_weight, down_other)
        parts = tp_parts(own)
    return call(last_kernel, jax.ShapeDtypeStruct(hidden.shape, BF16), [VMEM] * 5)(current, *parts)


def solution(mesh):
    return jax.shard_map(
        shards,
        mesh=mesh,
        in_specs=(
            P(None, "req"),
            P(None, "req"),
            P(None, "req", "tp"),
            P(None, "tp", "req"),
            P(None, "req"),
            P(None, "req", "tp"),
            P(None, "req", "tp"),
            P(None, "tp", "req"),
            P(None, "req", "tp", None, None, None),
            P("req", None),
            P(None, "req", "tp", None),
            P(None, "req", "tp"),
        ),
        out_specs=P(None, "req"),
        check_vma=False,
    )
```

```python
import functools
import math

import jax
import jax.numpy as jnp
import numpy as np
from jax import lax
from jax.experimental import pallas as pl
from jax.experimental.pallas import tpu as pltpu
from jax.sharding import PartitionSpec as P

D = 8192
LAYERS = 2
LANES = 128

MASK_FILL = -1e30
EPSILON = 1e-05

VMEM = pl.BlockSpec(memory_space=pltpu.VMEM)
SMEM = pl.BlockSpec(memory_space=pltpu.SMEM)
HBM = pl.BlockSpec(memory_space=pltpu.HBM)
F32 = jnp.float32
BF16 = jnp.bfloat16


def rotary_tables(position, head_size):
    freq_idx = np.arange(head_size // 2)
    angles = position * np.exp(freq_idx * (-2.0 * math.log(500000.0) / head_size))
    cosine, sine_part = np.cos(angles), np.sin(angles)
    scale = head_size**-0.5
    tables = np.stack([np.concatenate([cosine, cosine]), np.concatenate([-sine_part, sine_part])])
    return jnp.asarray(tables * scale, F32)


def call(kernel, out_shape, in_specs, scratch=(), limit=16, out_specs=None, flops=10000000000, nbytes=0):
    return pl.pallas_call(
        kernel,
        out_shape=out_shape,
        in_specs=in_specs,
        out_specs=out_specs if out_specs is not None else jax.tree.map(lambda _: VMEM, out_shape),
        scratch_shapes=list(scratch),
        compiler_params=pltpu.CompilerParams(vmem_limit_bytes=limit * 1024 * 1024),
        cost_estimate=pl.CostEstimate(flops=flops, bytes_accessed=nbytes, transcendentals=0),
    )


def core_side():
    return lax.rem(lax.axis_index("req"), 2)


def joined(own, other, axis):
    first = core_side() == 0
    return jnp.concatenate([jnp.where(first, own, other), jnp.where(first, other, own)], axis=axis)


def pair_copies(own_hbm, other_hbm, own_target, other_target, sems):
    return [
        pltpu.make_async_copy(own_hbm, own_target, sems.at[0]),
        pltpu.make_async_copy(other_hbm, other_target, sems.at[1]),
    ]


def side_slices(size):
    side = core_side()
    return (
        pl.ds(pl.multiple_of(side * size, LANES), size),
        pl.ds(pl.multiple_of((1 - side) * size, LANES), size),
    )


def column_copies(layer_no, own_hbm, other_hbm, weight, sems):
    own, other = side_slices(own_hbm.shape[2])
    return pair_copies(
        own_hbm.at[layer_no], other_hbm.at[layer_no], weight.at[:, own], weight.at[:, other], sems
    )


def row_copies(layer_no, own_hbm, other_hbm, weight, sems):
    half, _ = side_slices(weight.shape[1])
    own, other = side_slices(own_hbm.shape[1])
    return pair_copies(
        own_hbm.at[layer_no, :, half],
        other_hbm.at[layer_no, :, half],
        weight.at[own],
        weight.at[other],
        sems,
    )


def start_all(copies):
    for copy in copies:
        copy.start()


def wait_all(copies):
    for copy in copies:
        copy.wait()


def squares_in_lanes(current):
    squares = jnp.sum(current * current, axis=1, keepdims=True)
    high = squares.astype(BF16).astype(F32)
    lane = lax.broadcasted_iota(jnp.int32, (current.shape[0], LANES), 1)
    return jnp.where(lane == 0, high, jnp.where(lane == 1, squares - high, 0.0))


def store_blocks(packed, product):
    requests, width = product.shape
    blocks = width // LANES
    for k in range(blocks):
        packed[pl.ds(k, requests, stride=blocks), :] = product[:, k * LANES : (k + 1) * LANES]
    return packed[...]


def spread(packed, values, stride):
    for k in range(stride):
        packed[pl.ds(k, values.shape[0], stride=stride), :] = values
    return packed[...]


def rows_of(packed, requests, blocks):
    return jnp.concatenate(
        [packed[pl.ds(k, requests, stride=blocks), :] for k in range(blocks)], axis=1
    )


def repeat_into(out_ref, values):
    rows = values.shape[0]
    for i in range(out_ref.shape[0] // rows):
        out_ref[i * rows : (i + 1) * rows, :] = values


def pair_sum(current, parts):
    a, b, c, d = [part[...].astype(F32) for part in parts]
    return (current[...].astype(F32) + ((a + b) + (c + d))).astype(BF16)


def slot_table(homes, chosen, counts, pool_dev, requests):
    n_blocks = homes.shape[1]
    shape = (n_blocks, n_blocks)
    row = lax.broadcasted_iota(jnp.int32, shape, 0)
    col = lax.broadcasted_iota(jnp.int32, shape, 1)
    places = jnp.broadcast_to(homes, shape)
    here = lax.div(places, pool_dev) == row

    def across(column):
        return jnp.sum(jnp.where(row == col, column, 0.0), axis=0, keepdims=True)

    slots = jnp.sum(jnp.where(here, lax.rem(places, pool_dev), 0).astype(F32), axis=1, keepdims=True)
    found = [jnp.zeros((1, n_blocks), F32), across(slots)]
    for layer_no in range(LAYERS):
        listed = chosen[layer_no]
        entry = lax.broadcasted_iota(jnp.int32, (n_blocks, listed.shape[1]), 1)
        block = lax.broadcasted_iota(jnp.int32, (n_blocks, listed.shape[1]), 0)
        hit = (listed == block) & (entry < counts[layer_no])
        taken = across(jnp.max(jnp.where(hit, 1.0, 0.0), axis=1, keepdims=True))
        found.append(across(jnp.max(jnp.where(here, taken, 0.0), axis=1, keepdims=True)))
    line = jnp.concatenate(found, axis=1)
    mine = lax.broadcasted_iota(jnp.int32, (requests, LANES), 0) == lax.axis_index("req")
    return jnp.where(mine, line, 0.0)


def first_query_kernel(
    pool_dev,
    x_hbm,
    gain_hbm,
    weight_hbm,
    homes_hbm,
    chosen_hbm,
    count_hbm,
    keep_ref,
    send_ref,
    x,
    gain,
    weight,
    homes,
    chosen,
    counts,
    packed,
    sems,
):
    copies = [
        pltpu.make_async_copy(source, target, sems.at[i])
        for i, (source, target) in enumerate(
            [
                (homes_hbm, homes),
                (chosen_hbm, chosen),
                (count_hbm, counts),
                (x_hbm, x),
                (gain_hbm, gain),
                (weight_hbm.at[0], weight),
            ]
        )
    ]
    start_all(copies)
    wait_all(copies[:3])
    lists = [chosen[i, 0] for i in range(LAYERS)]
    limits = [counts[:, i : i + 1] for i in range(LAYERS)]
    table = slot_table(homes[...], lists, limits, pool_dev, x.shape[0])
    wait_all(copies[3:])
    current = x[...].astype(F32)
    scaled = (current * gain[0:1, :].astype(F32)).astype(BF16)
    product = jnp.dot(scaled, weight[...], preferred_element_type=F32)
    middle = product.shape[1] // 2
    first = core_side() == 0
    rows = packed.shape[0]
    keep_ref[:rows, :] = store_blocks(packed, jnp.where(first, product[:, :middle], product[:, middle:]))
    send = store_blocks(packed, jnp.where(first, product[:, middle:], product[:, :middle]))
    send_ref[:rows, :] = send.astype(BF16)
    extra = squares_in_lanes(current) + table
    keep_ref[rows:, :] = extra
    send_ref[rows:, :] = extra.astype(BF16)


def pair_total_kernel(keep_ref, received_ref, out_ref):
    repeat_into(out_ref, (keep_ref[...] + received_ref[...].astype(F32)).astype(BF16))


def pair_state_kernel(x, x_other, gain, gain_other, ffn, ffn_other, x_out, gain_out, ffn_out):
    for own, other, out in ((x, x_other, x_out), (gain, gain_other, gain_out), (ffn, ffn_other, ffn_out)):
        out[...] = joined(own[...].astype(F32), other[...].astype(F32), 1).astype(BF16)


def query_kernel(
    layer_no, x_ref, a, b, c, d, gain_ref, own_hbm, other_hbm, out_ref, payload_ref, weight, packed, sems
):
    copies = row_copies(layer_no, own_hbm, other_hbm, weight, sems)
    start_all(copies)
    out_ref[...] = pair_sum(x_ref, (a, b, c, d))
    current = out_ref[...].astype(F32)
    scaled = (current * gain_ref[layer_no : layer_no + 1, :].astype(F32)).astype(BF16)
    extra = squares_in_lanes(current)
    wait_all(copies)
    product = jnp.dot(scaled, weight[...], preferred_element_type=F32)
    rows = jnp.concatenate([store_blocks(packed, product), extra], axis=0)
    repeat_into(payload_ref, rows.astype(BF16))


def in_parts(values, count):
    parts = []
    for _ in range(count):
        part = values.astype(BF16).astype(F32)
        parts.append(part)
        values = values - part
    return parts


def stats_in_lanes(block_max, block_sum):
    shape = (block_max.shape[0], LANES)
    lane = lax.broadcasted_iota(jnp.int32, shape, 1)
    stats = jnp.zeros(shape, F32)
    for place, part in enumerate(in_parts(block_max, 3) + in_parts(block_sum, 2)):
        stats = jnp.where(lane == place, part, stats)
    return stats


def block_kernel(
    layer_no, sources, received_ref, table_ref, tables_ref, own_hbm, other_hbm, out_ref, table_out, blocks, packed, sems
):
    n_slots = blocks.shape[1]
    piece = n_slots // 2
    copies = [
        [
            pltpu.make_async_copy(
                pool.at[layer_no, pl.ds(at, piece), 0, part],
                blocks.at[b, pl.ds(at, piece), part],
                sems.at[part * 2 + at // piece, b],
            )
            for b, pool in enumerate((own_hbm, other_hbm))
        ]
        for part in range(2)
        for at in (0, piece)
    ]
    for pair in copies:
        start_all(pair)
    rows = packed.shape[0]
    totals = jnp.sum(received_ref[...].astype(F32).reshape(sources, -1, LANES), axis=0)
    extra = totals[rows:]
    requests = extra.shape[0]
    heads = rows // requests
    inv = lax.rsqrt((extra[:, 0:1] + extra[:, 1:2]) / D + EPSILON)
    queries = totals[:rows] * spread(packed, jnp.broadcast_to(inv, extra.shape), heads)
    queries = queries * tables_ref[0:1, :] + pltpu.roll(queries, LANES // 2, 1) * tables_ref[1:2, :]
    queries = queries.astype(BF16)

    table = extra if table_ref is None else table_ref[...]
    if table_out is not None:
        table_out[...] = extra
    me = lax.axis_index("req")
    lane = lax.broadcasted_iota(jnp.int32, table.shape, 1)
    request = lax.broadcasted_iota(jnp.int32, (requests, rows), 0)
    column = lax.broadcasted_iota(jnp.int32, (requests, rows), 1)
    row = lax.broadcasted_iota(jnp.int32, (2 * n_slots * heads, rows), 0)
    head = lax.rem(column, heads).astype(F32)
    places, used = [], []
    for b in range(2):
        store = me if b == 0 else me + 1 - 2 * core_side()
        slots = jnp.sum(jnp.where(lane == n_slots + store, table, 0.0), axis=1, keepdims=True)
        taken = jnp.where(lane == (2 + layer_no) * n_slots + store, table, 0.0)
        taken = jnp.broadcast_to(jnp.sum(taken, axis=1, keepdims=True), table.shape)
        used.append(spread(packed, taken, heads))
        target = jnp.where(
            lax.div(column, heads) == request, slots * (2 * heads) + (head + b * heads), 0.0
        )
        target = jnp.sum(target, axis=0, keepdims=True).astype(jnp.int32)
        places.append(jnp.where(row == target, 1.0, 0.0))
    by_slot = jnp.concatenate(places, axis=1)
    queries = jnp.dot(
        by_slot.astype(BF16), jnp.concatenate([queries, queries], axis=0), preferred_element_type=F32
    )
    group = 2 * heads
    mine = lax.broadcasted_iota(jnp.int32, (group, LANES), 0) < heads

    def of_slot(left, p, part, contract):
        if p % piece == 0:
            wait_all(copies[part * 2 + p // piece])
        left = left[p * group : (p + 1) * group]
        left = jnp.concatenate([jnp.where(mine, left, 0.0), jnp.where(mine, 0.0, left)], axis=1)
        right = jnp.concatenate([blocks[0, p, part], blocks[1, p, part]], axis=contract)
        return lax.dot_general(
            left.astype(BF16), right, (((1,), (contract,)), ((), ())), preferred_element_type=F32
        )

    scores = jnp.concatenate([of_slot(queries, p, 0, 1) for p in range(n_slots)], axis=0)
    block_max = jnp.max(scores, axis=1, keepdims=True)
    terms = jnp.exp(scores - block_max)
    block_sum = jnp.sum(terms, axis=1, keepdims=True)
    acc = jnp.concatenate([of_slot(terms, p, 1, 0) for p in range(n_slots)], axis=0)
    both = jnp.concatenate([acc, stats_in_lanes(block_max, block_sum)], axis=1).astype(BF16)
    both = jnp.dot(by_slot.T.astype(BF16), both, preferred_element_type=F32)
    sides = []
    for b in range(2):
        side = both[b * rows : (b + 1) * rows]
        stats = side[:, LANES:]
        block_max = stats[:, 0:1] + stats[:, 1:2] + stats[:, 2:3]
        block_max = jnp.where(used[b][:, 0:1] > 0.0, block_max, MASK_FILL)
        sides.append((block_max, stats[:, 3:4] + stats[:, 4:5], side[:, :LANES]))
    top = jnp.maximum(sides[0][0], sides[1][0])
    rescale = [jnp.exp(side[0] - top) for side in sides]
    total = rescale[0] * sides[0][1] + rescale[1] * sides[1][1]
    acc = rescale[0] * sides[0][2] + rescale[1] * sides[1][2]
    stats = stats_in_lanes(top, total).T
    extra = out_ref.shape[0] // sources - rows
    repeat_into(out_ref, jnp.concatenate([acc, stats[:extra]], axis=0).astype(BF16))


def first_block_kernel(sources, received_ref, tables_ref, own_hbm, other_hbm, out_ref, table_out, *scratch):
    block_kernel(
        0, sources, received_ref, None, tables_ref, own_hbm, other_hbm, out_ref, table_out, *scratch
    )


def later_block_kernel(
    layer_no, sources, received_ref, table_ref, tables_ref, own_hbm, other_hbm, out_ref, *scratch
):
    block_kernel(
        layer_no, sources, received_ref, table_ref, tables_ref, own_hbm, other_hbm, out_ref, None, *scratch
    )


def combine_kernel(sources, received_ref, out_ref):
    rows = out_ref.shape[0]
    both = received_ref[...].astype(F32).reshape(sources, -1, LANES)
    stats = [both[s, rows : rows + 8, :] for s in range(sources)]
    block_max = jnp.concatenate([x[0:1] + x[1:2] + x[2:3] for x in stats], axis=0)
    block_sum = jnp.concatenate([x[3:4] + x[4:5] for x in stats], axis=0)
    rescale = jnp.exp(block_max - jnp.max(block_max, axis=0, keepdims=True))
    factors = rescale / jnp.sum(rescale * block_sum, axis=0, keepdims=True)
    factors = jnp.concatenate([factors, jnp.zeros((LANES - sources, LANES), F32)], axis=0).T
    context = jnp.zeros((rows, LANES), F32)
    for s in range(sources):
        context += both[s, :rows, :] * factors[:, s : s + 1]
    out_ref[...] = context.astype(BF16)


def context_kernel(
    layer_no, requests, own_ref, other_ref, own_hbm, other_hbm, out_ref, weight, packed, sems
):
    copies = column_copies(layer_no, own_hbm, other_hbm, weight, sems)
    start_all(copies)
    sides = []
    for ref in (own_ref, other_ref):
        packed[...] = ref[...].astype(F32)
        sides.append(rows_of(packed, requests, packed.shape[0] // requests))
    rows = joined(sides[0], sides[1], 1).astype(BF16)
    wait_all(copies)
    out_ref[...] = jnp.dot(rows, weight[...], preferred_element_type=F32).astype(BF16)


def gate_up_kernel(
    layer_no,
    chunk,
    x_ref,
    a,
    b,
    c,
    d,
    gain_ref,
    gate_hbm,
    gate_other,
    up_hbm,
    up_other,
    out_ref,
    payload_ref,
    gate,
    up,
    packed,
    sems,
):
    width = gate.shape[1]
    piece = width // 2
    own_rows, other_rows = side_slices(gate_hbm.shape[1])
    steps = []
    for i, (own, other, weight) in enumerate(((gate_hbm, gate_other, gate), (up_hbm, up_other, up))):
        for j in range(2):
            columns = pl.ds(pl.multiple_of(core_side() * width + j * piece, LANES), piece)
            local = pl.ds(j * piece, piece)
            copies = pair_copies(
                own.at[layer_no, :, columns],
                other.at[layer_no, :, columns],
                weight.at[own_rows, local],
                weight.at[other_rows, local],
                sems.at[i * 2 + j],
            )
            start_all(copies)
            steps.append((i, j, copies, weight))
    requests = x_ref.shape[0]
    per_chunk = chunk // (packed.shape[0] // requests)
    stride = packed.shape[0] // requests
    count = requests // per_chunk
    blocks = gate.shape[1] // LANES
    half = stride // 2

    def store(row, values):
        for q in range(per_chunk):
            packed[pl.ds(q * stride + row, count, stride=chunk), :] = values[q * count : (q + 1) * count]

    out_ref[...] = pair_sum(x_ref, (a, b, c, d))
    current = out_ref[...].astype(F32)
    scaled = (current * gain_ref[layer_no : layer_no + 1, :].astype(F32)).astype(BF16)
    zeros = jnp.zeros((requests, LANES), F32)
    store(blocks, squares_in_lanes(current))
    for row in [*range(blocks + 1, half), *range(half + blocks, stride)]:
        store(row, zeros)
    for i, j, copies, weight in steps:
        wait_all(copies)
        product = jnp.dot(scaled, weight[:, j * piece : (j + 1) * piece], preferred_element_type=F32)
        for k in range(piece // LANES):
            store(i * half + j * (piece // LANES) + k, product[:, k * LANES : (k + 1) * LANES])
    payload_ref[...] = packed[...].astype(BF16)


def activation_kernel(blocks, sources, half, received_ref, out_ref):
    totals = jnp.sum(received_ref[...].astype(F32).reshape(sources, -1, LANES), axis=0)
    acts = []
    for at in range(0, totals.shape[0], 2 * half):
        squares = totals[at + blocks : at + blocks + 1, 0:1] + totals[at + blocks : at + blocks + 1, 1:2]
        inv = lax.rsqrt(squares / D + EPSILON)
        gate = totals[at : at + half] * inv
        acts.append(gate / (1.0 + jnp.exp(-gate)) * (totals[at + half : at + 2 * half] * inv))
    repeat_into(out_ref, jnp.concatenate(acts, axis=0).astype(BF16))


def down_kernel(
    layer_no, half, chunk, received_ref, own_hbm, other_hbm, out_ref, weight, packed, sems
):
    depth = weight.shape[0] // 2
    own_columns, other_columns = side_slices(own_hbm.shape[2])
    steps = []
    for side in range(2):
        rows = pl.ds(side * depth, depth)
        steps.append(
            pair_copies(
                own_hbm.at[layer_no, rows],
                other_hbm.at[layer_no, rows],
                weight.at[rows, own_columns],
                weight.at[rows, other_columns],
                sems.at[side],
            )
        )
        start_all(steps[side])
    packed[...] = received_ref[...].astype(F32)
    blocks = weight.shape[0] // LANES // 2
    per_chunk = chunk // half
    count = out_ref.shape[0] // per_chunk
    total = 0.0
    for side in range(2):
        columns = []
        for k in range(blocks):
            columns.append(
                jnp.concatenate(
                    [
                        packed[pl.ds(side * chunk + q * half + k, count, stride=2 * chunk), :]
                        for q in range(per_chunk)
                    ],
                    axis=0,
                ).astype(BF16)
            )
        rows = jnp.concatenate(columns, axis=1)
        wait_all(steps[side])
        total += jnp.dot(
            rows, weight[side * depth : (side + 1) * depth], preferred_element_type=F32
        )
    out_ref[...] = total.astype(BF16)


def last_kernel(x_ref, a, b, c, d, out_ref):
    total = pair_sum(x_ref, (a, b, c, d)).astype(F32)
    width = out_ref.shape[1]
    out_ref[...] = jnp.where(core_side() == 0, total[:, :width], total[:, width:]).astype(BF16)


def exchange(array, n_req):
    shape = array.shape
    sides = [list(range(core, n_req, 2)) for core in range(2)]
    count = n_req // 2
    blocks = array.reshape((count, shape[0] // count) + shape[1:])
    return lax.all_to_all(
        blocks, "req", split_axis=0, concat_axis=0, tiled=True, axis_index_groups=sides
    ).reshape(shape)


def exchange_all(array, n_req):
    shape = array.shape
    blocks = array.reshape((n_req, shape[0] // n_req) + shape[1:])
    return lax.all_to_all(blocks, "req", split_axis=0, concat_axis=0, tiled=True).reshape(shape)


def from_pair(array, n_req):
    return lax.ppermute(array, "req", [(i, i ^ 1) for i in range(n_req)])


def tp_parts(partial_sum):
    n_tp = lax.axis_size("tp")
    one, three, two = [
        lax.ppermute(partial_sum, "tp", [(i, (i + shift) % n_tp) for i in range(n_tp)])
        for shift in (1, 3, 2)
    ]
    return [partial_sum, two, one, three]


def shards(
    hidden,
    attn_gain,
    q_weight,
    o_weight,
    ffn_gain,
    gate_weight,
    up_weight,
    down_weight,
    kv_pool,
    block_home,
    chosen,
    chosen_count,
):
    n_req = lax.axis_size("req")
    requests, width = hidden.shape
    pool_dev = kv_pool.shape[1]
    block_tokens, head_size = kv_pool.shape[4:]
    heads = q_weight.shape[2] // head_size // 2
    side = n_req // 2
    q_rows = requests * heads
    sent_rows = q_rows + requests
    stat_rows = q_rows + 16
    f_rows = 16
    hidden_half = gate_weight.shape[2] // 2
    blocks = hidden_half // LANES
    tables = rotary_tables(float(block_home.shape[1] * block_tokens - 1), head_size)
    dma = pltpu.SemaphoreType.DMA

    def rows_type(rows, kind=BF16):
        return jax.ShapeDtypeStruct((rows, LANES), kind)

    def rows_scratch(rows):
        return pltpu.VMEM((rows, LANES), F32)

    def pair_type(rows):
        return jax.ShapeDtypeStruct((rows, 2 * width), BF16)

    keep, send = call(
        functools.partial(first_query_kernel, pool_dev),
        [rows_type(sent_rows, F32), rows_type(sent_rows)],
        [HBM] * 6,
        [
            pltpu.VMEM(hidden.shape, BF16),
            pltpu.VMEM(attn_gain.shape, BF16),
            pltpu.VMEM(q_weight.shape[1:], BF16),
            pltpu.VMEM(block_home.shape, jnp.int32),
            pltpu.VMEM(chosen.shape, jnp.int32),
            pltpu.VMEM((1, LAYERS), jnp.int32),
            rows_scratch(q_rows),
            dma((6,)),
        ],
        limit=61,
    )(
        hidden,
        attn_gain,
        q_weight,
        block_home,
        chosen,
        chosen_count.reshape(1, LAYERS),
    )
    payload = call(pair_total_kernel, rows_type(side * sent_rows), [VMEM] * 2)(
        keep, from_pair(send, n_req)
    )
    payload, kv_later, o_later, gate_later, up_later, down_later, q_later = lax.optimization_barrier(
        (payload, kv_pool, o_weight, gate_weight, up_weight, down_weight, q_weight)
    )
    pool_other = from_pair(kv_later, n_req)
    o_other = from_pair(o_later, n_req)
    gate_other = from_pair(gate_later, n_req)
    up_other = from_pair(up_later, n_req)
    down_other = from_pair(down_later, n_req)
    q_other = from_pair(q_later, n_req)
    current, attn_gain, ffn_gain = call(
        pair_state_kernel,
        [pair_type(requests), pair_type(LAYERS), pair_type(LAYERS)],
        [VMEM] * 6,
    )(
        hidden,
        from_pair(hidden, n_req),
        attn_gain,
        from_pair(attn_gain, n_req),
        ffn_gain,
        from_pair(ffn_gain, n_req),
    )

    parts = None
    table = None
    for layer_no in range(LAYERS):
        if parts is not None:
            current, payload = call(
                functools.partial(query_kernel, layer_no),
                [pair_type(requests), rows_type(side * sent_rows)],
                [VMEM] * 6 + [HBM] * 2,
                [
                    pltpu.VMEM((2 * width, heads * head_size), BF16),
                    rows_scratch(q_rows),
                    dma((2,)),
                ],
            )(current, *parts, attn_gain, q_weight, q_other)
        received = exchange(payload, n_req)
        scratch = [
            pltpu.VMEM((2, pool_dev, 2, block_tokens, head_size), BF16),
            rows_scratch(q_rows),
            dma((4, 2)),
        ]
        if table is None:
            payload, table = call(
                functools.partial(first_block_kernel, side),
                [rows_type(side * stat_rows), rows_type(requests, F32)],
                [VMEM] * 2 + [HBM] * 2,
                scratch,
            )(received, tables, kv_pool, pool_other)
        else:
            payload = call(
                functools.partial(later_block_kernel, layer_no, side),
                rows_type(side * stat_rows),
                [VMEM] * 3 + [HBM] * 2,
                scratch,
            )(received, table, tables, kv_pool, pool_other)
        context = call(functools.partial(combine_kernel, side), rows_type(q_rows), [VMEM])(
            exchange(payload, n_req)
        )
        own = call(
            functools.partial(context_kernel, layer_no, requests),
            pair_type(requests),
            [VMEM] * 2 + [HBM] * 2,
            [pltpu.VMEM((o_weight.shape[1], 2 * width), BF16), rows_scratch(q_rows), dma((2,))],
        )(context, from_pair(context, n_req), o_weight, o_other)
        chunk = requests // side * 2 * f_rows
        current, payload = call(
            functools.partial(gate_up_kernel, layer_no, chunk),
            [pair_type(requests), rows_type(requests * 2 * f_rows)],
            [VMEM] * 6 + [HBM] * 4,
            [
                pltpu.VMEM((2 * width, hidden_half), BF16),
                pltpu.VMEM((2 * width, hidden_half), BF16),
                rows_scratch(requests * 2 * f_rows),
                dma((4, 2)),
            ],
        )(current, *tp_parts(own), ffn_gain, gate_weight, gate_other, up_weight, up_other)
        chunk = requests // side * f_rows
        act = call(
            functools.partial(activation_kernel, blocks, side, f_rows),
            rows_type(n_req * chunk),
            [VMEM],
        )(exchange(payload, n_req))
        own = call(
            functools.partial(down_kernel, layer_no, f_rows, chunk),
            pair_type(requests),
            [VMEM] + [HBM] * 2,
            [
                pltpu.VMEM((down_weight.shape[1], 2 * width), BF16),
                rows_scratch(n_req * chunk),
                dma((2, 2)),
            ],
        )(exchange_all(act, n_req), down_weight, down_other)
        parts = tp_parts(own)
    return call(last_kernel, jax.ShapeDtypeStruct(hidden.shape, BF16), [VMEM] * 5)(current, *parts)


def solution(mesh):
    return jax.shard_map(
        shards,
        mesh=mesh,
        in_specs=(
            P(None, "req"),
            P(None, "req"),
            P(None, "req", "tp"),
            P(None, "tp", "req"),
            P(None, "req"),
            P(None, "req", "tp"),
            P(None, "req", "tp"),
            P(None, "tp", "req"),
            P(None, "req", "tp", None, None, None),
            P("req", None),
            P(None, "req", "tp", None),
            P(None, "req", "tp"),
        ),
        out_specs=P(None, "req"),
        check_vma=False,
    )
```

```python
import functools
import math

import jax
import jax.numpy as jnp
import numpy as np
from jax import lax
from jax.experimental import pallas as pl
from jax.experimental.pallas import tpu as pltpu
from jax.sharding import PartitionSpec as P

D = 8192
LAYERS = 2
LANES = 128

MASK_FILL = -1e30
EPSILON = 1e-05

VMEM = pl.BlockSpec(memory_space=pltpu.VMEM)
SMEM = pl.BlockSpec(memory_space=pltpu.SMEM)
HBM = pl.BlockSpec(memory_space=pltpu.HBM)
ANY = pl.BlockSpec(memory_space=pl.ANY)
F32 = jnp.float32
BF16 = jnp.bfloat16


def rotary_tables(position, head_size):
    freq_idx = np.arange(head_size // 2)
    angles = position * np.exp(freq_idx * (-2.0 * math.log(500000.0) / head_size))
    cosine, sine_part = np.cos(angles), np.sin(angles)
    scale = head_size**-0.5
    tables = np.stack([np.concatenate([cosine, cosine]), np.concatenate([-sine_part, sine_part])])
    return jnp.asarray(tables * scale, F32)


def call(kernel, out_shape, in_specs, scratch=(), limit=16, out_specs=None, flops=10000000000, nbytes=0):
    return pl.pallas_call(
        kernel,
        out_shape=out_shape,
        in_specs=in_specs,
        out_specs=out_specs if out_specs is not None else jax.tree.map(lambda _: VMEM, out_shape),
        scratch_shapes=list(scratch),
        compiler_params=pltpu.CompilerParams(vmem_limit_bytes=limit * 1024 * 1024),
        cost_estimate=pl.CostEstimate(flops=flops, bytes_accessed=nbytes, transcendentals=0),
    )


def core_side():
    return lax.rem(lax.axis_index("req"), 2)


def joined(own, other, axis):
    first = core_side() == 0
    return jnp.concatenate([jnp.where(first, own, other), jnp.where(first, other, own)], axis=axis)


def pair_copies(own_hbm, other_hbm, own_target, other_target, sems):
    return [
        pltpu.make_async_copy(own_hbm, own_target, sems.at[0]),
        pltpu.make_async_copy(other_hbm, other_target, sems.at[1]),
    ]


def side_slices(size):
    side = core_side()
    return (
        pl.ds(pl.multiple_of(side * size, LANES), size),
        pl.ds(pl.multiple_of((1 - side) * size, LANES), size),
    )


def column_copies(layer_no, own_hbm, other_hbm, weight, sems):
    own, other = side_slices(own_hbm.shape[2])
    return pair_copies(
        own_hbm.at[layer_no], other_hbm.at[layer_no], weight.at[:, own], weight.at[:, other], sems
    )


def row_copies(layer_no, own_hbm, other_hbm, weight, sems):
    half, _ = side_slices(weight.shape[1])
    own, other = side_slices(own_hbm.shape[1])
    return pair_copies(
        own_hbm.at[layer_no, :, half],
        other_hbm.at[layer_no, :, half],
        weight.at[own],
        weight.at[other],
        sems,
    )


def start_all(copies):
    for copy in copies:
        copy.start()


def wait_all(copies):
    for copy in copies:
        copy.wait()


def squares_in_lanes(current):
    squares = jnp.sum(current * current, axis=1, keepdims=True)
    high = squares.astype(BF16).astype(F32)
    lane = lax.broadcasted_iota(jnp.int32, (current.shape[0], LANES), 1)
    return jnp.where(lane == 0, high, jnp.where(lane == 1, squares - high, 0.0))


def along_lanes(column):
    n = column.shape[0]
    row = lax.broadcasted_iota(jnp.int32, (n, LANES), 0)
    lane = lax.broadcasted_iota(jnp.int32, (n, LANES), 1)
    return jnp.sum(jnp.where(row == lane, column, 0.0), axis=0, keepdims=True)


def along_rows(line, n):
    row = lax.broadcasted_iota(jnp.int32, (n, LANES), 0)
    lane = lax.broadcasted_iota(jnp.int32, (n, LANES), 1)
    return jnp.sum(jnp.where(row == lane, line, 0.0), axis=1, keepdims=True)


def square_rows(current, rows):
    squares = jnp.sum(current * current, axis=1, keepdims=True)
    high = squares.astype(BF16).astype(F32)
    row = lax.broadcasted_iota(jnp.int32, (rows, LANES), 0)
    low = jnp.where(row == 1, along_lanes(squares - high), 0.0)
    return jnp.where(row == 0, along_lanes(high), low)


def store_blocks(packed, product):
    requests, width = product.shape
    blocks = width // LANES
    for k in range(blocks):
        packed[pl.ds(k, requests, stride=blocks), :] = product[:, k * LANES : (k + 1) * LANES]
    return packed[...]


def spread(packed, values, stride):
    for k in range(stride):
        packed[pl.ds(k, values.shape[0], stride=stride), :] = values
    return packed[...]


def rows_of(packed, requests, blocks):
    return jnp.concatenate(
        [packed[pl.ds(k, requests, stride=blocks), :] for k in range(blocks)], axis=1
    )


def repeat_into(out_ref, values):
    rows = values.shape[0]
    for i in range(out_ref.shape[0] // rows):
        out_ref[i * rows : (i + 1) * rows, :] = values


def pair_sum(current, parts):
    a, b, c, d = [part[...].astype(F32) for part in parts]
    return (current[...].astype(F32) + ((a + b) + (c + d))).astype(BF16)


def slot_table(homes, chosen, counts, pool_dev, requests):
    n_blocks = homes.shape[1]
    shape = (n_blocks, n_blocks)
    row = lax.broadcasted_iota(jnp.int32, shape, 0)
    col = lax.broadcasted_iota(jnp.int32, shape, 1)
    places = jnp.broadcast_to(homes, shape)
    here = lax.div(places, pool_dev) == row

    def across(column):
        return jnp.sum(jnp.where(row == col, column, 0.0), axis=0, keepdims=True)

    slots = jnp.sum(jnp.where(here, lax.rem(places, pool_dev), 0).astype(F32), axis=1, keepdims=True)
    found = [jnp.zeros((1, n_blocks), F32), across(slots)]
    for layer_no in range(LAYERS):
        listed = chosen[layer_no]
        entry = lax.broadcasted_iota(jnp.int32, (n_blocks, listed.shape[1]), 1)
        block = lax.broadcasted_iota(jnp.int32, (n_blocks, listed.shape[1]), 0)
        hit = (listed == block) & (entry < counts[layer_no])
        taken = across(jnp.max(jnp.where(hit, 1.0, 0.0), axis=1, keepdims=True))
        found.append(across(jnp.max(jnp.where(here, taken, 0.0), axis=1, keepdims=True)))
    line = jnp.concatenate(found, axis=1)
    mine = lax.broadcasted_iota(jnp.int32, (requests, LANES), 0) == lax.axis_index("req")
    return jnp.where(mine, line, 0.0)


def first_query_kernel(
    pool_dev,
    x_hbm,
    gain_hbm,
    weight_hbm,
    homes_hbm,
    chosen_hbm,
    count_hbm,
    keep_ref,
    send_ref,
    x,
    gain,
    weight,
    homes,
    chosen,
    counts,
    packed,
    sems,
):
    copies = [
        pltpu.make_async_copy(source, target, sems.at[i])
        for i, (source, target) in enumerate(
            [
                (homes_hbm, homes),
                (chosen_hbm, chosen),
                (count_hbm, counts),
                (x_hbm, x),
                (gain_hbm, gain),
                (weight_hbm.at[0], weight),
            ]
        )
    ]
    start_all(copies)
    wait_all(copies[:3])
    lists = [chosen[i, 0] for i in range(LAYERS)]
    limits = [counts[:, i : i + 1] for i in range(LAYERS)]
    table = slot_table(homes[...], lists, limits, pool_dev, x.shape[0])
    wait_all(copies[3:])
    current = x[...].astype(F32)
    scaled = (current * gain[0:1, :].astype(F32)).astype(BF16)
    product = jnp.dot(scaled, weight[...], preferred_element_type=F32)
    middle = product.shape[1] // 2
    first = core_side() == 0
    rows = packed.shape[0]
    keep_ref[:rows, :] = store_blocks(packed, jnp.where(first, product[:, :middle], product[:, middle:]))
    send = store_blocks(packed, jnp.where(first, product[:, middle:], product[:, :middle]))
    send_ref[:rows, :] = send.astype(BF16)
    extra = squares_in_lanes(current) + table
    keep_ref[rows:, :] = extra
    send_ref[rows:, :] = extra.astype(BF16)


def fetch_kernel(sources, *refs):
    count = len(sources)
    ins, outs, sems = refs[:count], refs[count + 1 : -1], refs[-1]
    copies = [
        pltpu.make_async_copy(source(ref), outs[place].at[part], sems.at[i])
        for i, (ref, (source, place, part)) in enumerate(zip(ins, sources))
    ]
    start_all(copies)
    wait_all(copies)


def fetch(sources, operands, shapes, after):
    return call(
        functools.partial(fetch_kernel, sources),
        [jax.ShapeDtypeStruct(shape, BF16) for shape in shapes],
        [HBM] * len(operands) + [ANY],
        [pltpu.SemaphoreType.DMA((len(operands),))],
        flops=2000000000,
    )(*operands, after)


def pair_total_kernel(keep_ref, received_ref, out_ref):
    repeat_into(out_ref, (keep_ref[...] + received_ref[...].astype(F32)).astype(BF16))


def pair_state_kernel(x, x_other, gain, gain_other, ffn, ffn_other, x_out, gain_out, ffn_out):
    for own, other, out in ((x, x_other, x_out), (gain, gain_other, gain_out), (ffn, ffn_other, ffn_out)):
        out[...] = joined(own[...].astype(F32), other[...].astype(F32), 1).astype(BF16)


def query_kernel(layer_no, x_ref, a, b, c, d, gain_ref, weight_ref, out_ref, payload_ref, packed):
    out_ref[...] = pair_sum(x_ref, (a, b, c, d))
    current = out_ref[...].astype(F32)
    scaled = current * gain_ref[layer_no : layer_no + 1, :].astype(F32)
    middle = scaled.shape[1] // 2
    first = core_side() == 0
    mine = jnp.where(first, scaled[:, :middle], scaled[:, middle:]).astype(BF16)
    theirs = jnp.where(first, scaled[:, middle:], scaled[:, :middle]).astype(BF16)
    product = jnp.dot(mine, weight_ref[0], preferred_element_type=F32)
    product += jnp.dot(theirs, weight_ref[1], preferred_element_type=F32)
    extra = square_rows(current, payload_ref.shape[0] // 16 - packed.shape[0])
    rows = jnp.concatenate([store_blocks(packed, product), extra], axis=0)
    repeat_into(payload_ref, rows.astype(BF16))


def in_parts(values, count):
    parts = []
    for _ in range(count):
        part = values.astype(BF16).astype(F32)
        parts.append(part)
        values = values - part
    return parts


def stats_in_lanes(block_max, block_sum):
    shape = (block_max.shape[0], LANES)
    lane = lax.broadcasted_iota(jnp.int32, shape, 1)
    stats = jnp.zeros(shape, F32)
    for place, part in enumerate(in_parts(block_max, 3) + in_parts(block_sum, 2)):
        stats = jnp.where(lane == place, part, stats)
    return stats


def block_kernel(
    layer_no, sources, received_ref, table_ref, tables_ref, own_hbm, other_hbm, out_ref, table_out, blocks, packed, sems
):
    n_slots = blocks.shape[1]
    piece = n_slots // 1
    copies = [
        [
            pltpu.make_async_copy(
                pool.at[layer_no, pl.ds(at, piece), 0, part],
                blocks.at[b, pl.ds(at, piece), part],
                sems.at[(part * n_slots + at) // piece, b],
            )
            for b, pool in enumerate((own_hbm, other_hbm))
        ]
        for part in range(2)
        for at in range(0, n_slots, piece)
    ]
    for pair in copies:
        start_all(pair)
    rows = packed.shape[0]
    totals = jnp.sum(received_ref[...].astype(F32).reshape(sources, -1, LANES), axis=0)
    extra = totals[rows:]
    requests = extra.shape[0] if table_ref is None else table_ref.shape[0]
    heads = rows // requests
    if table_ref is None:
        squares = extra[:, 0:1] + extra[:, 1:2]
    else:
        squares = along_rows(extra[0:1] + extra[1:2], requests)
    inv = lax.rsqrt(squares / D + EPSILON)
    queries = totals[:rows] * spread(packed, jnp.broadcast_to(inv, (requests, LANES)), heads)
    queries = queries * tables_ref[0:1, :] + pltpu.roll(queries, LANES // 2, 1) * tables_ref[1:2, :]
    queries = queries.astype(BF16)

    table = extra if table_ref is None else table_ref[...]
    if table_out is not None:
        table_out[...] = extra
    me = lax.axis_index("req")
    lane = lax.broadcasted_iota(jnp.int32, table.shape, 1)
    request = lax.broadcasted_iota(jnp.int32, (requests, rows), 0)
    column = lax.broadcasted_iota(jnp.int32, (requests, rows), 1)
    row = lax.broadcasted_iota(jnp.int32, (2 * n_slots * heads, rows), 0)
    head = lax.rem(column, heads).astype(F32)
    places, used = [], []
    for b in range(2):
        store = me if b == 0 else me + 1 - 2 * core_side()
        slots = jnp.sum(jnp.where(lane == n_slots + store, table, 0.0), axis=1, keepdims=True)
        taken = jnp.where(lane == (2 + layer_no) * n_slots + store, table, 0.0)
        taken = jnp.broadcast_to(jnp.sum(taken, axis=1, keepdims=True), table.shape)
        used.append(spread(packed, taken, heads))
        target = jnp.where(
            lax.div(column, heads) == request, slots * (2 * heads) + (head + b * heads), 0.0
        )
        target = jnp.sum(target, axis=0, keepdims=True).astype(jnp.int32)
        places.append(jnp.where(row == target, 1.0, 0.0))
    by_slot = jnp.concatenate(places, axis=1)
    queries = jnp.dot(
        by_slot.astype(BF16), jnp.concatenate([queries, queries], axis=0), preferred_element_type=F32
    )
    group = 2 * heads
    mine = lax.broadcasted_iota(jnp.int32, (group, LANES), 0) < heads

    def of_slot(left, p, part, contract):
        if p % piece == 0:
            wait_all(copies[(part * n_slots + p) // piece])
        left = left[p * group : (p + 1) * group]
        left = jnp.concatenate([jnp.where(mine, left, 0.0), jnp.where(mine, 0.0, left)], axis=1)
        right = jnp.concatenate([blocks[0, p, part], blocks[1, p, part]], axis=contract)
        return lax.dot_general(
            left.astype(BF16), right, (((1,), (contract,)), ((), ())), preferred_element_type=F32
        )

    scores = jnp.concatenate([of_slot(queries, p, 0, 1) for p in range(n_slots)], axis=0)
    block_max = jnp.max(scores, axis=1, keepdims=True)
    terms = jnp.exp(scores - block_max)
    block_sum = jnp.sum(terms, axis=1, keepdims=True)
    acc = jnp.concatenate([of_slot(terms, p, 1, 0) for p in range(n_slots)], axis=0)
    both = jnp.concatenate([acc, stats_in_lanes(block_max, block_sum)], axis=1).astype(BF16)
    both = jnp.dot(by_slot.T.astype(BF16), both, preferred_element_type=F32)
    sides = []
    for b in range(2):
        side = both[b * rows : (b + 1) * rows]
        stats = side[:, LANES:]
        block_max = stats[:, 0:1] + stats[:, 1:2] + stats[:, 2:3]
        block_max = jnp.where(used[b][:, 0:1] > 0.0, block_max, MASK_FILL)
        sides.append((block_max, stats[:, 3:4] + stats[:, 4:5], side[:, :LANES]))
    top = jnp.maximum(sides[0][0], sides[1][0])
    rescale = [jnp.exp(side[0] - top) for side in sides]
    total = rescale[0] * sides[0][1] + rescale[1] * sides[1][1]
    acc = rescale[0] * sides[0][2] + rescale[1] * sides[1][2]
    stats = stats_in_lanes(top, total).T
    extra = out_ref.shape[0] // sources - rows
    repeat_into(out_ref, jnp.concatenate([acc, stats[:extra]], axis=0).astype(BF16))


def first_block_kernel(sources, received_ref, tables_ref, own_hbm, other_hbm, out_ref, table_out, *scratch):
    block_kernel(
        0, sources, received_ref, None, tables_ref, own_hbm, other_hbm, out_ref, table_out, *scratch
    )


def later_block_kernel(
    layer_no, sources, received_ref, table_ref, tables_ref, own_hbm, other_hbm, out_ref, *scratch
):
    block_kernel(
        layer_no, sources, received_ref, table_ref, tables_ref, own_hbm, other_hbm, out_ref, None, *scratch
    )


def combine_kernel(sources, received_ref, out_ref):
    rows = out_ref.shape[0]
    both = received_ref[...].astype(F32).reshape(sources, -1, LANES)
    stats = [both[s, rows : rows + 8, :] for s in range(sources)]
    block_max = jnp.concatenate([x[0:1] + x[1:2] + x[2:3] for x in stats], axis=0)
    block_sum = jnp.concatenate([x[3:4] + x[4:5] for x in stats], axis=0)
    rescale = jnp.exp(block_max - jnp.max(block_max, axis=0, keepdims=True))
    factors = rescale / jnp.sum(rescale * block_sum, axis=0, keepdims=True)
    factors = jnp.concatenate([factors, jnp.zeros((LANES - sources, LANES), F32)], axis=0).T
    context = jnp.zeros((rows, LANES), F32)
    for s in range(sources):
        context += both[s, :rows, :] * factors[:, s : s + 1]
    out_ref[...] = context.astype(BF16)


def context_kernel(
    layer_no, requests, own_ref, other_ref, own_hbm, other_hbm, out_ref, weight, packed, sems
):
    copies = column_copies(layer_no, own_hbm, other_hbm, weight, sems)
    start_all(copies)
    sides = []
    for ref in (own_ref, other_ref):
        packed[...] = ref[...].astype(F32)
        sides.append(rows_of(packed, requests, packed.shape[0] // requests))
    rows = joined(sides[0], sides[1], 1).astype(BF16)
    wait_all(copies)
    out_ref[...] = jnp.dot(rows, weight[...], preferred_element_type=F32).astype(BF16)


def gate_up_kernel(
    layer_no,
    chunk,
    x_ref,
    a,
    b,
    c,
    d,
    gain_ref,
    gate_hbm,
    gate_other,
    up_hbm,
    up_other,
    out_ref,
    payload_ref,
    gate,
    up,
    packed,
    sems,
):
    width = gate.shape[1]
    piece = width // 1
    own_rows, other_rows = side_slices(gate_hbm.shape[1])
    steps = []
    for i, (own, other, weight) in enumerate(((gate_hbm, gate_other, gate), (up_hbm, up_other, up))):
        for j in range(width // piece):
            columns = pl.ds(pl.multiple_of(core_side() * width + j * piece, LANES), piece)
            local = pl.ds(j * piece, piece)
            copies = pair_copies(
                own.at[layer_no, :, columns],
                other.at[layer_no, :, columns],
                weight.at[own_rows, local],
                weight.at[other_rows, local],
                sems.at[len(steps)],
            )
            start_all(copies)
            steps.append((i, j, copies, weight))
    requests = x_ref.shape[0]
    per_chunk = chunk // (packed.shape[0] // requests)
    stride = packed.shape[0] // requests
    count = requests // per_chunk
    blocks = gate.shape[1] // LANES
    half = stride // 2

    def store(row, values):
        for q in range(per_chunk):
            packed[pl.ds(q * stride + row, count, stride=chunk), :] = values[q * count : (q + 1) * count]

    out_ref[...] = pair_sum(x_ref, (a, b, c, d))
    current = out_ref[...].astype(F32)
    scaled = (current * gain_ref[layer_no : layer_no + 1, :].astype(F32)).astype(BF16)
    zeros = jnp.zeros((requests, LANES), F32)
    store(blocks, squares_in_lanes(current))
    for row in [*range(blocks + 1, half), *range(half + blocks, stride)]:
        store(row, zeros)
    for i, j, copies, weight in steps:
        wait_all(copies)
        product = jnp.dot(scaled, weight[:, j * piece : (j + 1) * piece], preferred_element_type=F32)
        for k in range(piece // LANES):
            store(i * half + j * (piece // LANES) + k, product[:, k * LANES : (k + 1) * LANES])
    payload_ref[...] = packed[...].astype(BF16)


def fetched_gate_up_kernel(
    layer_no, chunk, x_ref, a, b, c, d, gain_ref, gate_ref, up_ref, out_ref, payload_ref, packed
):
    requests = x_ref.shape[0]
    stride = packed.shape[0] // requests
    per_chunk = chunk // stride
    count = requests // per_chunk
    blocks = gate_ref.shape[2] // LANES
    half = stride // 2

    def store(row, values):
        for q in range(per_chunk):
            packed[pl.ds(q * stride + row, count, stride=chunk), :] = values[q * count : (q + 1) * count]

    out_ref[...] = pair_sum(x_ref, (a, b, c, d))
    current = out_ref[...].astype(F32)
    scaled = current * gain_ref[layer_no : layer_no + 1, :].astype(F32)
    middle = scaled.shape[1] // 2
    first = core_side() == 0
    mine = jnp.where(first, scaled[:, :middle], scaled[:, middle:]).astype(BF16)
    theirs = jnp.where(first, scaled[:, middle:], scaled[:, :middle]).astype(BF16)
    zeros = jnp.zeros((requests, LANES), F32)
    store(blocks, squares_in_lanes(current))
    for row in [*range(blocks + 1, half), *range(half + blocks, stride)]:
        store(row, zeros)
    for i, weight in enumerate((gate_ref, up_ref)):
        product = jnp.dot(mine, weight[0], preferred_element_type=F32)
        product += jnp.dot(theirs, weight[1], preferred_element_type=F32)
        for k in range(blocks):
            store(i * half + k, product[:, k * LANES : (k + 1) * LANES])
    payload_ref[...] = packed[...].astype(BF16)


def activation_kernel(blocks, sources, half, received_ref, out_ref):
    totals = jnp.sum(received_ref[...].astype(F32).reshape(sources, -1, LANES), axis=0)
    acts = []
    for at in range(0, totals.shape[0], 2 * half):
        squares = totals[at + blocks : at + blocks + 1, 0:1] + totals[at + blocks : at + blocks + 1, 1:2]
        inv = lax.rsqrt(squares / D + EPSILON)
        gate = totals[at : at + half] * inv
        acts.append(gate / (1.0 + jnp.exp(-gate)) * (totals[at + half : at + 2 * half] * inv))
    repeat_into(out_ref, jnp.concatenate(acts, axis=0).astype(BF16))


def down_kernel(
    layer_no, half, chunk, received_ref, own_hbm, other_hbm, out_ref, weight, packed, sems
):
    depth = weight.shape[0] // 14
    own_columns, other_columns = side_slices(own_hbm.shape[2])
    steps = []
    for step in range(weight.shape[0] // depth):
        rows = pl.ds(step * depth, depth)
        steps.append(
            pair_copies(
                own_hbm.at[layer_no, rows],
                other_hbm.at[layer_no, rows],
                weight.at[rows, own_columns],
                weight.at[rows, other_columns],
                sems.at[step],
            )
        )
        start_all(steps[step])
    packed[...] = received_ref[...].astype(F32)
    blocks = weight.shape[0] // LANES // 2
    per_chunk = chunk // half
    count = out_ref.shape[0] // per_chunk
    total = 0.0
    for side in range(2):
        columns = []
        for k in range(blocks):
            columns.append(
                jnp.concatenate(
                    [
                        packed[pl.ds(side * chunk + q * half + k, count, stride=2 * chunk), :]
                        for q in range(per_chunk)
                    ],
                    axis=0,
                ).astype(BF16)
            )
        rows = jnp.concatenate(columns, axis=1)
        for at in range(0, rows.shape[1], depth):
            first = side * rows.shape[1] + at
            wait_all(steps[first // depth])
            total += jnp.dot(
                rows[:, at : at + depth], weight[first : first + depth], preferred_element_type=F32
            )
    out_ref[...] = total.astype(BF16)


def last_kernel(x_ref, a, b, c, d, out_ref):
    total = pair_sum(x_ref, (a, b, c, d)).astype(F32)
    width = out_ref.shape[1]
    out_ref[...] = jnp.where(core_side() == 0, total[:, :width], total[:, width:]).astype(BF16)


def exchange(array, n_req):
    shape = array.shape
    sides = [list(range(core, n_req, 2)) for core in range(2)]
    count = n_req // 2
    blocks = array.reshape((count, shape[0] // count) + shape[1:])
    return lax.all_to_all(
        blocks, "req", split_axis=0, concat_axis=0, tiled=True, axis_index_groups=sides
    ).reshape(shape)


def exchange_all(array, n_req):
    shape = array.shape
    blocks = array.reshape((n_req, shape[0] // n_req) + shape[1:])
    return lax.all_to_all(blocks, "req", split_axis=0, concat_axis=0, tiled=True).reshape(shape)


def from_pair(array, n_req):
    return lax.ppermute(array, "req", [(i, i ^ 1) for i in range(n_req)])


def tp_parts(partial_sum):
    n_tp = lax.axis_size("tp")
    one, three, two = [
        lax.ppermute(partial_sum, "tp", [(i, (i + shift) % n_tp) for i in range(n_tp)])
        for shift in (1, 3, 2)
    ]
    return [partial_sum, two, one, three]


def shards(
    hidden,
    attn_gain,
    q_weight,
    o_weight,
    ffn_gain,
    gate_weight,
    up_weight,
    down_weight,
    kv_pool,
    block_home,
    chosen,
    chosen_count,
):
    n_req = lax.axis_size("req")
    requests, width = hidden.shape
    pool_dev = kv_pool.shape[1]
    block_tokens, head_size = kv_pool.shape[4:]
    heads = q_weight.shape[2] // head_size // 2
    side = n_req // 2
    q_rows = requests * heads
    sent_rows = q_rows + requests
    stat_rows = q_rows + 16
    f_rows = 16
    hidden_half = gate_weight.shape[2] // 2
    blocks = hidden_half // LANES
    tables = rotary_tables(float(block_home.shape[1] * block_tokens - 1), head_size)
    dma = pltpu.SemaphoreType.DMA

    def rows_type(rows, kind=BF16):
        return jax.ShapeDtypeStruct((rows, LANES), kind)

    def rows_scratch(rows):
        return pltpu.VMEM((rows, LANES), F32)

    def pair_type(rows):
        return jax.ShapeDtypeStruct((rows, 2 * width), BF16)

    keep, send = call(
        functools.partial(first_query_kernel, pool_dev),
        [rows_type(sent_rows, F32), rows_type(sent_rows)],
        [HBM] * 6,
        [
            pltpu.VMEM(hidden.shape, BF16),
            pltpu.VMEM(attn_gain.shape, BF16),
            pltpu.VMEM(q_weight.shape[1:], BF16),
            pltpu.VMEM(block_home.shape, jnp.int32),
            pltpu.VMEM(chosen.shape, jnp.int32),
            pltpu.VMEM((1, LAYERS), jnp.int32),
            rows_scratch(q_rows),
            dma((6,)),
        ],
        limit=61,
    )(
        hidden,
        attn_gain,
        q_weight,
        block_home,
        chosen,
        chosen_count.reshape(1, LAYERS),
    )
    payload = call(pair_total_kernel, rows_type(side * sent_rows), [VMEM] * 2)(
        keep, from_pair(send, n_req)
    )
    payload, kv_later, o_later, gate_later, up_later, down_later, q_later = lax.optimization_barrier(
        (payload, kv_pool, o_weight, gate_weight, up_weight, down_weight, q_weight)
    )
    pool_other = from_pair(kv_later, n_req)
    o_other = from_pair(o_later, n_req)
    gate_other = from_pair(gate_later, n_req)
    up_other = from_pair(up_later, n_req)
    down_other = from_pair(down_later, n_req)
    q_other = from_pair(q_later, n_req)
    current, attn_gain, ffn_gain = call(
        pair_state_kernel,
        [pair_type(requests), pair_type(LAYERS), pair_type(LAYERS)],
        [VMEM] * 6,
    )(
        hidden,
        from_pair(hidden, n_req),
        attn_gain,
        from_pair(attn_gain, n_req),
        ffn_gain,
        from_pair(ffn_gain, n_req),
    )

    parts = None
    table = None
    for layer_no in range(LAYERS):
        if parts is not None:

            def half_of(ref, l=layer_no):
                return ref.at[l, :, side_slices(ref.shape[2] // 2)[0]]

            (weights,) = fetch(
                [(half_of, 0, b) for b in range(2)],
                (q_weight, q_other),
                [(2, width, heads * head_size)],
                act,
            )
            current, payload = call(
                functools.partial(query_kernel, layer_no),
                [pair_type(requests), rows_type(side * stat_rows)],
                [VMEM] * 7,
                [rows_scratch(q_rows)],
            )(current, *parts, attn_gain, weights)
        received = exchange(payload, n_req)
        scratch = [
            pltpu.VMEM((2, pool_dev, 2, block_tokens, head_size), BF16),
            rows_scratch(q_rows),
            dma((2, 2)),
        ]
        if table is None:
            payload, table = call(
                functools.partial(first_block_kernel, side),
                [rows_type(side * stat_rows), rows_type(requests, F32)],
                [VMEM] * 2 + [HBM] * 2,
                scratch,
            )(received, tables, kv_pool, pool_other)
        else:
            payload = call(
                functools.partial(later_block_kernel, layer_no, side),
                rows_type(side * stat_rows),
                [VMEM] * 3 + [HBM] * 2,
                scratch,
            )(received, table, tables, kv_pool, pool_other)
        stats = payload
        context = call(functools.partial(combine_kernel, side), rows_type(q_rows), [VMEM])(
            exchange(payload, n_req)
        )
        own = call(
            functools.partial(context_kernel, layer_no, requests),
            pair_type(requests),
            [VMEM] * 2 + [HBM] * 2,
            [pltpu.VMEM((o_weight.shape[1], 2 * width), BF16), rows_scratch(q_rows), dma((2,))],
        )(context, from_pair(context, n_req), o_weight, o_other)
        chunk = requests // side * 2 * f_rows
        if layer_no in (1,):

            def half_of(ref, l=layer_no):
                return ref.at[l, :, side_slices(ref.shape[2] // 2)[0]]

            gate_up = fetch(
                [(half_of, place, b) for place in range(2) for b in range(2)],
                (gate_weight, gate_other, up_weight, up_other),
                [(2, width, hidden_half)] * 2,
                stats,
            )
            current, payload = call(
                functools.partial(fetched_gate_up_kernel, layer_no, chunk),
                [pair_type(requests), rows_type(requests * 2 * f_rows)],
                [VMEM] * 8,
                [rows_scratch(requests * 2 * f_rows)],
            )(current, own, *tp_parts(own)[1:], ffn_gain, *gate_up)
        else:
            current, payload = call(
                functools.partial(gate_up_kernel, layer_no, chunk),
                [pair_type(requests), rows_type(requests * 2 * f_rows)],
                [VMEM] * 6 + [HBM] * 4,
                [
                    pltpu.VMEM((2 * width, hidden_half), BF16),
                    pltpu.VMEM((2 * width, hidden_half), BF16),
                    rows_scratch(requests * 2 * f_rows),
                    dma((2, 2)),
                ],
            )(current, *tp_parts(own), ffn_gain, gate_weight, gate_other, up_weight, up_other)
        chunk = requests // side * f_rows
        act = call(
            functools.partial(activation_kernel, blocks, side, f_rows),
            rows_type(n_req * chunk),
            [VMEM],
        )(exchange(payload, n_req))
        own = call(
            functools.partial(down_kernel, layer_no, f_rows, chunk),
            pair_type(requests),
            [VMEM] + [HBM] * 2,
            [
                pltpu.VMEM((down_weight.shape[1], 2 * width), BF16),
                rows_scratch(n_req * chunk),
                dma((14, 2)),
            ],
        )(exchange_all(act, n_req), down_weight, down_other)
        parts = tp_parts(own)
    return call(last_kernel, jax.ShapeDtypeStruct(hidden.shape, BF16), [VMEM] * 5)(current, *parts)


def solution(mesh):
    return jax.shard_map(
        shards,
        mesh=mesh,
        in_specs=(
            P(None, "req"),
            P(None, "req"),
            P(None, "req", "tp"),
            P(None, "tp", "req"),
            P(None, "req"),
            P(None, "req", "tp"),
            P(None, "req", "tp"),
            P(None, "tp", "req"),
            P(None, "req", "tp", None, None, None),
            P("req", None),
            P(None, "req", "tp", None),
            P(None, "req", "tp"),
        ),
        out_specs=P(None, "req"),
        check_vma=False,
    )
```

```python
import functools
import math

import jax
import jax.numpy as jnp
import numpy as np
from jax import lax
from jax.experimental import pallas as pl
from jax.experimental.pallas import tpu as pltpu
from jax.sharding import PartitionSpec as P

D = 8192
LAYERS = 2
LANES = 128

MASK_FILL = -1e30
EPSILON = 1e-05

VMEM = pl.BlockSpec(memory_space=pltpu.VMEM)
SMEM = pl.BlockSpec(memory_space=pltpu.SMEM)
HBM = pl.BlockSpec(memory_space=pltpu.HBM)
ANY = pl.BlockSpec(memory_space=pl.ANY)
F32 = jnp.float32
BF16 = jnp.bfloat16


def rotary_tables(position, head_size):
    freq_idx = np.arange(head_size // 2)
    angles = position * np.exp(freq_idx * (-2.0 * math.log(500000.0) / head_size))
    cosine, sine_part = np.cos(angles), np.sin(angles)
    scale = head_size**-0.5
    tables = np.stack([np.concatenate([cosine, cosine]), np.concatenate([-sine_part, sine_part])])
    return jnp.asarray(tables * scale, F32)


def call(kernel, out_shape, in_specs, scratch=(), limit=16, out_specs=None, flops=10000000000, nbytes=0):
    return pl.pallas_call(
        kernel,
        out_shape=out_shape,
        in_specs=in_specs,
        out_specs=out_specs if out_specs is not None else jax.tree.map(lambda _: VMEM, out_shape),
        scratch_shapes=list(scratch),
        compiler_params=pltpu.CompilerParams(vmem_limit_bytes=limit * 1024 * 1024),
        cost_estimate=pl.CostEstimate(flops=flops, bytes_accessed=nbytes, transcendentals=0),
    )


def core_side():
    return lax.rem(lax.axis_index("req"), 2)


def joined(own, other, axis):
    first = core_side() == 0
    return jnp.concatenate([jnp.where(first, own, other), jnp.where(first, other, own)], axis=axis)


def pair_copies(own_hbm, other_hbm, own_target, other_target, sems):
    return [
        pltpu.make_async_copy(own_hbm, own_target, sems.at[0]),
        pltpu.make_async_copy(other_hbm, other_target, sems.at[1]),
    ]


def side_slices(size):
    side = core_side()
    return (
        pl.ds(pl.multiple_of(side * size, LANES), size),
        pl.ds(pl.multiple_of((1 - side) * size, LANES), size),
    )


def column_copies(layer_no, own_hbm, other_hbm, weight, sems):
    own, other = side_slices(own_hbm.shape[2])
    return pair_copies(
        own_hbm.at[layer_no], other_hbm.at[layer_no], weight.at[:, own], weight.at[:, other], sems
    )


def row_copies(layer_no, own_hbm, other_hbm, weight, sems):
    half, _ = side_slices(weight.shape[1])
    own, other = side_slices(own_hbm.shape[1])
    return pair_copies(
        own_hbm.at[layer_no, :, half],
        other_hbm.at[layer_no, :, half],
        weight.at[own],
        weight.at[other],
        sems,
    )


def start_all(copies):
    for copy in copies:
        copy.start()


def wait_all(copies):
    for copy in copies:
        copy.wait()


def squares_in_lanes(current):
    squares = jnp.sum(current * current, axis=1, keepdims=True)
    high = squares.astype(BF16).astype(F32)
    lane = lax.broadcasted_iota(jnp.int32, (current.shape[0], LANES), 1)
    return jnp.where(lane == 0, high, jnp.where(lane == 1, squares - high, 0.0))


def along_lanes(column):
    n = column.shape[0]
    row = lax.broadcasted_iota(jnp.int32, (n, LANES), 0)
    lane = lax.broadcasted_iota(jnp.int32, (n, LANES), 1)
    return jnp.sum(jnp.where(row == lane, column, 0.0), axis=0, keepdims=True)


def along_rows(line, n):
    row = lax.broadcasted_iota(jnp.int32, (n, LANES), 0)
    lane = lax.broadcasted_iota(jnp.int32, (n, LANES), 1)
    return jnp.sum(jnp.where(row == lane, line, 0.0), axis=1, keepdims=True)


def square_rows(current, rows):
    squares = jnp.sum(current * current, axis=1, keepdims=True)
    high = squares.astype(BF16).astype(F32)
    row = lax.broadcasted_iota(jnp.int32, (rows, LANES), 0)
    low = jnp.where(row == 1, along_lanes(squares - high), 0.0)
    return jnp.where(row == 0, along_lanes(high), low)


def store_blocks(packed, product):
    requests, width = product.shape
    blocks = width // LANES
    for k in range(blocks):
        packed[pl.ds(k, requests, stride=blocks), :] = product[:, k * LANES : (k + 1) * LANES]
    return packed[...]


def spread(packed, values, stride):
    for k in range(stride):
        packed[pl.ds(k, values.shape[0], stride=stride), :] = values
    return packed[...]


def rows_of(packed, requests, blocks):
    return jnp.concatenate(
        [packed[pl.ds(k, requests, stride=blocks), :] for k in range(blocks)], axis=1
    )


def repeat_into(out_ref, values):
    rows = values.shape[0]
    for i in range(out_ref.shape[0] // rows):
        out_ref[i * rows : (i + 1) * rows, :] = values


def pair_sum(current, parts):
    a, b, c, d = [part[...].astype(F32) for part in parts]
    return (current[...].astype(F32) + ((a + b) + (c + d))).astype(BF16)


def slot_table(homes, chosen, counts, pool_dev, requests):
    n_blocks = homes.shape[1]
    shape = (n_blocks, n_blocks)
    row = lax.broadcasted_iota(jnp.int32, shape, 0)
    col = lax.broadcasted_iota(jnp.int32, shape, 1)
    places = jnp.broadcast_to(homes, shape)
    here = lax.div(places, pool_dev) == row

    def across(column):
        return jnp.sum(jnp.where(row == col, column, 0.0), axis=0, keepdims=True)

    slots = jnp.sum(jnp.where(here, lax.rem(places, pool_dev), 0).astype(F32), axis=1, keepdims=True)
    found = [jnp.zeros((1, n_blocks), F32), across(slots)]
    for layer_no in range(LAYERS):
        listed = chosen[layer_no]
        entry = lax.broadcasted_iota(jnp.int32, (n_blocks, listed.shape[1]), 1)
        block = lax.broadcasted_iota(jnp.int32, (n_blocks, listed.shape[1]), 0)
        hit = (listed == block) & (entry < counts[layer_no])
        taken = across(jnp.max(jnp.where(hit, 1.0, 0.0), axis=1, keepdims=True))
        found.append(across(jnp.max(jnp.where(here, taken, 0.0), axis=1, keepdims=True)))
    line = jnp.concatenate(found, axis=1)
    mine = lax.broadcasted_iota(jnp.int32, (requests, LANES), 0) == lax.axis_index("req")
    return jnp.where(mine, line, 0.0)


def first_query_kernel(
    pool_dev,
    x_hbm,
    gain_hbm,
    weight_hbm,
    homes_hbm,
    chosen_hbm,
    count_hbm,
    keep_ref,
    send_ref,
    x,
    gain,
    weight,
    homes,
    chosen,
    counts,
    packed,
    sems,
):
    copies = [
        pltpu.make_async_copy(source, target, sems.at[i])
        for i, (source, target) in enumerate(
            [
                (homes_hbm, homes),
                (chosen_hbm, chosen),
                (count_hbm, counts),
                (x_hbm, x),
                (gain_hbm, gain),
                (weight_hbm.at[0], weight),
            ]
        )
    ]
    start_all(copies)
    wait_all(copies[:3])
    lists = [chosen[i, 0] for i in range(LAYERS)]
    limits = [counts[:, i : i + 1] for i in range(LAYERS)]
    table = slot_table(homes[...], lists, limits, pool_dev, x.shape[0])
    wait_all(copies[3:])
    current = x[...].astype(F32)
    scaled = (current * gain[0:1, :].astype(F32)).astype(BF16)
    product = jnp.dot(scaled, weight[...], preferred_element_type=F32)
    middle = product.shape[1] // 2
    first = core_side() == 0
    rows = packed.shape[0]
    keep_ref[:rows, :] = store_blocks(packed, jnp.where(first, product[:, :middle], product[:, middle:]))
    send = store_blocks(packed, jnp.where(first, product[:, middle:], product[:, :middle]))
    send_ref[:rows, :] = send.astype(BF16)
    extra = squares_in_lanes(current) + table
    keep_ref[rows:, :] = extra
    send_ref[rows:, :] = extra.astype(BF16)


def fetch_kernel(sources, *refs):
    count = len(sources)
    ins, outs, sems = refs[:count], refs[count + 1 : -1], refs[-1]
    copies = [
        pltpu.make_async_copy(source(ref), outs[place].at[part], sems.at[i])
        for i, (ref, (source, place, part)) in enumerate(zip(ins, sources))
    ]
    start_all(copies)
    wait_all(copies)


def fetch(sources, operands, shapes, after):
    return call(
        functools.partial(fetch_kernel, sources),
        [jax.ShapeDtypeStruct(shape, BF16) for shape in shapes],
        [HBM] * len(operands) + [ANY],
        [pltpu.SemaphoreType.DMA((len(operands),))],
        flops=2000000000,
    )(*operands, after)


def pair_total_kernel(keep_ref, received_ref, out_ref):
    repeat_into(out_ref, (keep_ref[...] + received_ref[...].astype(F32)).astype(BF16))


def pair_state_kernel(x, x_other, gain, gain_other, ffn, ffn_other, x_out, gain_out, ffn_out):
    for own, other, out in ((x, x_other, x_out), (gain, gain_other, gain_out), (ffn, ffn_other, ffn_out)):
        out[...] = joined(own[...].astype(F32), other[...].astype(F32), 1).astype(BF16)


def query_kernel(layer_no, x_ref, a, b, c, d, gain_ref, weight_ref, out_ref, payload_ref, packed):
    out_ref[...] = pair_sum(x_ref, (a, b, c, d))
    current = out_ref[...].astype(F32)
    scaled = current * gain_ref[layer_no : layer_no + 1, :].astype(F32)
    middle = scaled.shape[1] // 2
    first = core_side() == 0
    mine = jnp.where(first, scaled[:, :middle], scaled[:, middle:]).astype(BF16)
    theirs = jnp.where(first, scaled[:, middle:], scaled[:, :middle]).astype(BF16)
    product = jnp.dot(mine, weight_ref[0], preferred_element_type=F32)
    product += jnp.dot(theirs, weight_ref[1], preferred_element_type=F32)
    extra = square_rows(current, payload_ref.shape[0] // 16 - packed.shape[0])
    rows = jnp.concatenate([store_blocks(packed, product), extra], axis=0)
    repeat_into(payload_ref, rows.astype(BF16))


def in_parts(values, count):
    parts = []
    for _ in range(count):
        part = values.astype(BF16).astype(F32)
        parts.append(part)
        values = values - part
    return parts


def stats_in_lanes(block_max, block_sum):
    shape = (block_max.shape[0], LANES)
    lane = lax.broadcasted_iota(jnp.int32, shape, 1)
    stats = jnp.zeros(shape, F32)
    for place, part in enumerate(in_parts(block_max, 3) + in_parts(block_sum, 2)):
        stats = jnp.where(lane == place, part, stats)
    return stats


def block_kernel(
    layer_no, sources, received_ref, table_ref, tables_ref, own_hbm, other_hbm, out_ref, table_out, blocks, packed, sems
):
    n_slots = blocks.shape[1]
    piece = n_slots // 1
    copies = [
        [
            pltpu.make_async_copy(
                pool.at[layer_no, pl.ds(at, piece), 0, part],
                blocks.at[b, pl.ds(at, piece), part],
                sems.at[(part * n_slots + at) // piece, b],
            )
            for b, pool in enumerate((own_hbm, other_hbm))
        ]
        for part in range(2)
        for at in range(0, n_slots, piece)
    ]
    for pair in copies:
        start_all(pair)
    rows = packed.shape[0]
    totals = jnp.sum(received_ref[...].astype(F32).reshape(sources, -1, LANES), axis=0)
    extra = totals[rows:]
    requests = extra.shape[0] if table_ref is None else table_ref.shape[0]
    heads = rows // requests
    if table_ref is None:
        squares = extra[:, 0:1] + extra[:, 1:2]
    else:
        squares = along_rows(extra[0:1] + extra[1:2], requests)
    inv = lax.rsqrt(squares / D + EPSILON)
    queries = totals[:rows] * spread(packed, jnp.broadcast_to(inv, (requests, LANES)), heads)
    queries = queries * tables_ref[0:1, :] + pltpu.roll(queries, LANES // 2, 1) * tables_ref[1:2, :]
    queries = queries.astype(BF16)

    table = extra if table_ref is None else table_ref[...]
    if table_out is not None:
        table_out[...] = extra
    me = lax.axis_index("req")
    lane = lax.broadcasted_iota(jnp.int32, table.shape, 1)
    request = lax.broadcasted_iota(jnp.int32, (requests, rows), 0)
    column = lax.broadcasted_iota(jnp.int32, (requests, rows), 1)
    row = lax.broadcasted_iota(jnp.int32, (2 * n_slots * heads, rows), 0)
    head = lax.rem(column, heads).astype(F32)
    places, used = [], []
    for b in range(2):
        store = me if b == 0 else me + 1 - 2 * core_side()
        slots = jnp.sum(jnp.where(lane == n_slots + store, table, 0.0), axis=1, keepdims=True)
        taken = jnp.where(lane == (2 + layer_no) * n_slots + store, table, 0.0)
        taken = jnp.broadcast_to(jnp.sum(taken, axis=1, keepdims=True), table.shape)
        used.append(spread(packed, taken, heads))
        target = jnp.where(
            lax.div(column, heads) == request, slots * (2 * heads) + (head + b * heads), 0.0
        )
        target = jnp.sum(target, axis=0, keepdims=True).astype(jnp.int32)
        places.append(jnp.where(row == target, 1.0, 0.0))
    by_slot = jnp.concatenate(places, axis=1)
    queries = jnp.dot(
        by_slot.astype(BF16), jnp.concatenate([queries, queries], axis=0), preferred_element_type=F32
    )
    group = 2 * heads
    mine = lax.broadcasted_iota(jnp.int32, (group, LANES), 0) < heads

    def of_slot(left, p, part, contract):
        if p % piece == 0:
            wait_all(copies[(part * n_slots + p) // piece])
        left = left[p * group : (p + 1) * group]
        left = jnp.concatenate([jnp.where(mine, left, 0.0), jnp.where(mine, 0.0, left)], axis=1)
        right = jnp.concatenate([blocks[0, p, part], blocks[1, p, part]], axis=contract)
        return lax.dot_general(
            left.astype(BF16), right, (((1,), (contract,)), ((), ())), preferred_element_type=F32
        )

    scores = jnp.concatenate([of_slot(queries, p, 0, 1) for p in range(n_slots)], axis=0)
    block_max = jnp.max(scores, axis=1, keepdims=True)
    terms = jnp.exp(scores - block_max)
    block_sum = jnp.sum(terms, axis=1, keepdims=True)
    acc = jnp.concatenate([of_slot(terms, p, 1, 0) for p in range(n_slots)], axis=0)
    both = jnp.concatenate([acc, stats_in_lanes(block_max, block_sum)], axis=1).astype(BF16)
    both = jnp.dot(by_slot.T.astype(BF16), both, preferred_element_type=F32)
    sides = []
    for b in range(2):
        side = both[b * rows : (b + 1) * rows]
        stats = side[:, LANES:]
        block_max = stats[:, 0:1] + stats[:, 1:2] + stats[:, 2:3]
        block_max = jnp.where(used[b][:, 0:1] > 0.0, block_max, MASK_FILL)
        sides.append((block_max, stats[:, 3:4] + stats[:, 4:5], side[:, :LANES]))
    top = jnp.maximum(sides[0][0], sides[1][0])
    rescale = [jnp.exp(side[0] - top) for side in sides]
    total = rescale[0] * sides[0][1] + rescale[1] * sides[1][1]
    acc = rescale[0] * sides[0][2] + rescale[1] * sides[1][2]
    stats = stats_in_lanes(top, total).T
    extra = out_ref.shape[0] // sources - rows
    repeat_into(out_ref, jnp.concatenate([acc, stats[:extra]], axis=0).astype(BF16))


def first_block_kernel(
    sources, received_ref, tables_ref, own_hbm, other_hbm, fetched_before, out_ref, table_out, *scratch
):
    del fetched_before
    block_kernel(
        0, sources, received_ref, None, tables_ref, own_hbm, other_hbm, out_ref, table_out, *scratch
    )


def later_block_kernel(
    layer_no, sources, received_ref, table_ref, tables_ref, own_hbm, other_hbm, out_ref, *scratch
):
    block_kernel(
        layer_no, sources, received_ref, table_ref, tables_ref, own_hbm, other_hbm, out_ref, None, *scratch
    )


def combine_kernel(sources, received_ref, out_ref):
    rows = out_ref.shape[0]
    both = received_ref[...].astype(F32).reshape(sources, -1, LANES)
    stats = [both[s, rows : rows + 8, :] for s in range(sources)]
    block_max = jnp.concatenate([x[0:1] + x[1:2] + x[2:3] for x in stats], axis=0)
    block_sum = jnp.concatenate([x[3:4] + x[4:5] for x in stats], axis=0)
    rescale = jnp.exp(block_max - jnp.max(block_max, axis=0, keepdims=True))
    factors = rescale / jnp.sum(rescale * block_sum, axis=0, keepdims=True)
    factors = jnp.concatenate([factors, jnp.zeros((LANES - sources, LANES), F32)], axis=0).T
    context = jnp.zeros((rows, LANES), F32)
    for s in range(sources):
        context += both[s, :rows, :] * factors[:, s : s + 1]
    out_ref[...] = context.astype(BF16)


def context_kernel(
    layer_no, requests, own_ref, other_ref, own_hbm, other_hbm, out_ref, weight, packed, sems
):
    copies = column_copies(layer_no, own_hbm, other_hbm, weight, sems)
    start_all(copies)
    sides = []
    for ref in (own_ref, other_ref):
        packed[...] = ref[...].astype(F32)
        sides.append(rows_of(packed, requests, packed.shape[0] // requests))
    rows = joined(sides[0], sides[1], 1).astype(BF16)
    wait_all(copies)
    out_ref[...] = jnp.dot(rows, weight[...], preferred_element_type=F32).astype(BF16)


def gate_up_kernel(
    layer_no,
    chunk,
    x_ref,
    a,
    b,
    c,
    d,
    gain_ref,
    gate_hbm,
    gate_other,
    up_hbm,
    up_other,
    out_ref,
    payload_ref,
    gate,
    up,
    packed,
    sems,
):
    width = gate.shape[1]
    piece = width // 1
    own_rows, other_rows = side_slices(gate_hbm.shape[1])
    steps = []
    for i, (own, other, weight) in enumerate(((gate_hbm, gate_other, gate), (up_hbm, up_other, up))):
        for j in range(width // piece):
            columns = pl.ds(pl.multiple_of(core_side() * width + j * piece, LANES), piece)
            local = pl.ds(j * piece, piece)
            copies = pair_copies(
                own.at[layer_no, :, columns],
                other.at[layer_no, :, columns],
                weight.at[own_rows, local],
                weight.at[other_rows, local],
                sems.at[len(steps)],
            )
            start_all(copies)
            steps.append((i, j, copies, weight))
    requests = x_ref.shape[0]
    per_chunk = chunk // (packed.shape[0] // requests)
    stride = packed.shape[0] // requests
    count = requests // per_chunk
    blocks = gate.shape[1] // LANES
    half = stride // 2

    def store(row, values):
        for q in range(per_chunk):
            packed[pl.ds(q * stride + row, count, stride=chunk), :] = values[q * count : (q + 1) * count]

    out_ref[...] = pair_sum(x_ref, (a, b, c, d))
    current = out_ref[...].astype(F32)
    scaled = (current * gain_ref[layer_no : layer_no + 1, :].astype(F32)).astype(BF16)
    zeros = jnp.zeros((requests, LANES), F32)
    store(blocks, squares_in_lanes(current))
    for row in [*range(blocks + 1, half), *range(half + blocks, stride)]:
        store(row, zeros)
    for i, j, copies, weight in steps:
        wait_all(copies)
        product = jnp.dot(scaled, weight[:, j * piece : (j + 1) * piece], preferred_element_type=F32)
        for k in range(piece // LANES):
            store(i * half + j * (piece // LANES) + k, product[:, k * LANES : (k + 1) * LANES])
    payload_ref[...] = packed[...].astype(BF16)


def fetched_gate_up_kernel(
    layer_no, chunk, x_ref, a, b, c, d, gain_ref, gate_ref, up_ref, out_ref, payload_ref, packed
):
    requests = x_ref.shape[0]
    stride = packed.shape[0] // requests
    per_chunk = chunk // stride
    count = requests // per_chunk
    blocks = gate_ref.shape[2] // LANES
    half = stride // 2

    def store(row, values):
        for q in range(per_chunk):
            packed[pl.ds(q * stride + row, count, stride=chunk), :] = values[q * count : (q + 1) * count]

    out_ref[...] = pair_sum(x_ref, (a, b, c, d))
    current = out_ref[...].astype(F32)
    scaled = current * gain_ref[layer_no : layer_no + 1, :].astype(F32)
    middle = scaled.shape[1] // 2
    first = core_side() == 0
    mine = jnp.where(first, scaled[:, :middle], scaled[:, middle:]).astype(BF16)
    theirs = jnp.where(first, scaled[:, middle:], scaled[:, :middle]).astype(BF16)
    zeros = jnp.zeros((requests, LANES), F32)
    store(blocks, squares_in_lanes(current))
    for row in [*range(blocks + 1, half), *range(half + blocks, stride)]:
        store(row, zeros)
    for i, weight in enumerate((gate_ref, up_ref)):
        product = jnp.dot(mine, weight[0], preferred_element_type=F32)
        product += jnp.dot(theirs, weight[1], preferred_element_type=F32)
        for k in range(blocks):
            store(i * half + k, product[:, k * LANES : (k + 1) * LANES])
    payload_ref[...] = packed[...].astype(BF16)


def activation_kernel(blocks, sources, half, received_ref, out_ref):
    totals = jnp.sum(received_ref[...].astype(F32).reshape(sources, -1, LANES), axis=0)
    acts = []
    for at in range(0, totals.shape[0], 2 * half):
        squares = totals[at + blocks : at + blocks + 1, 0:1] + totals[at + blocks : at + blocks + 1, 1:2]
        inv = lax.rsqrt(squares / D + EPSILON)
        gate = totals[at : at + half] * inv
        acts.append(gate / (1.0 + jnp.exp(-gate)) * (totals[at + half : at + 2 * half] * inv))
    repeat_into(out_ref, jnp.concatenate(acts, axis=0).astype(BF16))


def down_kernel(
    layer_no, half, chunk, received_ref, own_hbm, other_hbm, out_ref, weight, packed, sems
):
    depth = weight.shape[0] // 14
    own_columns, other_columns = side_slices(own_hbm.shape[2])
    steps = []
    for step in range(weight.shape[0] // depth):
        rows = pl.ds(step * depth, depth)
        steps.append(
            pair_copies(
                own_hbm.at[layer_no, rows],
                other_hbm.at[layer_no, rows],
                weight.at[rows, own_columns],
                weight.at[rows, other_columns],
                sems.at[step],
            )
        )
        start_all(steps[step])
    packed[...] = received_ref[...].astype(F32)
    blocks = weight.shape[0] // LANES // 2
    per_chunk = chunk // half
    count = out_ref.shape[0] // per_chunk
    total = 0.0
    for side in range(2):
        columns = []
        for k in range(blocks):
            columns.append(
                jnp.concatenate(
                    [
                        packed[pl.ds(side * chunk + q * half + k, count, stride=2 * chunk), :]
                        for q in range(per_chunk)
                    ],
                    axis=0,
                ).astype(BF16)
            )
        rows = jnp.concatenate(columns, axis=1)
        for at in range(0, rows.shape[1], depth):
            first = side * rows.shape[1] + at
            wait_all(steps[first // depth])
            total += jnp.dot(
                rows[:, at : at + depth], weight[first : first + depth], preferred_element_type=F32
            )
    out_ref[...] = total.astype(BF16)


def last_kernel(x_ref, a, b, c, d, out_ref):
    total = pair_sum(x_ref, (a, b, c, d)).astype(F32)
    width = out_ref.shape[1]
    out_ref[...] = jnp.where(core_side() == 0, total[:, :width], total[:, width:]).astype(BF16)


def exchange(array, n_req):
    shape = array.shape
    sides = [list(range(core, n_req, 2)) for core in range(2)]
    count = n_req // 2
    blocks = array.reshape((count, shape[0] // count) + shape[1:])
    return lax.all_to_all(
        blocks, "req", split_axis=0, concat_axis=0, tiled=True, axis_index_groups=sides
    ).reshape(shape)


def exchange_all(array, n_req):
    shape = array.shape
    blocks = array.reshape((n_req, shape[0] // n_req) + shape[1:])
    return lax.all_to_all(blocks, "req", split_axis=0, concat_axis=0, tiled=True).reshape(shape)


def from_pair(array, n_req):
    return lax.ppermute(array, "req", [(i, i ^ 1) for i in range(n_req)])


def tp_parts(partial_sum):
    n_tp = lax.axis_size("tp")
    one, three, two = [
        lax.ppermute(partial_sum, "tp", [(i, (i + shift) % n_tp) for i in range(n_tp)])
        for shift in (1, 3, 2)
    ]
    return [partial_sum, two, one, three]


def shards(
    hidden,
    attn_gain,
    q_weight,
    o_weight,
    ffn_gain,
    gate_weight,
    up_weight,
    down_weight,
    kv_pool,
    block_home,
    chosen,
    chosen_count,
):
    n_req = lax.axis_size("req")
    requests, width = hidden.shape
    pool_dev = kv_pool.shape[1]
    block_tokens, head_size = kv_pool.shape[4:]
    heads = q_weight.shape[2] // head_size // 2
    side = n_req // 2
    q_rows = requests * heads
    sent_rows = q_rows + requests
    stat_rows = q_rows + 16
    f_rows = 16
    hidden_half = gate_weight.shape[2] // 2
    blocks = hidden_half // LANES
    tables = rotary_tables(float(block_home.shape[1] * block_tokens - 1), head_size)
    dma = pltpu.SemaphoreType.DMA

    def rows_type(rows, kind=BF16):
        return jax.ShapeDtypeStruct((rows, LANES), kind)

    def rows_scratch(rows):
        return pltpu.VMEM((rows, LANES), F32)

    def pair_type(rows):
        return jax.ShapeDtypeStruct((rows, 2 * width), BF16)

    keep, send = call(
        functools.partial(first_query_kernel, pool_dev),
        [rows_type(sent_rows, F32), rows_type(sent_rows)],
        [HBM] * 6,
        [
            pltpu.VMEM(hidden.shape, BF16),
            pltpu.VMEM(attn_gain.shape, BF16),
            pltpu.VMEM(q_weight.shape[1:], BF16),
            pltpu.VMEM(block_home.shape, jnp.int32),
            pltpu.VMEM(chosen.shape, jnp.int32),
            pltpu.VMEM((1, LAYERS), jnp.int32),
            rows_scratch(q_rows),
            dma((6,)),
        ],
        limit=61,
    )(
        hidden,
        attn_gain,
        q_weight,
        block_home,
        chosen,
        chosen_count.reshape(1, LAYERS),
    )
    payload = call(pair_total_kernel, rows_type(side * sent_rows), [VMEM] * 2)(
        keep, from_pair(send, n_req)
    )
    payload, kv_later, o_later, gate_later, up_later, down_later, q_later = lax.optimization_barrier(
        (payload, kv_pool, o_weight, gate_weight, up_weight, down_weight, q_weight)
    )
    pool_other = from_pair(kv_later, n_req)
    o_other = from_pair(o_later, n_req)
    gate_other = from_pair(gate_later, n_req)
    up_other = from_pair(up_later, n_req)
    down_other = from_pair(down_later, n_req)
    q_other = from_pair(q_later, n_req)
    current, attn_gain, ffn_gain = call(
        pair_state_kernel,
        [pair_type(requests), pair_type(LAYERS), pair_type(LAYERS)],
        [VMEM] * 6,
    )(
        hidden,
        from_pair(hidden, n_req),
        attn_gain,
        from_pair(attn_gain, n_req),
        ffn_gain,
        from_pair(ffn_gain, n_req),
    )

    parts = None
    table = None
    for layer_no in range(LAYERS):
        if parts is not None:

            def half_of(ref, l=layer_no):
                return ref.at[l, :, side_slices(ref.shape[2] // 2)[0]]

            (weights,) = fetch(
                [(half_of, 0, b) for b in range(2)],
                (q_weight, q_other),
                [(2, width, heads * head_size)],
                act,
            )
            current, payload = call(
                functools.partial(query_kernel, layer_no),
                [pair_type(requests), rows_type(side * stat_rows)],
                [VMEM] * 7,
                [rows_scratch(q_rows)],
            )(current, *parts, attn_gain, weights)
        received = exchange(payload, n_req)
        scratch = [
            pltpu.VMEM((2, pool_dev, 2, block_tokens, head_size), BF16),
            rows_scratch(q_rows),
            dma((2, 2)),
        ]
        if table is None:
            payload, table = call(
                functools.partial(first_block_kernel, side),
                [rows_type(side * stat_rows), rows_type(requests, F32)],
                [VMEM] * 2 + [HBM] * 2 + [ANY],
                scratch,
            )(received, tables, kv_pool, pool_other, o_other)
        else:
            payload = call(
                functools.partial(later_block_kernel, layer_no, side),
                rows_type(side * stat_rows),
                [VMEM] * 3 + [HBM] * 2,
                scratch,
            )(received, table, tables, kv_pool, pool_other)
        stats = payload
        context = call(functools.partial(combine_kernel, side), rows_type(q_rows), [VMEM])(
            exchange(payload, n_req)
        )
        own = call(
            functools.partial(context_kernel, layer_no, requests),
            pair_type(requests),
            [VMEM] * 2 + [HBM] * 2,
            [pltpu.VMEM((o_weight.shape[1], 2 * width), BF16), rows_scratch(q_rows), dma((2,))],
        )(context, from_pair(context, n_req), o_weight, o_other)
        chunk = requests // side * 2 * f_rows
        if layer_no in (1,):

            def half_of(ref, l=layer_no):
                return ref.at[l, :, side_slices(ref.shape[2] // 2)[0]]

            gate_up = fetch(
                [(half_of, place, b) for place in range(2) for b in range(2)],
                (gate_weight, gate_other, up_weight, up_other),
                [(2, width, hidden_half)] * 2,
                stats,
            )
            current, payload = call(
                functools.partial(fetched_gate_up_kernel, layer_no, chunk),
                [pair_type(requests), rows_type(requests * 2 * f_rows)],
                [VMEM] * 8,
                [rows_scratch(requests * 2 * f_rows)],
            )(current, own, *tp_parts(own)[1:], ffn_gain, *gate_up)
        else:
            current, payload = call(
                functools.partial(gate_up_kernel, layer_no, chunk),
                [pair_type(requests), rows_type(requests * 2 * f_rows)],
                [VMEM] * 6 + [HBM] * 4,
                [
                    pltpu.VMEM((2 * width, hidden_half), BF16),
                    pltpu.VMEM((2 * width, hidden_half), BF16),
                    rows_scratch(requests * 2 * f_rows),
                    dma((2, 2)),
                ],
            )(current, *tp_parts(own), ffn_gain, gate_weight, gate_other, up_weight, up_other)
        chunk = requests // side * f_rows
        act = call(
            functools.partial(activation_kernel, blocks, side, f_rows),
            rows_type(n_req * chunk),
            [VMEM],
        )(exchange(payload, n_req))
        own = call(
            functools.partial(down_kernel, layer_no, f_rows, chunk),
            pair_type(requests),
            [VMEM] + [HBM] * 2,
            [
                pltpu.VMEM((down_weight.shape[1], 2 * width), BF16),
                rows_scratch(n_req * chunk),
                dma((14, 2)),
            ],
        )(exchange_all(act, n_req), down_weight, down_other)
        parts = tp_parts(own)
    return call(last_kernel, jax.ShapeDtypeStruct(hidden.shape, BF16), [VMEM] * 5)(current, *parts)


def solution(mesh):
    return jax.shard_map(
        shards,
        mesh=mesh,
        in_specs=(
            P(None, "req"),
            P(None, "req"),
            P(None, "req", "tp"),
            P(None, "tp", "req"),
            P(None, "req"),
            P(None, "req", "tp"),
            P(None, "req", "tp"),
            P(None, "tp", "req"),
            P(None, "req", "tp", None, None, None),
            P("req", None),
            P(None, "req", "tp", None),
            P(None, "req", "tp"),
        ),
        out_specs=P(None, "req"),
        check_vma=False,
    )
```

```python
import functools
import math

import jax
import jax.numpy as jnp
import numpy as np
from jax import lax
from jax.experimental import pallas as pl
from jax.experimental.pallas import tpu as pltpu
from jax.sharding import PartitionSpec as P

D = 8192
LAYERS = 2
LANES = 128

MASK_FILL = -1e30
EPSILON = 1e-05

VMEM = pl.BlockSpec(memory_space=pltpu.VMEM)
SMEM = pl.BlockSpec(memory_space=pltpu.SMEM)
HBM = pl.BlockSpec(memory_space=pltpu.HBM)
ANY = pl.BlockSpec(memory_space=pl.ANY)
F32 = jnp.float32
BF16 = jnp.bfloat16


def rotary_tables(position, head_size):
    freq_idx = np.arange(head_size // 2)
    angles = position * np.exp(freq_idx * (-2.0 * math.log(500000.0) / head_size))
    cosine, sine_part = np.cos(angles), np.sin(angles)
    scale = head_size**-0.5
    tables = np.stack([np.concatenate([cosine, cosine]), np.concatenate([-sine_part, sine_part])])
    return jnp.asarray(tables * scale, F32)


def call(kernel, out_shape, in_specs, scratch=(), limit=16, out_specs=None, flops=10000000000, nbytes=0):
    return pl.pallas_call(
        kernel,
        out_shape=out_shape,
        in_specs=in_specs,
        out_specs=out_specs if out_specs is not None else jax.tree.map(lambda _: VMEM, out_shape),
        scratch_shapes=list(scratch),
        compiler_params=pltpu.CompilerParams(vmem_limit_bytes=limit * 1024 * 1024),
        cost_estimate=pl.CostEstimate(flops=flops, bytes_accessed=nbytes, transcendentals=0),
    )


def core_side():
    return lax.rem(lax.axis_index("req"), 2)


def joined(own, other, axis):
    first = core_side() == 0
    return jnp.concatenate([jnp.where(first, own, other), jnp.where(first, other, own)], axis=axis)


def pair_copies(own_hbm, other_hbm, own_target, other_target, sems):
    return [
        pltpu.make_async_copy(own_hbm, own_target, sems.at[0]),
        pltpu.make_async_copy(other_hbm, other_target, sems.at[1]),
    ]


def side_slices(size):
    side = core_side()
    return (
        pl.ds(pl.multiple_of(side * size, LANES), size),
        pl.ds(pl.multiple_of((1 - side) * size, LANES), size),
    )


def column_copies(layer_no, own_hbm, other_hbm, weight, sems):
    own, other = side_slices(own_hbm.shape[2])
    return pair_copies(
        own_hbm.at[layer_no], other_hbm.at[layer_no], weight.at[:, own], weight.at[:, other], sems
    )


def row_copies(layer_no, own_hbm, other_hbm, weight, sems):
    half, _ = side_slices(weight.shape[1])
    own, other = side_slices(own_hbm.shape[1])
    return pair_copies(
        own_hbm.at[layer_no, :, half],
        other_hbm.at[layer_no, :, half],
        weight.at[own],
        weight.at[other],
        sems,
    )


def start_all(copies):
    for copy in copies:
        copy.start()


def wait_all(copies):
    for copy in copies:
        copy.wait()


def squares_in_lanes(current):
    squares = jnp.sum(current * current, axis=1, keepdims=True)
    high = squares.astype(BF16).astype(F32)
    lane = lax.broadcasted_iota(jnp.int32, (current.shape[0], LANES), 1)
    return jnp.where(lane == 0, high, jnp.where(lane == 1, squares - high, 0.0))


def along_lanes(column):
    n = column.shape[0]
    row = lax.broadcasted_iota(jnp.int32, (n, LANES), 0)
    lane = lax.broadcasted_iota(jnp.int32, (n, LANES), 1)
    return jnp.sum(jnp.where(row == lane, column, 0.0), axis=0, keepdims=True)


def along_rows(line, n):
    row = lax.broadcasted_iota(jnp.int32, (n, LANES), 0)
    lane = lax.broadcasted_iota(jnp.int32, (n, LANES), 1)
    return jnp.sum(jnp.where(row == lane, line, 0.0), axis=1, keepdims=True)


def square_rows(current, rows):
    squares = jnp.sum(current * current, axis=1, keepdims=True)
    high = squares.astype(BF16).astype(F32)
    row = lax.broadcasted_iota(jnp.int32, (rows, LANES), 0)
    low = jnp.where(row == 1, along_lanes(squares - high), 0.0)
    return jnp.where(row == 0, along_lanes(high), low)


def store_blocks(packed, product):
    requests, width = product.shape
    blocks = width // LANES
    for k in range(blocks):
        packed[pl.ds(k, requests, stride=blocks), :] = product[:, k * LANES : (k + 1) * LANES]
    return packed[...]


def spread(packed, values, stride):
    for k in range(stride):
        packed[pl.ds(k, values.shape[0], stride=stride), :] = values
    return packed[...]


def rows_of(packed, requests, blocks):
    return jnp.concatenate(
        [packed[pl.ds(k, requests, stride=blocks), :] for k in range(blocks)], axis=1
    )


def repeat_into(out_ref, values):
    rows = values.shape[0]
    for i in range(out_ref.shape[0] // rows):
        out_ref[i * rows : (i + 1) * rows, :] = values


def pair_sum(current, parts):
    a, b, c, d = [part[...].astype(F32) for part in parts]
    return (current[...].astype(F32) + ((a + b) + (c + d))).astype(BF16)


def slot_table(homes, chosen, counts, pool_dev, requests):
    n_blocks = homes.shape[1]
    shape = (n_blocks, n_blocks)
    row = lax.broadcasted_iota(jnp.int32, shape, 0)
    col = lax.broadcasted_iota(jnp.int32, shape, 1)
    places = jnp.broadcast_to(homes, shape)
    here = lax.div(places, pool_dev) == row

    def across(column):
        return jnp.sum(jnp.where(row == col, column, 0.0), axis=0, keepdims=True)

    slots = jnp.sum(jnp.where(here, lax.rem(places, pool_dev), 0).astype(F32), axis=1, keepdims=True)
    found = [jnp.zeros((1, n_blocks), F32), across(slots)]
    for layer_no in range(LAYERS):
        listed = chosen[layer_no]
        entry = lax.broadcasted_iota(jnp.int32, (n_blocks, listed.shape[1]), 1)
        block = lax.broadcasted_iota(jnp.int32, (n_blocks, listed.shape[1]), 0)
        hit = (listed == block) & (entry < counts[layer_no])
        taken = across(jnp.max(jnp.where(hit, 1.0, 0.0), axis=1, keepdims=True))
        found.append(across(jnp.max(jnp.where(here, taken, 0.0), axis=1, keepdims=True)))
    line = jnp.concatenate(found, axis=1)
    mine = lax.broadcasted_iota(jnp.int32, (requests, LANES), 0) == lax.axis_index("req")
    return jnp.where(mine, line, 0.0)


def first_query_kernel(
    pool_dev,
    x_hbm,
    gain_hbm,
    weight_hbm,
    homes_hbm,
    chosen_hbm,
    count_hbm,
    keep_ref,
    send_ref,
    x,
    gain,
    weight,
    homes,
    chosen,
    counts,
    packed,
    sems,
):
    copies = [
        pltpu.make_async_copy(source, target, sems.at[i])
        for i, (source, target) in enumerate(
            [
                (homes_hbm, homes),
                (chosen_hbm, chosen),
                (count_hbm, counts),
                (x_hbm, x),
                (gain_hbm, gain),
                (weight_hbm.at[0], weight),
            ]
        )
    ]
    start_all(copies)
    wait_all(copies[:3])
    lists = [chosen[i, 0] for i in range(LAYERS)]
    limits = [counts[:, i : i + 1] for i in range(LAYERS)]
    table = slot_table(homes[...], lists, limits, pool_dev, x.shape[0])
    wait_all(copies[3:])
    current = x[...].astype(F32)
    scaled = (current * gain[0:1, :].astype(F32)).astype(BF16)
    product = jnp.dot(scaled, weight[...], preferred_element_type=F32)
    middle = product.shape[1] // 2
    first = core_side() == 0
    rows = packed.shape[0]
    keep_ref[:rows, :] = store_blocks(packed, jnp.where(first, product[:, :middle], product[:, middle:]))
    send = store_blocks(packed, jnp.where(first, product[:, middle:], product[:, :middle]))
    send_ref[:rows, :] = send.astype(BF16)
    extra = squares_in_lanes(current) + table
    keep_ref[rows:, :] = extra
    send_ref[rows:, :] = extra.astype(BF16)


def fetch_kernel(sources, *refs):
    count = len(sources)
    ins, outs, sems = refs[:count], refs[count + 1 : -1], refs[-1]
    copies = [
        pltpu.make_async_copy(source(ref), outs[place].at[part], sems.at[i])
        for i, (ref, (source, place, part)) in enumerate(zip(ins, sources))
    ]
    start_all(copies)
    wait_all(copies)


def fetch(sources, operands, shapes, after):
    return call(
        functools.partial(fetch_kernel, sources),
        [jax.ShapeDtypeStruct(shape, BF16) for shape in shapes],
        [HBM] * len(operands) + [ANY],
        [pltpu.SemaphoreType.DMA((len(operands),))],
        flops=2000000000,
    )(*operands, after)


def pair_total_kernel(keep_ref, received_ref, out_ref):
    repeat_into(out_ref, (keep_ref[...] + received_ref[...].astype(F32)).astype(BF16))


def pair_state_kernel(x, x_other, gain, gain_other, ffn, ffn_other, x_out, gain_out, ffn_out):
    for own, other, out in ((x, x_other, x_out), (gain, gain_other, gain_out), (ffn, ffn_other, ffn_out)):
        out[...] = joined(own[...].astype(F32), other[...].astype(F32), 1).astype(BF16)


def query_kernel(layer_no, x_ref, a, b, c, d, gain_ref, weight_ref, out_ref, payload_ref, packed):
    out_ref[...] = pair_sum(x_ref, (a, b, c, d))
    current = out_ref[...].astype(F32)
    scaled = current * gain_ref[layer_no : layer_no + 1, :].astype(F32)
    middle = scaled.shape[1] // 2
    first = core_side() == 0
    mine = jnp.where(first, scaled[:, :middle], scaled[:, middle:]).astype(BF16)
    theirs = jnp.where(first, scaled[:, middle:], scaled[:, :middle]).astype(BF16)
    product = jnp.dot(mine, weight_ref[0], preferred_element_type=F32)
    product += jnp.dot(theirs, weight_ref[1], preferred_element_type=F32)
    extra = square_rows(current, payload_ref.shape[0] // 16 - packed.shape[0])
    rows = jnp.concatenate([store_blocks(packed, product), extra], axis=0)
    repeat_into(payload_ref, rows.astype(BF16))


def in_parts(values, count):
    parts = []
    for _ in range(count):
        part = values.astype(BF16).astype(F32)
        parts.append(part)
        values = values - part
    return parts


def stats_in_lanes(block_max, block_sum):
    shape = (block_max.shape[0], LANES)
    lane = lax.broadcasted_iota(jnp.int32, shape, 1)
    stats = jnp.zeros(shape, F32)
    for place, part in enumerate(in_parts(block_max, 3) + in_parts(block_sum, 2)):
        stats = jnp.where(lane == place, part, stats)
    return stats


def block_kernel(
    layer_no, sources, received_ref, table_ref, tables_ref, own_hbm, other_hbm, out_ref, table_out, blocks, packed, sems
):
    n_slots = blocks.shape[1]
    piece = n_slots // 1
    copies = [
        [
            pltpu.make_async_copy(
                pool.at[layer_no, pl.ds(at, piece), 0, part],
                blocks.at[b, pl.ds(at, piece), part],
                sems.at[(part * n_slots + at) // piece, b],
            )
            for b, pool in enumerate((own_hbm, other_hbm))
        ]
        for part in range(2)
        for at in range(0, n_slots, piece)
    ]
    for pair in copies:
        start_all(pair)
    rows = packed.shape[0]
    totals = jnp.sum(received_ref[...].astype(F32).reshape(sources, -1, LANES), axis=0)
    extra = totals[rows:]
    requests = extra.shape[0] if table_ref is None else table_ref.shape[0]
    heads = rows // requests
    if table_ref is None:
        squares = extra[:, 0:1] + extra[:, 1:2]
    else:
        squares = along_rows(extra[0:1] + extra[1:2], requests)
    inv = lax.rsqrt(squares / D + EPSILON)
    queries = totals[:rows] * spread(packed, jnp.broadcast_to(inv, (requests, LANES)), heads)
    queries = queries * tables_ref[0:1, :] + pltpu.roll(queries, LANES // 2, 1) * tables_ref[1:2, :]
    queries = queries.astype(BF16)

    table = extra if table_ref is None else table_ref[...]
    if table_out is not None:
        table_out[...] = extra
    me = lax.axis_index("req")
    lane = lax.broadcasted_iota(jnp.int32, table.shape, 1)
    request = lax.broadcasted_iota(jnp.int32, (requests, rows), 0)
    column = lax.broadcasted_iota(jnp.int32, (requests, rows), 1)
    row = lax.broadcasted_iota(jnp.int32, (2 * n_slots * heads, rows), 0)
    head = lax.rem(column, heads).astype(F32)
    places, used = [], []
    for b in range(2):
        store = me if b == 0 else me + 1 - 2 * core_side()
        slots = jnp.sum(jnp.where(lane == n_slots + store, table, 0.0), axis=1, keepdims=True)
        taken = jnp.where(lane == (2 + layer_no) * n_slots + store, table, 0.0)
        taken = jnp.broadcast_to(jnp.sum(taken, axis=1, keepdims=True), table.shape)
        used.append(spread(packed, taken, heads))
        target = jnp.where(
            lax.div(column, heads) == request, slots * (2 * heads) + (head + b * heads), 0.0
        )
        target = jnp.sum(target, axis=0, keepdims=True).astype(jnp.int32)
        places.append(jnp.where(row == target, 1.0, 0.0))
    by_slot = jnp.concatenate(places, axis=1)
    queries = jnp.dot(
        by_slot.astype(BF16), jnp.concatenate([queries, queries], axis=0), preferred_element_type=F32
    )
    group = 2 * heads
    mine = lax.broadcasted_iota(jnp.int32, (group, LANES), 0) < heads

    def of_slot(left, p, part, contract):
        if p % piece == 0:
            wait_all(copies[(part * n_slots + p) // piece])
        left = left[p * group : (p + 1) * group]
        left = jnp.concatenate([jnp.where(mine, left, 0.0), jnp.where(mine, 0.0, left)], axis=1)
        right = jnp.concatenate([blocks[0, p, part], blocks[1, p, part]], axis=contract)
        return lax.dot_general(
            left.astype(BF16), right, (((1,), (contract,)), ((), ())), preferred_element_type=F32
        )

    scores = jnp.concatenate([of_slot(queries, p, 0, 1) for p in range(n_slots)], axis=0)
    block_max = jnp.max(scores, axis=1, keepdims=True)
    terms = jnp.exp(scores - block_max)
    block_sum = jnp.sum(terms, axis=1, keepdims=True)
    acc = jnp.concatenate([of_slot(terms, p, 1, 0) for p in range(n_slots)], axis=0)
    both = jnp.concatenate([acc, stats_in_lanes(block_max, block_sum)], axis=1).astype(BF16)
    both = jnp.dot(by_slot.T.astype(BF16), both, preferred_element_type=F32)
    sides = []
    for b in range(2):
        side = both[b * rows : (b + 1) * rows]
        stats = side[:, LANES:]
        block_max = stats[:, 0:1] + stats[:, 1:2] + stats[:, 2:3]
        block_max = jnp.where(used[b][:, 0:1] > 0.0, block_max, MASK_FILL)
        sides.append((block_max, stats[:, 3:4] + stats[:, 4:5], side[:, :LANES]))
    top = jnp.maximum(sides[0][0], sides[1][0])
    rescale = [jnp.exp(side[0] - top) for side in sides]
    total = rescale[0] * sides[0][1] + rescale[1] * sides[1][1]
    acc = rescale[0] * sides[0][2] + rescale[1] * sides[1][2]
    stats = stats_in_lanes(top, total).T
    extra = out_ref.shape[0] // sources - rows
    repeat_into(out_ref, jnp.concatenate([acc, stats[:extra]], axis=0).astype(BF16))


def first_block_kernel(
    sources, received_ref, tables_ref, own_hbm, other_hbm, fetched_before, out_ref, table_out, *scratch
):
    del fetched_before
    block_kernel(
        0, sources, received_ref, None, tables_ref, own_hbm, other_hbm, out_ref, table_out, *scratch
    )


def later_block_kernel(
    layer_no, sources, received_ref, table_ref, tables_ref, own_hbm, other_hbm, out_ref, *scratch
):
    block_kernel(
        layer_no, sources, received_ref, table_ref, tables_ref, own_hbm, other_hbm, out_ref, None, *scratch
    )


def combine_kernel(sources, received_ref, out_ref):
    rows = out_ref.shape[0]
    both = received_ref[...].astype(F32).reshape(sources, -1, LANES)
    stats = [both[s, rows : rows + 8, :] for s in range(sources)]
    block_max = jnp.concatenate([x[0:1] + x[1:2] + x[2:3] for x in stats], axis=0)
    block_sum = jnp.concatenate([x[3:4] + x[4:5] for x in stats], axis=0)
    rescale = jnp.exp(block_max - jnp.max(block_max, axis=0, keepdims=True))
    factors = rescale / jnp.sum(rescale * block_sum, axis=0, keepdims=True)
    factors = jnp.concatenate([factors, jnp.zeros((LANES - sources, LANES), F32)], axis=0).T
    context = jnp.zeros((rows, LANES), F32)
    for s in range(sources):
        context += both[s, :rows, :] * factors[:, s : s + 1]
    out_ref[...] = context.astype(BF16)


def context_kernel(
    layer_no, requests, own_ref, other_ref, own_hbm, other_hbm, out_ref, weight, packed, sems
):
    copies = column_copies(layer_no, own_hbm, other_hbm, weight, sems)
    start_all(copies)
    sides = []
    for ref in (own_ref, other_ref):
        packed[...] = ref[...].astype(F32)
        sides.append(rows_of(packed, requests, packed.shape[0] // requests))
    rows = joined(sides[0], sides[1], 1).astype(BF16)
    wait_all(copies)
    out_ref[...] = jnp.dot(rows, weight[...], preferred_element_type=F32).astype(BF16)


def gate_up_kernel(
    layer_no,
    chunk,
    x_ref,
    a,
    b,
    c,
    d,
    gain_ref,
    gate_hbm,
    gate_other,
    up_hbm,
    up_other,
    out_ref,
    payload_ref,
    gate,
    up,
    packed,
    sems,
):
    width = gate.shape[1]
    piece = width // 1
    own_rows, other_rows = side_slices(gate_hbm.shape[1])
    steps = []
    for i, (own, other, weight) in enumerate(((gate_hbm, gate_other, gate), (up_hbm, up_other, up))):
        for j in range(width // piece):
            columns = pl.ds(pl.multiple_of(core_side() * width + j * piece, LANES), piece)
            local = pl.ds(j * piece, piece)
            copies = pair_copies(
                own.at[layer_no, :, columns],
                other.at[layer_no, :, columns],
                weight.at[own_rows, local],
                weight.at[other_rows, local],
                sems.at[len(steps)],
            )
            start_all(copies)
            steps.append((i, j, copies, weight))
    requests = x_ref.shape[0]
    per_chunk = chunk // (packed.shape[0] // requests)
    stride = packed.shape[0] // requests
    count = requests // per_chunk
    blocks = gate.shape[1] // LANES
    half = stride // 2

    def store(row, values):
        for q in range(per_chunk):
            packed[pl.ds(q * stride + row, count, stride=chunk), :] = values[q * count : (q + 1) * count]

    out_ref[...] = pair_sum(x_ref, (a, b, c, d))
    current = out_ref[...].astype(F32)
    scaled = (current * gain_ref[layer_no : layer_no + 1, :].astype(F32)).astype(BF16)
    zeros = jnp.zeros((requests, LANES), F32)
    store(blocks, squares_in_lanes(current))
    for row in [*range(blocks + 1, half), *range(half + blocks, stride)]:
        store(row, zeros)
    for i, j, copies, weight in steps:
        wait_all(copies)
        product = jnp.dot(scaled, weight[:, j * piece : (j + 1) * piece], preferred_element_type=F32)
        for k in range(piece // LANES):
            store(i * half + j * (piece // LANES) + k, product[:, k * LANES : (k + 1) * LANES])
    payload_ref[...] = packed[...].astype(BF16)


def fetched_gate_up_kernel(
    layer_no, chunk, x_ref, a, b, c, d, gain_ref, gate_ref, up_ref, out_ref, payload_ref, packed
):
    requests = x_ref.shape[0]
    stride = packed.shape[0] // requests
    per_chunk = chunk // stride
    count = requests // per_chunk
    blocks = gate_ref.shape[2] // LANES
    half = stride // 2

    def store(row, values):
        for q in range(per_chunk):
            packed[pl.ds(q * stride + row, count, stride=chunk), :] = values[q * count : (q + 1) * count]

    out_ref[...] = pair_sum(x_ref, (a, b, c, d))
    current = out_ref[...].astype(F32)
    scaled = current * gain_ref[layer_no : layer_no + 1, :].astype(F32)
    middle = scaled.shape[1] // 2
    first = core_side() == 0
    mine = jnp.where(first, scaled[:, :middle], scaled[:, middle:]).astype(BF16)
    theirs = jnp.where(first, scaled[:, middle:], scaled[:, :middle]).astype(BF16)
    zeros = jnp.zeros((requests, LANES), F32)
    store(blocks, squares_in_lanes(current))
    for row in [*range(blocks + 1, half), *range(half + blocks, stride)]:
        store(row, zeros)
    for i, weight in enumerate((gate_ref, up_ref)):
        product = jnp.dot(mine, weight[0], preferred_element_type=F32)
        product += jnp.dot(theirs, weight[1], preferred_element_type=F32)
        for k in range(blocks):
            store(i * half + k, product[:, k * LANES : (k + 1) * LANES])
    payload_ref[...] = packed[...].astype(BF16)


def activation_kernel(blocks, sources, half, received_ref, out_ref):
    totals = jnp.sum(received_ref[...].astype(F32).reshape(sources, -1, LANES), axis=0)
    acts = []
    for at in range(0, totals.shape[0], 2 * half):
        squares = totals[at + blocks : at + blocks + 1, 0:1] + totals[at + blocks : at + blocks + 1, 1:2]
        inv = lax.rsqrt(squares / D + EPSILON)
        gate = totals[at : at + half] * inv
        acts.append(gate / (1.0 + jnp.exp(-gate)) * (totals[at + half : at + 2 * half] * inv))
    repeat_into(out_ref, jnp.concatenate(acts, axis=0).astype(BF16))


def down_kernel(
    layer_no, half, chunk, received_ref, own_hbm, other_hbm, out_ref, weight, packed, sems
):
    depth = weight.shape[0] // 14
    own_columns, other_columns = side_slices(own_hbm.shape[2])
    steps = []
    for step in range(weight.shape[0] // depth):
        rows = pl.ds(step * depth, depth)
        steps.append(
            pair_copies(
                own_hbm.at[layer_no, rows],
                other_hbm.at[layer_no, rows],
                weight.at[rows, own_columns],
                weight.at[rows, other_columns],
                sems.at[step],
            )
        )
        start_all(steps[step])
    packed[...] = received_ref[...].astype(F32)
    blocks = weight.shape[0] // LANES // 2
    per_chunk = chunk // half
    count = out_ref.shape[0] // per_chunk
    total = 0.0
    for side in range(2):
        columns = []
        for k in range(blocks):
            columns.append(
                jnp.concatenate(
                    [
                        packed[pl.ds(side * chunk + q * half + k, count, stride=2 * chunk), :]
                        for q in range(per_chunk)
                    ],
                    axis=0,
                ).astype(BF16)
            )
        rows = jnp.concatenate(columns, axis=1)
        for at in range(0, rows.shape[1], depth):
            first = side * rows.shape[1] + at
            wait_all(steps[first // depth])
            total += jnp.dot(
                rows[:, at : at + depth], weight[first : first + depth], preferred_element_type=F32
            )
    out_ref[...] = total.astype(BF16)


def last_kernel(x_ref, a, b, c, d, out_ref):
    total = pair_sum(x_ref, (a, b, c, d)).astype(F32)
    width = out_ref.shape[1]
    out_ref[...] = jnp.where(core_side() == 0, total[:, :width], total[:, width:]).astype(BF16)


def exchange(array, n_req):
    shape = array.shape
    sides = [list(range(core, n_req, 2)) for core in range(2)]
    count = n_req // 2
    blocks = array.reshape((count, shape[0] // count) + shape[1:])
    return lax.all_to_all(
        blocks, "req", split_axis=0, concat_axis=0, tiled=True, axis_index_groups=sides
    ).reshape(shape)


def exchange_all(array, n_req):
    shape = array.shape
    blocks = array.reshape((n_req, shape[0] // n_req) + shape[1:])
    return lax.all_to_all(blocks, "req", split_axis=0, concat_axis=0, tiled=True).reshape(shape)


def from_pair(array, n_req):
    return lax.ppermute(array, "req", [(i, i ^ 1) for i in range(n_req)])


def tp_parts(partial_sum):
    n_tp = lax.axis_size("tp")
    one, three, two = [
        lax.ppermute(partial_sum, "tp", [(i, (i + shift) % n_tp) for i in range(n_tp)])
        for shift in (1, 3, 2)
    ]
    return [partial_sum, two, one, three]


def shards(
    hidden,
    attn_gain,
    q_weight,
    o_weight,
    ffn_gain,
    gate_weight,
    up_weight,
    down_weight,
    kv_pool,
    block_home,
    chosen,
    chosen_count,
):
    n_req = lax.axis_size("req")
    requests, width = hidden.shape
    pool_dev = kv_pool.shape[1]
    block_tokens, head_size = kv_pool.shape[4:]
    heads = q_weight.shape[2] // head_size // 2
    side = n_req // 2
    q_rows = requests * heads
    sent_rows = q_rows + requests
    stat_rows = q_rows + 16
    f_rows = 16
    hidden_half = gate_weight.shape[2] // 2
    blocks = hidden_half // LANES
    tables = rotary_tables(float(block_home.shape[1] * block_tokens - 1), head_size)
    dma = pltpu.SemaphoreType.DMA

    def rows_type(rows, kind=BF16):
        return jax.ShapeDtypeStruct((rows, LANES), kind)

    def rows_scratch(rows):
        return pltpu.VMEM((rows, LANES), F32)

    def pair_type(rows):
        return jax.ShapeDtypeStruct((rows, 2 * width), BF16)

    keep, send = call(
        functools.partial(first_query_kernel, pool_dev),
        [rows_type(sent_rows, F32), rows_type(sent_rows)],
        [HBM] * 6,
        [
            pltpu.VMEM(hidden.shape, BF16),
            pltpu.VMEM(attn_gain.shape, BF16),
            pltpu.VMEM(q_weight.shape[1:], BF16),
            pltpu.VMEM(block_home.shape, jnp.int32),
            pltpu.VMEM(chosen.shape, jnp.int32),
            pltpu.VMEM((1, LAYERS), jnp.int32),
            rows_scratch(q_rows),
            dma((6,)),
        ],
        limit=61,
    )(
        hidden,
        attn_gain,
        q_weight,
        block_home,
        chosen,
        chosen_count.reshape(1, LAYERS),
    )
    payload = call(pair_total_kernel, rows_type(side * sent_rows), [VMEM] * 2)(
        keep, from_pair(send, n_req)
    )
    payload, kv_later, o_later, gate_later, up_later, down_later = lax.optimization_barrier(
        (payload, kv_pool, o_weight, gate_weight, up_weight, down_weight)
    )
    pool_other = from_pair(kv_later, n_req)
    o_other = from_pair(o_later, n_req)
    gate_other = from_pair(gate_later, n_req)
    up_other = from_pair(up_later, n_req)
    down_other = from_pair(down_later, n_req)
    current, attn_gain, ffn_gain = call(
        pair_state_kernel,
        [pair_type(requests), pair_type(LAYERS), pair_type(LAYERS)],
        [VMEM] * 6,
    )(
        hidden,
        from_pair(hidden, n_req),
        attn_gain,
        from_pair(attn_gain, n_req),
        ffn_gain,
        from_pair(ffn_gain, n_req),
    )

    parts = None
    table = None
    for layer_no in range(LAYERS):
        if parts is not None:

            def half_of(ref, l=layer_no):
                return ref.at[l, :, side_slices(ref.shape[2] // 2)[0]]

            (weights,) = fetch(
                [(half_of, 0, b) for b in range(2)],
                (q_weight, q_other),
                [(2, width, heads * head_size)],
                act,
            )
            current, payload = call(
                functools.partial(query_kernel, layer_no),
                [pair_type(requests), rows_type(side * stat_rows)],
                [VMEM] * 7,
                [rows_scratch(q_rows)],
            )(current, *parts, attn_gain, weights)
        received = exchange(payload, n_req)
        scratch = [
            pltpu.VMEM((2, pool_dev, 2, block_tokens, head_size), BF16),
            rows_scratch(q_rows),
            dma((2, 2)),
        ]
        if table is None:
            payload, table = call(
                functools.partial(first_block_kernel, side),
                [rows_type(side * stat_rows), rows_type(requests, F32)],
                [VMEM] * 2 + [HBM] * 2 + [ANY],
                scratch,
            )(received, tables, kv_pool, pool_other, o_other)
        else:
            payload = call(
                functools.partial(later_block_kernel, layer_no, side),
                rows_type(side * stat_rows),
                [VMEM] * 3 + [HBM] * 2,
                scratch,
            )(received, table, tables, kv_pool, pool_other)
        stats = payload
        context = call(functools.partial(combine_kernel, side), rows_type(q_rows), [VMEM])(
            exchange(payload, n_req)
        )
        own = call(
            functools.partial(context_kernel, layer_no, requests),
            pair_type(requests),
            [VMEM] * 2 + [HBM] * 2,
            [pltpu.VMEM((o_weight.shape[1], 2 * width), BF16), rows_scratch(q_rows), dma((2,))],
        )(context, from_pair(context, n_req), o_weight, o_other)
        chunk = requests // side * 2 * f_rows
        if layer_no in (1,):

            def half_of(ref, l=layer_no):
                return ref.at[l, :, side_slices(ref.shape[2] // 2)[0]]

            gate_up = fetch(
                [(half_of, place, b) for place in range(2) for b in range(2)],
                (gate_weight, gate_other, up_weight, up_other),
                [(2, width, hidden_half)] * 2,
                stats,
            )
            current, payload = call(
                functools.partial(fetched_gate_up_kernel, layer_no, chunk),
                [pair_type(requests), rows_type(requests * 2 * f_rows)],
                [VMEM] * 8,
                [rows_scratch(requests * 2 * f_rows)],
            )(current, own, *tp_parts(own)[1:], ffn_gain, *gate_up)
        else:
            current, payload = call(
                functools.partial(gate_up_kernel, layer_no, chunk),
                [pair_type(requests), rows_type(requests * 2 * f_rows)],
                [VMEM] * 6 + [HBM] * 4,
                [
                    pltpu.VMEM((2 * width, hidden_half), BF16),
                    pltpu.VMEM((2 * width, hidden_half), BF16),
                    rows_scratch(requests * 2 * f_rows),
                    dma((2, 2)),
                ],
            )(current, *tp_parts(own), ffn_gain, gate_weight, gate_other, up_weight, up_other)
        chunk = requests // side * f_rows
        act = call(
            functools.partial(activation_kernel, blocks, side, f_rows),
            rows_type(n_req * chunk),
            [VMEM],
        )(exchange(payload, n_req))
        acts = exchange_all(act, n_req)
        if layer_no == 0:
            acts, q_later = lax.optimization_barrier((acts, q_weight))
            q_other = from_pair(q_later, n_req)
        own = call(
            functools.partial(down_kernel, layer_no, f_rows, chunk),
            pair_type(requests),
            [VMEM] + [HBM] * 2,
            [
                pltpu.VMEM((down_weight.shape[1], 2 * width), BF16),
                rows_scratch(n_req * chunk),
                dma((14, 2)),
            ],
        )(acts, down_weight, down_other)
        parts = tp_parts(own)
    return call(last_kernel, jax.ShapeDtypeStruct(hidden.shape, BF16), [VMEM] * 5)(current, *parts)


def solution(mesh):
    return jax.shard_map(
        shards,
        mesh=mesh,
        in_specs=(
            P(None, "req"),
            P(None, "req"),
            P(None, "req", "tp"),
            P(None, "tp", "req"),
            P(None, "req"),
            P(None, "req", "tp"),
            P(None, "req", "tp"),
            P(None, "tp", "req"),
            P(None, "req", "tp", None, None, None),
            P("req", None),
            P(None, "req", "tp", None),
            P(None, "req", "tp"),
        ),
        out_specs=P(None, "req"),
        check_vma=False,
    )
```
